256 devices in a mesh: mol: 8 (over x, core), task: 32 (over z, y).
Axes of the slice: x: 4, y: 4, z: 8, core: 2. Of those that a mesh axis runs over, the one named last changes fastest.
Arguments:
- node_embed: bfloat16 [12288, 6272], P(('mol', 'task')), may hold values from -6 to 6
- wigner: bfloat16 [256, 29, 49], replicated, as said below
- source: int32 [49152], P(('mol', 'task')), may hold values from 0 to 47
- target: int32 [49152], P(('mol', 'task')), may hold values from 0 to 47
- rotation: int32 [49152], P(('mol', 'task')), may hold values from 0 to 255
- edge_filter: bfloat16 [49152, 128], P(('mol', 'task')), may hold values from -6 to 6
- edge_count: int32 [256], P(('mol', 'task')), may hold values from 1 to 192, as said below
- w_zero: bfloat16 [1792, 896], P('task'), may hold values from -0.125 to 0.125
- w_one_real: bfloat16 [1536, 768], P('task'), may hold values from -0.109375 to 0.109375
- w_one_imag: bfloat16 [1536, 768], P('task'), may hold values from -0.109375 to 0.109375
- w_two_real: bfloat16 [1280, 640], P('task'), may hold values from -0.125 to 0.125
- w_two_imag: bfloat16 [1280, 640], P('task'), may hold values from -0.125 to 0.125
- atom_struct: int32 [12288], P(('mol', 'task')), may hold values from 0 to 3
- struct_task: int32 [1024], P(('mol', 'task')), may hold values from 0 to 4
- task_head: float32 [5, 128], replicated, may hold values from -0.5 to 0.5
Outputs:
- update: bfloat16 [12288, 6272], P(('mol', 'task'))
- energy: float32 [1024], P(('mol', 'task'))
The draws below stay inside these ranges and needn't reach their ends.
Inputs may be any that keep to these rules, and one draw needn't show every extreme that they name: Each device has ceil(edge_count / 64) live blocks; for every task index and every mol index i below 4, the live blocks of mol index i and of mol index i + 4 sum to at most 4. `wigner`: entry (r, j) is zero unless edge-frame row r and coefficient j have the same degree.
All inputs are finite; a program needn't handle non-finite values.
Results may differ from the reference program's by a relative error of at most 0.0057.
Values may be sent and summed in bfloat16 or wider, within the bound.
No kernel may reach another device: no remote copies, remote signals or barrier semaphores. Data moves between devices by JAX's collectives and lax.ppermute only.
A program may use at most 128 MiB of HBM per device.

```python
import jax
import jax.numpy as jnp
import numpy as np
from jax import lax

C = 128
COEF = 49
MROWS = 29
BLK = 64
CAP = 3
ATOM_DEV = 48
STRUCT_DEV = 4
NROT = 256
NTASK = 5
ATOMS = 12288
EDGES = 49152
STRUCTS = 1024
N_MOL = 8
N_TASK = 32


def draw_wigner(key, part):
    key = jax.random.fold_in(key, 7)
    row_degree = np.array(list(range(7)) + list(range(1, 7)) + list(range(1, 7)) + list(range(2, 7)) + list(range(2, 7)))
    column_degree = np.floor(np.sqrt(np.arange(49) + 0.5)).astype(np.int64)
    pattern = (row_degree[:, None] == column_degree[None, :]).astype(np.float32)
    pattern = pattern / np.sqrt(2.0 * column_degree[None, :] + 1.0).astype(np.float32)
    base_values = jax.random.normal(key, (NROT, MROWS, COEF), jnp.float32)
    return (base_values * jnp.asarray(pattern)[None, :, :]).astype(jnp.bfloat16)


def draw_edge_count(key, part):
    key = jax.random.fold_in(key, 3)
    first_key, second_key, third_key, fourth_key = jax.random.split(key, 4)
    half_mol = N_MOL // 2
    keep_blocks = (CAP + 1) // 2
    heavy = jax.random.randint(first_key, (half_mol, N_TASK), keep_blocks, CAP + 1).at[0, 0].set(CAP)
    light = jax.random.randint(second_key, (half_mol, N_TASK), 1, 2 * keep_blocks - heavy + 1)
    flipped = jax.random.randint(third_key, (half_mol, N_TASK), 0, 2).at[0, 0].set(1)
    upper_half = jnp.where(flipped == 1, heavy, light)
    lower_half = jnp.where(flipped == 1, light, heavy)
    blocks = jnp.concatenate((upper_half, lower_half), axis=0)
    remainder = jax.random.randint(fourth_key, (N_MOL, N_TASK), 1, BLK + 1).at[0, 0].set(BLK)
    totals = (blocks - 1) * BLK + remainder
    return totals.reshape(N_MOL * N_TASK).astype(jnp.int32)


def with_ends(values, own_key, low, top_value):
    longest = values.shape.index(max(values.shape))
    spots = []
    for shift in (0, 1):
        where = [jax.random.randint(jax.random.fold_in(own_key, axis), (), 0, length) for axis, length in enumerate(values.shape)]
        where[longest] = (where[longest] + shift) % values.shape[longest]
        spots.append(tuple(where))
    return values.at[spots[0]].set(low).at[spots[1]].set(top_value)


def shard_levels(own_key, shape, shards, smallest, top_value):
    def one(position, parts):
        heights = jax.random.uniform(jax.random.fold_in(jax.random.fold_in(own_key, 6), position), (parts,), jnp.float32, smallest / len(shards), top_value / len(shards))
        return jnp.repeat(jnp.exp(heights), shape[position] // parts).reshape((-1,) + (1,) * (len(shape) - position - 1))

    loudness = one(*shards[0])
    for cut in shards[1:]:
        loudness = loudness * one(*cut)
    return loudness


def scatter_about(own_key, dims, width, reach, cuts=(), kind=jnp.bfloat16):
    factor_of = shard_levels(own_key, dims, cuts, -0.22, 0.18) if cuts else 1.0
    values = jax.random.normal(own_key, dims, jnp.float32) * width * factor_of
    return jnp.minimum(jnp.maximum(values, -reach), reach).astype(kind)


def setup_inputs(seed: int = 0) -> dict:
    seeds = jax.random.split(jax.random.key(seed), 16)
    return {
        "node_embed": scatter_about(seeds[0], (ATOMS, COEF * C), 1.0, 6.0, ((0, 256),)),
        "wigner": draw_wigner(jax.random.fold_in(seeds[15], 71), 0),
        "source": with_ends(jax.random.randint(seeds[2], (EDGES,), 0, ATOM_DEV), jax.random.fold_in(seeds[2], 1), 0, ATOM_DEV - 1).astype(jnp.int32),
        "target": with_ends(jax.random.randint(seeds[3], (EDGES,), 0, ATOM_DEV), jax.random.fold_in(seeds[3], 1), 0, ATOM_DEV - 1).astype(jnp.int32),
        "rotation": with_ends(jax.random.randint(seeds[4], (EDGES,), 0, NROT), jax.random.fold_in(seeds[4], 1), 0, NROT - 1).astype(jnp.int32),
        "edge_filter": scatter_about(seeds[5], (EDGES, C), 1.0, 6.0, ((0, 256),)),
        "edge_count": draw_edge_count(jax.random.fold_in(seeds[15], 71), 0),
        "w_zero": scatter_about(seeds[7], (14 * C, 7 * C), (14 * C) ** -0.5, 0.125, ((0, 32),)),
        "w_one_real": scatter_about(seeds[8], (12 * C, 6 * C), (24 * C) ** -0.5, 0.109375, ((0, 32),)),
        "w_one_imag": scatter_about(seeds[9], (12 * C, 6 * C), (24 * C) ** -0.5, 0.109375, ((0, 32),)),
        "w_two_real": scatter_about(seeds[10], (10 * C, 5 * C), (20 * C) ** -0.5, 0.125, ((0, 32),)),
        "w_two_imag": scatter_about(seeds[11], (10 * C, 5 * C), (20 * C) ** -0.5, 0.125, ((0, 32),)),
        "atom_struct": with_ends(jax.random.randint(seeds[12], (ATOMS,), 0, STRUCT_DEV), jax.random.fold_in(seeds[12], 1), 0, STRUCT_DEV - 1).astype(jnp.int32),
        "struct_task": with_ends(jax.random.randint(seeds[13], (STRUCTS,), 0, NTASK), jax.random.fold_in(seeds[13], 1), 0, NTASK - 1).astype(jnp.int32),
        "task_head": scatter_about(seeds[14], (NTASK, C), C ** -0.5, 0.5, (), jnp.float32),
    }


def product_full(left_side, right_side):
    return jnp.dot(left_side.astype(jnp.float32), right_side.astype(jnp.float32), precision=lax.Precision.HIGHEST)


def convolve(features, filters, weights):
    w_zero, w_one_real, w_one_imag, w_two_real, w_two_imag = weights
    number = features.shape[0]
    doubled = features.shape[2]
    channels = doubled // 2

    def section(first_row, final_row):
        return features[:, first_row:final_row, :].reshape(number, (final_row - first_row) * doubled)

    order_zero = section(0, 7)
    plus_one = section(7, 13)
    minus_one = section(13, 19)
    plus_two = section(19, 24)
    minus_two = section(24, 29)
    pieces = [
        product_full(order_zero, w_zero).reshape(number, 7, channels),
        (product_full(plus_one, w_one_real) - product_full(minus_one, w_one_imag)).reshape(number, 6, channels),
        (product_full(minus_one, w_one_real) + product_full(plus_one, w_one_imag)).reshape(number, 6, channels),
        (product_full(plus_two, w_two_real) - product_full(minus_two, w_two_imag)).reshape(number, 5, channels),
        (product_full(minus_two, w_two_real) + product_full(plus_two, w_two_imag)).reshape(number, 5, channels),
    ]
    joined = jnp.concatenate(pieces, axis=1)
    return (joined * filters[:, None, :].astype(jnp.float32)).astype(jnp.bfloat16)


def reference(node_embed, wigner, source, target, rotation, edge_filter, edge_count, w_zero, w_one_real, w_one_imag, w_two_real, w_two_imag, atom_struct, struct_task, task_head):
    weights = (w_zero, w_one_real, w_one_imag, w_two_real, w_two_imag)
    num_atoms = node_embed.shape[0]
    cube = node_embed.reshape(num_atoms, COEF, C)
    blocks_total = N_MOL * N_TASK * CAP

    def advance(summed, block):
        device = block // CAP
        first_slot = (block * BLK).astype(jnp.int32)
        atom_base = (device * ATOM_DEV).astype(jnp.int32)
        sources = lax.dynamic_slice_in_dim(source, first_slot, BLK) + atom_base
        targets = lax.dynamic_slice_in_dim(target, first_slot, BLK) + atom_base
        bins = lax.dynamic_slice_in_dim(rotation, first_slot, BLK)
        raw_filter = lax.dynamic_slice_in_dim(edge_filter, first_slot, BLK, 0)
        slots = (block % CAP) * BLK + jnp.arange(BLK, dtype=jnp.int32)
        live = slots < edge_count[device]
        filters = jnp.where(live[:, None], raw_filter, jnp.zeros_like(raw_filter))

        def compute(summed_in):
            matrices = jnp.take(wigner, bins, axis=0).astype(jnp.float32)
            pairs = jnp.concatenate((jnp.take(cube, sources, axis=0), jnp.take(cube, targets, axis=0)), axis=2).astype(jnp.float32)
            features = jnp.einsum("nij,njc->nic", matrices, pairs, precision=lax.Precision.HIGHEST).astype(jnp.bfloat16)
            message = convolve(features, filters, weights)
            back = jnp.einsum("nij,nic->njc", matrices, message.astype(jnp.float32), precision=lax.Precision.HIGHEST)
            return summed_in.at[targets].add(back.reshape(BLK, COEF * C))

        return lax.cond(jnp.any(live), compute, lambda summed_in: summed_in, summed), None

    start_sum = jnp.zeros((num_atoms, COEF * C), jnp.float32)
    summed, _ = lax.scan(advance, start_sum, jnp.arange(blocks_total, dtype=jnp.int32))
    update = summed.astype(jnp.bfloat16)
    device_of = jnp.arange(num_atoms, dtype=jnp.int32) // ATOM_DEV
    global_struct = device_of * STRUCT_DEV + atom_struct
    struct_head = jnp.take(task_head, struct_task, axis=0)
    atom_head = jnp.take(struct_head, global_struct, axis=0)
    scalar_part = node_embed[:, :C].astype(jnp.float32) + summed[:, :C]
    per_atom = jnp.sum(scalar_part * atom_head, axis=1)
    energy = jax.ops.segment_sum(per_atom, global_struct, num_segments=struct_task.shape[0])
    return update, energy
```

```python
import jax
import jax.numpy as jnp
from jax import lax
from jax.experimental import pallas as pl
from jax.experimental.pallas import tpu as pltpu
from jax.sharding import PartitionSpec as P

C = 128
COEF = 49
MROWS = 29
EDGES = 192
ATOMS = 48
NROT = 256
FLAT = MROWS * COEF
TILES = 86
VMEM = pltpu.VMEM
SMEM = pltpu.SMEM
BF = jnp.bfloat16
F32 = jnp.float32

ROWS = [[degree] for degree in range(7)]
for degree in range(1, 7):
    ROWS[degree] += [6 + degree, 12 + degree]
for degree in range(2, 7):
    ROWS[degree] += [17 + degree, 22 + degree]

MADE = (
    tuple(range(7, 19)) + (0, 1, 29),
    tuple(range(19, 29)) + (2, 3, 4, 5, 6),
)

H0 = ((0, 0), (0, -1))
H1 = ((0, 1), (0, 2))
U = (
    ((0, 0), (-1, 0)),
    ((1, 0), (4, 0)),
    ((-2, 0), (3, 0)),
    ((2, 0), (-3, 0)),
)


def moved(blocks, z, y):
    return [(a + z, b + y) for a, b in blocks]


def block_offsets():
    first = moved(H0, 0, 0) + moved(H1, 0, 0)
    for step in (1, 2, 3):
        for half in (H0, H1):
            first += moved(half, -step, 0) + moved(half, step, 0)
    first += moved(H0, -4, 0) + moved(H1, 4, 0)
    second = moved(U[0], 0, 0) + moved(U[1], 0, 0) + moved(U[2], 0, 0) + moved(U[3], 0, 0)
    for part in U:
        second += moved(part, 0, -1) + moved(part, 0, 1)
    second += moved(U[0], 0, -2) + moved(U[2], 0, 2)
    second += moved(U[1], 0, -2) + moved(U[3], 0, 2)
    return first, second


def feature_kernel(
    core, node, wig, source, target, rotation, filt, own, send, d_out, xs, xt, fz, fa, ff, sem
):
    hot_s = (source[...] == lax.broadcasted_iota(jnp.int32, (EDGES, ATOMS), 1)).astype(BF)
    hot_t = (target[...] == lax.broadcasted_iota(jnp.int32, (EDGES, ATOMS), 1)).astype(BF)
    hot_r = (rotation[...] == lax.broadcasted_iota(jnp.int32, (EDGES, NROT), 1)).astype(BF)
    d_out[...] = jnp.dot(hot_r, wig[...], preferred_element_type=F32)
    for part in range(7):
        cols = pl.ds(part * 896, 896)
        xs[:, cols] = jnp.dot(hot_s, node[:, cols], preferred_element_type=F32)
        xt[:, cols] = jnp.dot(hot_t, node[:, cols], preferred_element_type=F32)
    ff[:, :C] = filt[...]
    ff[:, C:] = filt[...]
    is_second = core[0]
    base_one = is_second * 12
    base_two = (1 - is_second) * 12

    def one_block(block, carry):
        rows = pl.ds(pl.multiple_of(block * 16, 16), 16)
        for degree in range(7):
            sums = {}
            for j in range(degree * degree, (degree + 1) * (degree + 1)):
                a = xs[rows, j * C : (j + 1) * C]
                b = xt[rows, j * C : (j + 1) * C]
                for r in ROWS[degree]:
                    k = r * COEF + j
                    d = jnp.broadcast_to(d_out[rows, k : k + 1], (16, C))
                    if r in sums:
                        sums[r] = (sums[r][0] + d * a, sums[r][1] + d * b)
                    else:
                        sums[r] = (d * a, d * b)
            for r in ROWS[degree]:
                one, two = (v.astype(BF) for v in sums[r])
                if r < 7:
                    ref, plane = fz, r
                elif r < 19:
                    ref, plane = fa, base_one + (r - 7)
                else:
                    q = r - 19
                    ref, plane = fa, base_two + (q // 5) * 6 + q % 5
                ref[plane, rows, :C] = one
                ref[plane, rows, C:] = two
        return carry

    lax.fori_loop(0, EDGES // 16, one_block, 0)
    copies = []
    for place, out in ((0, own), (12, send)):
        copies += [
            pltpu.make_async_copy(fz, out.at[pl.ds(0, 7)], sem.at[len(copies)]),
            pltpu.make_async_copy(
                fa.at[pl.ds(place, 12)], out.at[pl.ds(7, 12)], sem.at[len(copies) + 1]
            ),
            pltpu.make_async_copy(ff, out.at[19], sem.at[len(copies) + 2]),
        ]
    for copy in copies:
        copy.start()
    for copy in copies:
        copy.wait()


def features(core, node, wig, source, target, rotation, filt):
    vm = pl.BlockSpec(memory_space=VMEM)
    anywhere = pl.BlockSpec(memory_space=pl.ANY)
    return pl.pallas_call(
        feature_kernel,
        out_shape=(
            jax.ShapeDtypeStruct((20, EDGES, 2 * C), BF),
            jax.ShapeDtypeStruct((20, EDGES, 2 * C), BF),
            jax.ShapeDtypeStruct((EDGES, FLAT), F32),
        ),
        in_specs=[pl.BlockSpec(memory_space=SMEM)] + [vm] * 6,
        out_specs=(anywhere, anywhere, vm),
        scratch_shapes=[
            VMEM((EDGES, COEF * C), F32),
            VMEM((EDGES, COEF * C), F32),
            VMEM((7, EDGES, 2 * C), BF),
            VMEM((24, EDGES, 2 * C), BF),
            VMEM((EDGES, 2 * C), BF),
            pltpu.SemaphoreType.DMA((6,)),
        ],
        compiler_params=pltpu.CompilerParams(vmem_limit_bytes=40 * 2**20),
        cost_estimate=pl.CostEstimate(flops=6 * 10**9, bytes_accessed=8 * 10**6, transcendentals=0),
        name="features",
    )(core, node, wig, source, target, rotation, filt)


def weight_rows(ref, groups, first, count, g):
    per_tile = ref.at[pl.ds(first * groups, count * groups)].reshape(count, groups, 8, C)
    return per_tile[:, g].reshape(count * 8, C)


def conv_kernel(core, shard, *refs):
    blocks = refs[:18]
    own, got, mine, other, wa, wb, wc, xz, xa, fl, wsem, fsem = refs[18:]

    def fetch(per_shard):
        copies = []
        index = 0
        for block in blocks:
            for part in range(block.shape[0] // TILES):
                t = shard[index]
                first = part * TILES
                for dst, count in zip((wa, wb, wc), per_shard):
                    copies.append(
                        pltpu.make_async_copy(
                            block.at[pl.ds(first, count)],
                            dst.at[pl.ds(t * count, count)],
                            wsem.at[len(copies)],
                        )
                    )
                    first += count
                index += 1
        return copies

    def fetch_features(pieces):
        copies = []
        for who, src in enumerate((own, got)):
            for k in range(7):
                copies.append(
                    pltpu.make_async_copy(
                        src.at[k], xz.at[k, pl.ds(who * EDGES, EDGES)], fsem.at[len(copies)]
                    )
                )
            for sign in range(2):
                for k in range(pieces):
                    copies.append(
                        pltpu.make_async_copy(
                            src.at[7 + sign * 6 + k],
                            xa.at[k, pl.ds((sign * 2 + who) * EDGES, EDGES)],
                            fsem.at[len(copies)],
                        )
                    )
            copies.append(
                pltpu.make_async_copy(
                    src.at[19], fl.at[pl.ds(who * EDGES, EDGES)], fsem.at[len(copies)]
                )
            )
        return copies

    def finish(plane, value, filters):
        message = (value * filters).astype(BF)
        mine[plane] = message[:EDGES]
        other[plane] = message[EDGES:]

    def run(pieces, zero_groups, per_shard):
        waits = fetch_features(pieces) + fetch(per_shard)
        for copy in waits:
            copy.start()
        for copy in waits:
            copy.wait()
        filters = fl[:, :C].astype(F32)

        def column(g, carry):
            real = jnp.zeros((4 * EDGES, C), F32)
            imag = jnp.zeros((4 * EDGES, C), F32)
            for k in range(pieces):
                x = xa[k]
                real += jnp.dot(x, weight_rows(wa, pieces, k * 32, 32, g), preferred_element_type=F32)
                imag += jnp.dot(x, weight_rows(wb, pieces, k * 32, 32, g), preferred_element_type=F32)
            half = 2 * EDGES
            finish(g, real[:half] - imag[half:], filters)
            finish(pieces + g, real[half:] + imag[:half], filters)
            return carry

        lax.fori_loop(0, pieces, column, 0)

        def zero_column(g, carry):
            total = jnp.zeros((2 * EDGES, C), F32)
            for k in range(7):
                total += jnp.dot(
                    xz[k], weight_rows(wc, zero_groups, k * 32, 32, g), preferred_element_type=F32
                )
            finish(2 * pieces + g, total, filters)
            return carry

        lax.fori_loop(0, zero_groups, zero_column, 0)

    @pl.when(core[0] == 0)
    def _():
        run(6, 2, (36, 36, 14))

    @pl.when(core[0] == 1)
    def _():
        run(5, 5, (25, 25, 35))


def convolve(core, shard, blocks, own, got):
    vm = pl.BlockSpec(memory_space=VMEM)
    anywhere = pl.BlockSpec(memory_space=pl.ANY)
    smem = pl.BlockSpec(memory_space=SMEM)
    out = jax.ShapeDtypeStruct((15, EDGES, C), BF)
    return pl.pallas_call(
        conv_kernel,
        out_shape=(out, out),
        in_specs=[smem, smem] + [anywhere] * 20,
        out_specs=(vm, vm),
        scratch_shapes=[
            VMEM((32 * 36, 8, C), BF),
            VMEM((32 * 36, 8, C), BF),
            VMEM((32 * 35, 8, C), BF),
            VMEM((7, 2 * EDGES, 2 * C), BF),
            VMEM((6, 4 * EDGES, 2 * C), BF),
            VMEM((2 * EDGES, 2 * C), BF),
            pltpu.SemaphoreType.DMA((96,)),
            pltpu.SemaphoreType.DMA((40,)),
        ],
        compiler_params=pltpu.CompilerParams(vmem_limit_bytes=40 * 2**20),
        cost_estimate=pl.CostEstimate(flops=4 * 10**9, bytes_accessed=12 * 10**6, transcendentals=0),
        name="convolve",
    )(core, shard, *blocks, own, got)


def back_kernel(
    place_mine, place_got, task, mine, got, d, target, node, struct, head, update, energy, m, hi, lo, sem
):
    copies = []
    for i in range(15):
        copies.append(pltpu.make_async_copy(mine.at[i], m.at[place_mine[i]], sem.at[2 * i]))
        copies.append(pltpu.make_async_copy(got.at[i], m.at[place_got[i]], sem.at[2 * i + 1]))
    for copy in copies:
        copy.start()
    for copy in copies:
        copy.wait()

    def one_block(block, carry):
        rows = pl.ds(pl.multiple_of(block * 16, 16), 16)
        for degree in range(7):
            parts = {r: m[r, rows, :].astype(F32) for r in ROWS[degree]}
            for j in range(degree * degree, (degree + 1) * (degree + 1)):
                total = None
                for r in ROWS[degree]:
                    k = r * COEF + j
                    term = jnp.broadcast_to(d[rows, k : k + 1], (16, C)) * parts[r]
                    total = term if total is None else total + term
                top = total.astype(BF)
                hi[rows, j * C : (j + 1) * C] = top
                lo[rows, j * C : (j + 1) * C] = (total - top.astype(F32)).astype(BF)
        return carry

    lax.fori_loop(0, EDGES // 16, one_block, 0)
    hot = (target[...] == lax.broadcasted_iota(jnp.int32, (ATOMS, EDGES), 0)).astype(BF)
    for part in range(7):
        cols = pl.ds(part * 896, 896)
        total = jnp.dot(hot, hi[:, cols], preferred_element_type=F32) + jnp.dot(
            hot, lo[:, cols], preferred_element_type=F32
        )
        update[:, cols] = total.astype(BF)
        if part == 0:
            scalar_part = node[:, :C].astype(F32) + total[:, :C]
    lane = lax.broadcasted_iota(jnp.int32, (1, C), 1)
    result = jnp.zeros((1, C), F32)
    for s in range(4):
        member = jnp.where(struct[...] == s, scalar_part, 0.0) * head[pl.ds(task[s], 1), :]
        value = jnp.sum(jnp.sum(member, axis=0, keepdims=True), axis=1, keepdims=True)
        result = jnp.where(lane == s, value, result)
    energy[...] = result


def turn_back(place_mine, place_got, task, mine, got, d, target, node, struct, head):
    vm = pl.BlockSpec(memory_space=VMEM)
    anywhere = pl.BlockSpec(memory_space=pl.ANY)
    smem = pl.BlockSpec(memory_space=SMEM)
    return pl.pallas_call(
        back_kernel,
        out_shape=(
            jax.ShapeDtypeStruct((ATOMS, COEF * C), BF),
            jax.ShapeDtypeStruct((1, C), F32),
        ),
        in_specs=[smem] * 3 + [anywhere] * 2 + [vm] * 5,
        out_specs=(vm, vm),
        scratch_shapes=[
            VMEM((30, EDGES, C), BF),
            VMEM((EDGES, COEF * C), BF),
            VMEM((EDGES, COEF * C), BF),
            pltpu.SemaphoreType.DMA((30,)),
        ],
        compiler_params=pltpu.CompilerParams(vmem_limit_bytes=40 * 2**20),
        cost_estimate=pl.CostEstimate(flops=10**9, bytes_accessed=4 * 10**6, transcendentals=0),
        name="turn_back",
    )(place_mine, place_got, task, mine, got, d, target, node, struct, head)


def exchange(value, sizes, steps_first, steps_second):
    mol, nz, ny = sizes
    pairs = []
    for device in range(mol * nz * ny):
        m, t = divmod(device, nz * ny)
        z, y = divmod(t, ny)
        dz, dy = steps_first if m % 2 == 0 else steps_second
        to = ((z + dz) % nz) * ny + (y + dy) % ny
        pairs.append((device, m * nz * ny + to))
    return lax.ppermute(value, ("mol", "task"), pairs)


def tiles_of(w):
    rows, cols = w.shape
    return w.reshape(rows // 8, 8, cols // C, C).transpose(0, 2, 1, 3).reshape(-1, 8, C)


def body(
    node_embed,
    wigner,
    source,
    target,
    rotation,
    edge_filter,
    edge_count,
    w_zero,
    w_one_real,
    w_one_imag,
    w_two_real,
    w_two_imag,
    atom_struct,
    struct_task,
    task_head,
):
    sizes = (8, 8, 4)
    core = lax.axis_index("mol") % 2
    task = lax.axis_index("task")
    z, y = task // 4, task % 4
    first = core == 0

    def pick(a, b):
        return jnp.where(first, a, b)

    zero_tiles = w_zero
    pack_first = jnp.concatenate(
        (tiles_of(w_one_real), tiles_of(w_one_imag), tiles_of(zero_tiles[:, : 2 * C]))
    )
    pack_second = jnp.concatenate(
        (
            tiles_of(w_two_real),
            tiles_of(w_two_imag),
            tiles_of(zero_tiles[:, 2 * C :]),
            jnp.zeros((1, 8, C), BF),
        )
    )
    b0 = pick(pack_first, pack_second)
    a1 = exchange(b0, sizes, (0, 1), (1, 0))
    a2 = exchange(b0, sizes, (0, -1), (-1, 0))
    a3 = exchange(b0, sizes, (0, 2), (4, 0))
    h0 = jnp.concatenate((b0, a1))
    h1 = jnp.concatenate((a2, a3))

    def forth(value, second=(0, 1)):
        return exchange(value, sizes, (1, 0), second)

    def aft(value, second=(0, -1)):
        return exchange(value, sizes, (-1, 0), second)

    p1p = forth(pick(h0, jnp.concatenate((a1, a3))), (1, 0))
    p1m = aft(pick(h0, h1), (-1, 0))
    s2 = pick(h1, h0)
    p2p, p2m = forth(s2), aft(s2)
    p3p, p3m = forth(pick(p1p, h1)), aft(pick(p1m, h1))
    p4p, p4m = forth(pick(p2p, p1p)), aft(pick(p2m, p1p))
    p5p, p5m = forth(pick(p3p, p1m)), aft(pick(p3m, p1m))
    p6p, p6m = forth(pick(p4p, p2p)), aft(p4m)
    p7p, p7m = forth(pick(p5p, p3p)), aft(pick(p6m, p5m))

    blocks = (b0, a1, a2, a3, p1p, p1m, p2p, p2m, p3p, p3m, p4p, p4m, p5p, p5m, p6p, p6m, p7p, p7m)
    offsets_first, offsets_second = block_offsets()
    table = jnp.asarray((offsets_first, offsets_second), jnp.int32)[core]
    shard = ((z + table[:, 0]) % 8) * 4 + (y + table[:, 1]) % 4

    live = (jnp.arange(EDGES, dtype=jnp.int32) < edge_count[0])[:, None]
    filters = jnp.where(live, edge_filter, jnp.zeros_like(edge_filter))
    core_vec = core.reshape(1).astype(jnp.int32)
    own, send, d = features(
        core_vec,
        node_embed,
        wigner.reshape(NROT, FLAT),
        source.reshape(EDGES, 1),
        target.reshape(EDGES, 1),
        rotation.reshape(EDGES, 1),
        filters,
    )
    swap = [(i, i ^ 1) for i in range(8)]
    got = lax.ppermute(send, "mol", swap)
    mine, other = convolve(core_vec, shard, blocks, own, got)
    back = lax.ppermute(other, "mol", swap)
    places = jnp.asarray(MADE, jnp.int32)
    update, energy = turn_back(
        places[core],
        places[1 - core],
        struct_task,
        mine,
        back,
        d,
        target.reshape(1, EDGES),
        node_embed,
        atom_struct.reshape(ATOMS, 1),
        task_head,
    )
    return update, energy[0, :4]


def solution(mesh):
    both = P(("mol", "task"))
    wide = P(("mol", "task"), None)
    rows = P("task", None)
    in_specs = (wide, P(), both, both, both, wide, both, rows, rows, rows, rows, rows, both, both, P())
    return jax.shard_map(
        body, mesh=mesh, in_specs=in_specs, out_specs=(wide, both), check_vma=False
    )
```

```python
import jax
import jax.numpy as jnp
from jax import lax
from jax.experimental import pallas as pl
from jax.experimental.pallas import tpu as pltpu
from jax.sharding import PartitionSpec as P

C = 128
COEF = 49
MROWS = 29
EDGES = 192
ATOMS = 48
NROT = 256
TILES = 86
VMEM = pltpu.VMEM
SMEM = pltpu.SMEM
BF = jnp.bfloat16
F32 = jnp.float32

ROWS = [[degree] for degree in range(7)]
for degree in range(1, 7):
    ROWS[degree] += [6 + degree, 12 + degree]
for degree in range(2, 7):
    ROWS[degree] += [17 + degree, 22 + degree]

MADE = (
    tuple(range(7, 19)) + (0, 1, 29),
    tuple(range(19, 29)) + (2, 3, 4, 5, 6),
)

H0 = ((0, 0), (0, -1))
H1 = ((0, 1), (0, 2))
U = (
    ((0, 0), (-1, 0)),
    ((1, 0), (4, 0)),
    ((-2, 0), (3, 0)),
    ((2, 0), (-3, 0)),
)


def moved(blocks, z, y):
    return [(a + z, b + y) for a, b in blocks]


def block_offsets():
    first = moved(H0, 0, 0) + moved(H1, 0, 0) + moved(H0, -1, 0) + moved(H1, 1, 0)
    for step in (1, 2, 3):
        first += moved(H1, -step, 0) + moved(H0, -step - 1, 0)
        first += moved(H0, step, 0) + moved(H1, step + 1, 0)
    second = [block for part in U for block in part]
    for part in (0, 2):
        for y in (-1, 1):
            second += moved(U[part], 0, y) + moved(U[part + 1], 0, y)
    for part in (0, 2):
        second += moved(U[part], 0, 2) + moved(U[part + 1], 0, 2)
    return first, second


def feature_kernel(
    core, node, wig, source, target, rotation, filt, own, send, wc_out, x, xs, xt, wc, fz, fa, ff, sem
):
    wc[...] = jnp.zeros_like(wc)
    for degree in range(7):
        at = degree * degree
        for r in ROWS[degree]:
            wc[r * 16 : r * 16 + 2 * degree + 1, :] = wig[r, at : at + 2 * degree + 1, :].astype(F32)
    entries = wc[...].astype(BF)
    wc_out[...] = entries
    for j in range(COEF):
        x[j * ATOMS : (j + 1) * ATOMS, :] = node[:, j * C : (j + 1) * C]
    width = 13 * ATOMS
    lane = lax.broadcasted_iota(jnp.int32, (1, width), 1)
    atom = lane % ATOMS
    xs[...] = (source[...] == atom).astype(F32).astype(BF)
    xt[...] = (target[...] == atom).astype(F32).astype(BF)
    hot_r = (rotation[...] == lax.broadcasted_iota(jnp.int32, (1, NROT), 1)).astype(F32).astype(BF)
    d_all = lax.dot_general(
        hot_r, entries, (((1,), (1,)), ((), ())), preferred_element_type=F32
    ).astype(BF)
    ff[:, :C] = filt[...]
    ff[:, C:] = filt[...]
    is_second = core[0]
    base_one = is_second * 12
    base_two = (1 - is_second) * 12
    for degree in range(7):
        wide = (2 * degree + 1) * ATOMS
        at = degree * degree
        which = lax.broadcasted_iota(jnp.int32, (C, wide), 0)
        which = which - lax.broadcasted_iota(jnp.int32, (C, wide), 1) // ATOMS
        coefs = x[at * ATOMS : at * ATOMS + wide, :]
        for r in ROWS[degree]:
            part, offset = divmod(r, 8)
            spread = (which == offset * 16).astype(F32).astype(BF)
            d = d_all[:, part * C : (part + 1) * C]
            d = jnp.dot(d, spread, preferred_element_type=F32).astype(BF)
            one = jnp.dot(d * xs[:, :wide], coefs, preferred_element_type=F32).astype(BF)
            two = jnp.dot(d * xt[:, :wide], coefs, preferred_element_type=F32).astype(BF)
            if r < 7:
                ref, plane = fz, r
            elif r < 19:
                ref, plane = fa, base_one + (r - 7)
            else:
                q = r - 19
                ref, plane = fa, base_two + (q // 5) * 6 + q % 5
            ref[plane, :, :C] = one
            ref[plane, :, C:] = two
    copies = []
    for place, out in ((0, own), (12, send)):
        copies += [
            pltpu.make_async_copy(fz, out.at[pl.ds(0, 7)], sem.at[len(copies)]),
            pltpu.make_async_copy(
                fa.at[pl.ds(place, 12)], out.at[pl.ds(7, 12)], sem.at[len(copies) + 1]
            ),
            pltpu.make_async_copy(ff, out.at[19], sem.at[len(copies) + 2]),
        ]
    for copy in copies:
        copy.start()
    for copy in copies:
        copy.wait()


def features(core, node, wig, source, target, rotation, filt):
    vm = pl.BlockSpec(memory_space=VMEM)
    anywhere = pl.BlockSpec(memory_space=pl.ANY)
    return pl.pallas_call(
        feature_kernel,
        out_shape=(
            jax.ShapeDtypeStruct((20, EDGES, 2 * C), BF),
            jax.ShapeDtypeStruct((20, EDGES, 2 * C), BF),
            jax.ShapeDtypeStruct((4 * C, NROT), BF),
        ),
        in_specs=[pl.BlockSpec(memory_space=SMEM)] + [vm] * 6,
        out_specs=(anywhere, anywhere, vm),
        scratch_shapes=[
            VMEM((COEF * ATOMS, C), BF),
            VMEM((EDGES, 13 * ATOMS), BF),
            VMEM((EDGES, 13 * ATOMS), BF),
            VMEM((4 * C, NROT), F32),
            VMEM((7, EDGES, 2 * C), BF),
            VMEM((24, EDGES, 2 * C), BF),
            VMEM((EDGES, 2 * C), BF),
            pltpu.SemaphoreType.DMA((6,)),
        ],
        compiler_params=pltpu.CompilerParams(vmem_limit_bytes=16 * 2**20),
        cost_estimate=pl.CostEstimate(flops=6 * 10**9, bytes_accessed=8 * 10**6, transcendentals=0),
        name="features",
    )(core, node, wig, source, target, rotation, filt)


def conv_kernel(core, shard, *refs):
    blocks = refs[:12]
    own, got, mine, other, w_all, xz, xa, fl, fsem = refs[12:]

    def place_blocks():
        index = 0
        for block in blocks:
            for part in range(block.shape[0] // TILES):
                w_all[shard[index]] = block[part * TILES : (part + 1) * TILES]
                index += 1

    def rows_of(first, count, g):
        tiles = w_all[:, pl.ds(first + g * count, count)]
        return tiles.reshape(32 * count * 8, C)

    def fetch_features(pieces):
        copies = []

        def add(src, dst):
            copies.append(pltpu.make_async_copy(src, dst, fsem.at[len(copies)]))

        for who, src in enumerate((own, got)):
            for k in range(7):
                add(src.at[k], xz.at[pl.ds(who * EDGES, EDGES), pl.ds(k * 2 * C, 2 * C)])
            for sign in range(2):
                for k in range(pieces):
                    add(
                        src.at[7 + sign * 6 + k],
                        xa.at[pl.ds((sign * 2 + who) * EDGES, EDGES), pl.ds(k * 2 * C, 2 * C)],
                    )
            add(src.at[19], fl.at[pl.ds(who * EDGES, EDGES)])
        return copies

    def finish(plane, value, filters):
        message = (value * filters).astype(BF)
        mine[plane] = message[:EDGES]
        other[plane] = message[EDGES:]

    def run(pieces, tiles, zero_groups):
        waits = fetch_features(pieces)
        for copy in waits:
            copy.start()
        place_blocks()
        for copy in waits:
            copy.wait()
        filters = fl[:, :C].astype(F32)
        deep = pieces * 2 * C
        half = 2 * EDGES
        size = pieces * tiles

        def column(g, carry):
            w = jnp.concatenate(
                (rows_of(0, tiles, g), rows_of(size, tiles, g)), axis=1
            )
            both = jnp.dot(xa[:, :deep], w, preferred_element_type=F32)
            finish(g, both[:half, :C] - both[half:, C:], filters)
            finish(pieces + g, both[half:, :C] + both[:half, C:], filters)
            return carry

        lax.fori_loop(0, pieces, column, 0)
        for g in range(0, zero_groups, 2):
            count = min(2, zero_groups - g)
            w = jnp.concatenate(
                [rows_of(2 * size, 7, g + i) for i in range(count)], axis=1
            )
            total = jnp.dot(xz[...], w, preferred_element_type=F32)
            for i in range(count):
                finish(2 * pieces + g + i, total[:, i * C : (i + 1) * C], filters)

    @pl.when(core[0] == 0)
    def _():
        run(6, 6, 2)

    @pl.when(core[0] == 1)
    def _():
        run(5, 5, 5)


def convolve(core, shard, blocks, own, got):
    vm = pl.BlockSpec(memory_space=VMEM)
    anywhere = pl.BlockSpec(memory_space=pl.ANY)
    smem = pl.BlockSpec(memory_space=SMEM)
    out = jax.ShapeDtypeStruct((15, EDGES, C), BF)
    return pl.pallas_call(
        conv_kernel,
        out_shape=(out, out),
        in_specs=[smem, smem] + [vm] * 12 + [anywhere] * 2,
        out_specs=(vm, vm),
        scratch_shapes=[
            VMEM((32, TILES, 8, C), BF),
            VMEM((2 * EDGES, 14 * C), BF),
            VMEM((4 * EDGES, 12 * C), BF),
            VMEM((2 * EDGES, 2 * C), BF),
            pltpu.SemaphoreType.DMA((40,)),
        ],
        compiler_params=pltpu.CompilerParams(vmem_limit_bytes=24 * 2**20),
        cost_estimate=pl.CostEstimate(flops=4 * 10**9, bytes_accessed=12 * 10**6, transcendentals=0),
        name="convolve",
    )(core, shard, *blocks, own, got)


def back_kernel(
    place_mine, place_got, task, mine, got, wig, rotation, target, node, struct, head, update, energy, m, d, sem
):
    copies = []
    for i in range(15):
        copies.append(
            pltpu.make_async_copy(mine.at[i], m.at[place_mine[i], pl.ds(0, EDGES)], sem.at[2 * i])
        )
        copies.append(
            pltpu.make_async_copy(got.at[i], m.at[place_got[i], pl.ds(0, EDGES)], sem.at[2 * i + 1])
        )
    for copy in copies:
        copy.start()
    hot_r = lax.broadcasted_iota(jnp.int32, (NROT, EDGES), 0) == rotation[...]
    hot_r = hot_r.astype(F32).astype(BF)
    d[...] = jnp.dot(wig[...], hot_r, preferred_element_type=F32)
    ends = lax.broadcasted_iota(jnp.int32, (ATOMS, EDGES), 0) == target[...]
    for copy in copies:
        copy.wait()
    for degree in range(7):
        span = range(degree * degree, (degree + 1) * (degree + 1))
        total = None
        for r in ROWS[degree]:
            hot = jnp.concatenate(
                [jnp.where(ends, d[r * 16 + j : r * 16 + j + 1, :], 0.0).astype(BF) for j in range(len(span))],
                axis=0,
            )
            term = jnp.dot(hot, m[r], preferred_element_type=F32)
            total = term if total is None else total + term
        for place, j in enumerate(span):
            value = total[place * ATOMS : (place + 1) * ATOMS]
            update[:, j * C : (j + 1) * C] = value.astype(BF)
            if j == 0:
                scalar_part = node[:, :C].astype(F32) + value
    lane = lax.broadcasted_iota(jnp.int32, (1, C), 1)
    result = jnp.zeros((1, C), F32)
    for s in range(4):
        member = jnp.where(struct[...] == s, scalar_part, 0.0) * head[pl.ds(task[s], 1), :]
        value = jnp.sum(jnp.sum(member, axis=0, keepdims=True), axis=1, keepdims=True)
        result = jnp.where(lane == s, value, result)
    energy[...] = result


def turn_back(place_mine, place_got, task, mine, got, wig, rotation, target, node, struct, head):
    vm = pl.BlockSpec(memory_space=VMEM)
    anywhere = pl.BlockSpec(memory_space=pl.ANY)
    smem = pl.BlockSpec(memory_space=SMEM)
    return pl.pallas_call(
        back_kernel,
        out_shape=(
            jax.ShapeDtypeStruct((ATOMS, COEF * C), BF),
            jax.ShapeDtypeStruct((1, C), F32),
        ),
        in_specs=[smem] * 3 + [anywhere] * 2 + [vm] * 6,
        out_specs=(vm, vm),
        scratch_shapes=[
            VMEM((30, EDGES, C), BF),
            VMEM((4 * C, EDGES), F32),
            pltpu.SemaphoreType.DMA((30,)),
        ],
        compiler_params=pltpu.CompilerParams(vmem_limit_bytes=16 * 2**20),
        cost_estimate=pl.CostEstimate(flops=10**9, bytes_accessed=4 * 10**6, transcendentals=0),
        name="turn_back",
    )(place_mine, place_got, task, mine, got, wig, rotation, target, node, struct, head)


def exchange(value, sizes, steps_first, steps_second):
    mol, nz, ny = sizes
    pairs = []
    for device in range(mol * nz * ny):
        m, t = divmod(device, nz * ny)
        z, y = divmod(t, ny)
        dz, dy = steps_first if m % 2 == 0 else steps_second
        to = ((z + dz) % nz) * ny + (y + dy) % ny
        pairs.append((device, m * nz * ny + to))
    return lax.ppermute(value, ("mol", "task"), pairs)


def tiles_of(w):
    rows, cols = w.shape
    return w.reshape(rows // 8, 8, cols // C, C).transpose(2, 0, 1, 3).reshape(-1, 8, C)


def body(
    node_embed,
    wigner,
    source,
    target,
    rotation,
    edge_filter,
    edge_count,
    w_zero,
    w_one_real,
    w_one_imag,
    w_two_real,
    w_two_imag,
    atom_struct,
    struct_task,
    task_head,
):
    sizes = (8, 8, 4)
    core = lax.axis_index("mol") % 2
    task = lax.axis_index("task")
    z, y = task // 4, task % 4
    first = core == 0

    def pick(a, b):
        return jnp.where(first, a, b)

    zero_tiles = w_zero
    pack_first = jnp.concatenate(
        (tiles_of(w_one_real), tiles_of(w_one_imag), tiles_of(zero_tiles[:, : 2 * C]))
    )
    pack_second = jnp.concatenate(
        (
            tiles_of(w_two_real),
            tiles_of(w_two_imag),
            tiles_of(zero_tiles[:, 2 * C :]),
            jnp.zeros((1, 8, C), BF),
        )
    )
    b0 = pick(pack_first, pack_second)
    a1 = exchange(b0, sizes, (0, 1), (1, 0))
    a2 = exchange(b0, sizes, (0, -1), (-1, 0))
    a3 = exchange(b0, sizes, (0, 2), (4, 0))
    h0 = jnp.concatenate((b0, a1))
    h1 = jnp.concatenate((a2, a3))

    def forth(value, second=(0, 1)):
        return exchange(value, sizes, (1, 0), second)

    def aft(value, second=(0, -1)):
        return exchange(value, sizes, (-1, 0), second)

    p1p = forth(pick(h0, jnp.concatenate((a1, a3))), (1, 0))
    p1m = aft(h1, (-1, 0))
    s1p = forth(jnp.concatenate((pick(h1, h0), pick(p1p, h1))))
    s1m = aft(jnp.concatenate((h0, pick(p1m, h1))))
    p1 = jnp.concatenate((p1p, p1m))
    s2p, s2m = forth(pick(s1p, p1)), aft(pick(s1m, p1))
    s3p, s3m = forth(pick(s2p, s1p)), aft(s2m)

    blocks = (b0, a1, a2, a3, p1p, p1m, s1p, s1m, s2p, s2m, s3p, s3m)
    offsets_first, offsets_second = block_offsets()
    table = jnp.asarray((offsets_first, offsets_second), jnp.int32)[core]
    shard = ((z + table[:, 0]) % 8) * 4 + (y + table[:, 1]) % 4

    live = (jnp.arange(EDGES, dtype=jnp.int32) < edge_count[0])[:, None]
    filters = jnp.where(live, edge_filter, jnp.zeros_like(edge_filter))
    core_vec = core.reshape(1).astype(jnp.int32)
    own, send, entries = features(
        core_vec,
        node_embed,
        wigner.transpose(1, 2, 0),
        source.reshape(EDGES, 1),
        target.reshape(EDGES, 1),
        rotation.reshape(EDGES, 1),
        filters,
    )
    swap = [(i, i ^ 1) for i in range(8)]
    got = lax.ppermute(send, "mol", swap)
    mine, other = convolve(core_vec, shard, blocks, own, got)
    back = lax.ppermute(other, "mol", swap)
    places = jnp.asarray(MADE, jnp.int32)
    update, energy = turn_back(
        places[core],
        places[1 - core],
        struct_task,
        mine,
        back,
        entries,
        rotation.reshape(1, EDGES),
        target.reshape(1, EDGES),
        node_embed,
        atom_struct.reshape(ATOMS, 1),
        task_head,
    )
    return update, energy[0, :4]


def solution(mesh):
    both = P(("mol", "task"))
    wide = P(("mol", "task"), None)
    rows = P("task", None)
    in_specs = (wide, P(), both, both, both, wide, both, rows, rows, rows, rows, rows, both, both, P())
    return jax.shard_map(
        body, mesh=mesh, in_specs=in_specs, out_specs=(wide, both), check_vma=False
    )
```

```python
import jax
import jax.numpy as jnp
from jax import lax
from jax.experimental import pallas as pl
from jax.experimental.pallas import tpu as pltpu
from jax.sharding import PartitionSpec as P

C = 128
COEF = 49
MROWS = 29
EDGES = 192
ATOMS = 48
NROT = 256
TILES = 86
LATE = 8
VMEM = pltpu.VMEM
SMEM = pltpu.SMEM
BF = jnp.bfloat16
F32 = jnp.float32

ROWS = [[degree] for degree in range(7)]
for degree in range(1, 7):
    ROWS[degree] += [6 + degree, 12 + degree]
for degree in range(2, 7):
    ROWS[degree] += [17 + degree, 22 + degree]

MADE = (
    tuple(range(7, 19)) + (0, 1, 29),
    tuple(range(19, 29)) + (2, 3, 4, 5, 6),
)

H0 = ((0, 0), (0, -1))
H1 = ((0, 1), (0, 2))
U = (
    ((0, 0), (-1, 0)),
    ((1, 0), (4, 0)),
    ((-2, 0), (3, 0)),
    ((2, 0), (-3, 0)),
)


def moved(blocks, z, y):
    return [(a + z, b + y) for a, b in blocks]


def block_offsets():
    first = moved(H0, 0, 0) + moved(H1, 0, 0) + moved(H0, -1, 0) + moved(H1, 1, 0)
    for step in (1, 2, 3):
        first += moved(H1, -step, 0) + moved(H0, -step - 1, 0)
        first += moved(H0, step, 0) + moved(H1, step + 1, 0)
    second = [block for part in U for block in part]
    for part in (0, 2):
        for y in (-1, 1):
            second += moved(U[part], 0, y) + moved(U[part + 1], 0, y)
    for part in (0, 2):
        second += moved(U[part], 0, 2) + moved(U[part + 1], 0, 2)
    return first, second


def feature_kernel(
    core, node, wig, source, target, rotation, filt, own, send, wc_out, x, xs, xt, wc, fz, fa, ff, sem
):
    wc[...] = jnp.zeros_like(wc)
    for degree in range(7):
        at = degree * degree
        for r in ROWS[degree]:
            wc[r * 16 : r * 16 + 2 * degree + 1, :] = wig[r, at : at + 2 * degree + 1, :].astype(F32)
    entries = wc[...].astype(BF)
    wc_out[...] = entries
    for j in range(COEF):
        x[j * ATOMS : (j + 1) * ATOMS, :] = node[:, j * C : (j + 1) * C]
    width = 13 * ATOMS
    lane = lax.broadcasted_iota(jnp.int32, (1, width), 1)
    atom = lane % ATOMS
    xs[...] = (source[...] == atom).astype(F32).astype(BF)
    xt[...] = (target[...] == atom).astype(F32).astype(BF)
    hot_r = (rotation[...] == lax.broadcasted_iota(jnp.int32, (1, NROT), 1)).astype(F32).astype(BF)
    d_all = lax.dot_general(
        hot_r, entries, (((1,), (1,)), ((), ())), preferred_element_type=F32
    ).astype(BF)
    ff[:, :C] = filt[...]
    ff[:, C:] = filt[...]
    is_second = core[0]
    base_one = is_second * 12
    base_two = (1 - is_second) * 12
    for degree in range(7):
        wide = (2 * degree + 1) * ATOMS
        at = degree * degree
        which = lax.broadcasted_iota(jnp.int32, (C, wide), 0)
        which = which - lax.broadcasted_iota(jnp.int32, (C, wide), 1) // ATOMS
        coefs = x[at * ATOMS : at * ATOMS + wide, :]
        for r in ROWS[degree]:
            part, offset = divmod(r, 8)
            spread = (which == offset * 16).astype(F32).astype(BF)
            d = d_all[:, part * C : (part + 1) * C]
            d = jnp.dot(d, spread, preferred_element_type=F32).astype(BF)
            one = jnp.dot(d * xs[:, :wide], coefs, preferred_element_type=F32).astype(BF)
            two = jnp.dot(d * xt[:, :wide], coefs, preferred_element_type=F32).astype(BF)
            if r < 7:
                ref, plane = fz, r
            elif r < 19:
                ref, plane = fa, base_one + (r - 7)
            else:
                q = r - 19
                ref, plane = fa, base_two + (q // 5) * 6 + q % 5
            ref[plane, :, :C] = one
            ref[plane, :, C:] = two
    copies = []
    for place, out in ((0, own), (12, send)):
        copies += [
            pltpu.make_async_copy(fz, out.at[pl.ds(0, 7)], sem.at[len(copies)]),
            pltpu.make_async_copy(
                fa.at[pl.ds(place, 12)], out.at[pl.ds(7, 12)], sem.at[len(copies) + 1]
            ),
            pltpu.make_async_copy(ff, out.at[19], sem.at[len(copies) + 2]),
        ]
    for copy in copies:
        copy.start()
    for copy in copies:
        copy.wait()


def features(core, node, wig, source, target, rotation, filt):
    vm = pl.BlockSpec(memory_space=VMEM)
    anywhere = pl.BlockSpec(memory_space=pl.ANY)
    return pl.pallas_call(
        feature_kernel,
        out_shape=(
            jax.ShapeDtypeStruct((20, EDGES, 2 * C), BF),
            jax.ShapeDtypeStruct((20, EDGES, 2 * C), BF),
            jax.ShapeDtypeStruct((4 * C, NROT), BF),
        ),
        in_specs=[pl.BlockSpec(memory_space=SMEM)] + [vm] * 6,
        out_specs=(anywhere, anywhere, vm),
        scratch_shapes=[
            VMEM((COEF * ATOMS, C), BF),
            VMEM((EDGES, 13 * ATOMS), BF),
            VMEM((EDGES, 13 * ATOMS), BF),
            VMEM((4 * C, NROT), F32),
            VMEM((7, EDGES, 2 * C), BF),
            VMEM((24, EDGES, 2 * C), BF),
            VMEM((EDGES, 2 * C), BF),
            pltpu.SemaphoreType.DMA((6,)),
        ],
        compiler_params=pltpu.CompilerParams(vmem_limit_bytes=8 * 2**20),
        cost_estimate=pl.CostEstimate(flops=6 * 10**9, bytes_accessed=8 * 10**6, transcendentals=0),
        name="features",
    )(core, node, wig, source, target, rotation, filt)


def pack_kernel(core, zero, one_real, one_imag, two_real, two_imag, out):
    def run(parts):
        at = 0
        for ref, first, groups in parts:
            tiles = ref.shape[0] // 8
            for g in range(first, first + groups):
                out[at : at + tiles] = ref[:, g * C : (g + 1) * C].reshape(tiles, 8, C)
                at += tiles
        if at < TILES:
            out[at:] = jnp.zeros((TILES - at, 8, C), BF)

    @pl.when(core[0] == 0)
    def _():
        run(((one_real, 0, 6), (one_imag, 0, 6), (zero, 0, 2)))

    @pl.when(core[0] == 1)
    def _():
        run(((two_real, 0, 5), (two_imag, 0, 5), (zero, 2, 5)))


def pack(core, zero, one_real, one_imag, two_real, two_imag):
    vm = pl.BlockSpec(memory_space=VMEM)
    return pl.pallas_call(
        pack_kernel,
        out_shape=jax.ShapeDtypeStruct((TILES, 8, C), BF),
        in_specs=[pl.BlockSpec(memory_space=SMEM)] + [vm] * 5,
        out_specs=vm,
        compiler_params=pltpu.CompilerParams(vmem_limit_bytes=4 * 2**20),
        name="pack",
    )(core, zero, one_real, one_imag, two_real, two_imag)


def by_core(core, run):
    @pl.when(core[0] == 0)
    def _():
        run(6, 6, 2)

    @pl.when(core[0] == 1)
    def _():
        run(5, 5, 5)


def group_rows(held, first, count, g):
    tiles = held[:, pl.ds(first + g * count, count)]
    return tiles.reshape(held.shape[0] * count * 8, C)


def early_kernel(core, shard, *refs):
    blocks = refs[:10]
    own, got, part, part_zero, late, late_zero, w_all, xz, xa, fsem = refs[10:]

    def fetch_features(pieces):
        copies = []

        def add(src, dst):
            copies.append(pltpu.make_async_copy(src, dst, fsem.at[len(copies)]))

        for who, src in enumerate((own, got)):
            for k in range(7):
                add(src.at[k], xz.at[pl.ds(who * EDGES, EDGES), pl.ds(k * 2 * C, 2 * C)])
            for sign in range(2):
                for k in range(pieces):
                    add(
                        src.at[7 + sign * 6 + k],
                        xa.at[pl.ds((sign * 2 + who) * EDGES, EDGES), pl.ds(k * 2 * C, 2 * C)],
                    )
        return copies

    def chosen(rows, deep):
        lane = lax.broadcasted_iota(jnp.int32, (1, LATE * rows), 1)
        wanted = lane
        for i in range(LATE):
            here = jnp.logical_and(lane >= i * rows, lane < (i + 1) * rows)
            wanted = jnp.where(here, lane + (shard[32 - LATE + i] - i) * rows, wanted)
        return (lax.broadcasted_iota(jnp.int32, (deep, 1), 0) == wanted).astype(F32).astype(BF)

    def run(pieces, tiles, zero_groups):
        copies = fetch_features(pieces)
        for copy in copies:
            copy.start()
        for copy in copies:
            copy.wait()
        deep = pieces * 2 * C
        size = pieces * tiles

        def column(g, carry):
            w = jnp.concatenate(
                (group_rows(w_all, 0, tiles, g), group_rows(w_all, size, tiles, g)), axis=1
            )
            part[g] = jnp.dot(xa[:, :deep], w, preferred_element_type=F32)
            return carry

        lax.fori_loop(0, pieces, column, 0)
        for g in range(0, zero_groups, 2):
            count = min(2, zero_groups - g)
            w = jnp.concatenate(
                [group_rows(w_all, 2 * size, 7, g + i) for i in range(count)], axis=1
            )
            part_zero[g // 2, :, : count * C] = jnp.dot(xz[...], w, preferred_element_type=F32)
        rows = tiles * 8
        late[:, : LATE * rows] = jnp.dot(
            xa[:, :deep], chosen(rows, deep), preferred_element_type=F32
        ).astype(BF)
        late_zero[...] = jnp.dot(
            xz[...], chosen(56, 14 * C), preferred_element_type=F32
        ).astype(BF)

    def place(block, index):
        def one(i, carry):
            w_all[shard[index + i]] = block[pl.ds(i * TILES, TILES)]
            return carry

        lax.fori_loop(0, block.shape[0] // TILES, one, 0)

    index = 0
    for block in blocks:
        place(block, index)
        index += block.shape[0] // TILES

    def clear(i, carry):
        w_all[shard[32 - LATE + i]] = jnp.zeros((TILES, 8, C), BF)
        return carry

    lax.fori_loop(0, LATE, clear, 0)
    by_core(core, run)


def mix_early(core, shard, blocks, own, got):
    vm = pl.BlockSpec(memory_space=VMEM)
    anywhere = pl.BlockSpec(memory_space=pl.ANY)
    smem = pl.BlockSpec(memory_space=SMEM)
    return pl.pallas_call(
        early_kernel,
        out_shape=(
            jax.ShapeDtypeStruct((6, 4 * EDGES, 2 * C), F32),
            jax.ShapeDtypeStruct((3, 2 * EDGES, 2 * C), F32),
            jax.ShapeDtypeStruct((4 * EDGES, LATE * 48), BF),
            jax.ShapeDtypeStruct((2 * EDGES, LATE * 56), BF),
        ),
        in_specs=[smem, smem] + [vm] * 10 + [anywhere] * 2,
        out_specs=(vm,) * 4,
        scratch_shapes=[
            VMEM((32, TILES, 8, C), BF),
            VMEM((2 * EDGES, 14 * C), BF),
            VMEM((4 * EDGES, 12 * C), BF),
            pltpu.SemaphoreType.DMA((38,)),
        ],
        compiler_params=pltpu.CompilerParams(vmem_limit_bytes=20 * 2**20),
        cost_estimate=pl.CostEstimate(flops=4 * 10**9, bytes_accessed=12 * 10**6, transcendentals=0),
        name="mix_early",
    )(core, shard, *blocks, own, got)


def late_kernel(core, up, down, part, part_zero, late, late_zero, own, got, mine, other, fl, fsem):
    copies = [
        pltpu.make_async_copy(src.at[19], fl.at[pl.ds(who * EDGES, EDGES)], fsem.at[who])
        for who, src in enumerate((own, got))
    ]
    for copy in copies:
        copy.start()
    for copy in copies:
        copy.wait()

    def finish(plane, value, filters):
        message = (value * filters).astype(BF)
        mine[plane] = message[:EDGES]
        other[plane] = message[EDGES:]

    def run(pieces, tiles, zero_groups):
        filters = fl[:, :C].astype(F32)
        half = 2 * EDGES
        size = pieces * tiles

        def rows_of(first, count, g):
            return jnp.concatenate(
                (group_rows(up, first, count, g), group_rows(down, first, count, g)), axis=0
            )

        def column(g, carry):
            w = jnp.concatenate((rows_of(0, tiles, g), rows_of(size, tiles, g)), axis=1)
            both = part[g] + jnp.dot(
                late[:, : LATE * tiles * 8], w, preferred_element_type=F32
            )
            finish(g, both[:half, :C] - both[half:, C:], filters)
            finish(pieces + g, both[half:, :C] + both[:half, C:], filters)
            return carry

        lax.fori_loop(0, pieces, column, 0)
        for g in range(0, zero_groups, 2):
            count = min(2, zero_groups - g)
            w = jnp.concatenate([rows_of(2 * size, 7, g + i) for i in range(count)], axis=1)
            total = part_zero[g // 2, :, : count * C] + jnp.dot(
                late_zero[...], w, preferred_element_type=F32
            )
            for i in range(count):
                finish(2 * pieces + g + i, total[:, i * C : (i + 1) * C], filters)

    by_core(core, run)


def mix_late(core, up, down, part, part_zero, late, late_zero, own, got):
    vm = pl.BlockSpec(memory_space=VMEM)
    anywhere = pl.BlockSpec(memory_space=pl.ANY)
    out = jax.ShapeDtypeStruct((15, EDGES, C), BF)
    return pl.pallas_call(
        late_kernel,
        out_shape=(out, out),
        in_specs=[pl.BlockSpec(memory_space=SMEM)] + [vm] * 6 + [anywhere] * 2,
        out_specs=(vm, vm),
        scratch_shapes=[VMEM((2 * EDGES, 2 * C), BF), pltpu.SemaphoreType.DMA((2,))],
        compiler_params=pltpu.CompilerParams(vmem_limit_bytes=8 * 2**20),
        cost_estimate=pl.CostEstimate(flops=10**9, bytes_accessed=8 * 10**6, transcendentals=0),
        name="mix_late",
    )(core, up, down, part, part_zero, late, late_zero, own, got)


def ends_kernel(wig, rotation, target, after, out):
    del after
    hot_r = lax.broadcasted_iota(jnp.int32, (NROT, EDGES), 0) == rotation[...]
    d = jnp.dot(wig[...], hot_r.astype(F32).astype(BF), preferred_element_type=F32)
    ends = lax.broadcasted_iota(jnp.int32, (ATOMS, EDGES), 0) == target[...]
    at = 0
    for degree in range(7):
        for r in ROWS[degree]:
            for j in range(2 * degree + 1):
                entry = d[r * 16 + j : r * 16 + j + 1, :]
                out[at : at + ATOMS, :] = jnp.where(ends, entry, 0.0).astype(BF)
                at += ATOMS


def ends_of(wig, rotation, target, after):
    vm = pl.BlockSpec(memory_space=VMEM)
    return pl.pallas_call(
        ends_kernel,
        out_shape=jax.ShapeDtypeStruct((235 * ATOMS, EDGES), BF),
        in_specs=[vm] * 3 + [pl.BlockSpec(memory_space=pl.ANY)],
        out_specs=vm,
        compiler_params=pltpu.CompilerParams(vmem_limit_bytes=4 * 2**20),
        cost_estimate=pl.CostEstimate(flops=10**8, bytes_accessed=6 * 10**6, transcendentals=0),
        name="ends_of",
    )(wig, rotation, target, after)


def back_kernel(
    place_mine, place_got, task, mine, got, hot, node, struct, head, update, energy, m, first, sem
):
    copies = [pltpu.make_async_copy(node.at[:, pl.ds(0, C)], first, sem.at[30])]
    for i in range(15):
        copies.append(pltpu.make_async_copy(mine.at[i], m.at[place_mine[i]], sem.at[2 * i]))
        copies.append(pltpu.make_async_copy(got.at[i], m.at[place_got[i]], sem.at[2 * i + 1]))
    for copy in copies:
        copy.start()
    for copy in copies:
        copy.wait()
    at = 0
    for degree in range(7):
        span = 2 * degree + 1
        total = None
        for r in ROWS[degree]:
            term = jnp.dot(hot[at : at + span * ATOMS, :], m[r], preferred_element_type=F32)
            total = term if total is None else total + term
            at += span * ATOMS
        for place in range(span):
            value = total[place * ATOMS : (place + 1) * ATOMS]
            j = degree * degree + place
            update[:, j * C : (j + 1) * C] = value.astype(BF)
            if j == 0:
                scalar_part = first[...].astype(F32) + value
    for s in range(4):
        member = jnp.where(struct[...] == s, scalar_part, 0.0) * head[pl.ds(task[s], 1), :]
        energy[s] = jnp.sum(member)


def turn_back(place_mine, place_got, task, mine, got, hot, node, struct, head):
    vm = pl.BlockSpec(memory_space=VMEM)
    anywhere = pl.BlockSpec(memory_space=pl.ANY)
    smem = pl.BlockSpec(memory_space=SMEM)
    return pl.pallas_call(
        back_kernel,
        out_shape=(
            jax.ShapeDtypeStruct((ATOMS, COEF * C), BF),
            jax.ShapeDtypeStruct((4,), F32),
        ),
        in_specs=[smem] * 3 + [anywhere] * 2 + [vm, anywhere, vm, vm],
        out_specs=(vm, smem),
        scratch_shapes=[
            VMEM((30, EDGES, C), BF),
            VMEM((ATOMS, C), BF),
            pltpu.SemaphoreType.DMA((31,)),
        ],
        compiler_params=pltpu.CompilerParams(vmem_limit_bytes=6 * 2**20),
        cost_estimate=pl.CostEstimate(flops=10**9, bytes_accessed=4 * 10**6, transcendentals=0),
        name="turn_back",
    )(place_mine, place_got, task, mine, got, hot, node, struct, head)


def exchange(value, sizes, steps_first, steps_second):
    mol, nz, ny = sizes
    pairs = []
    for device in range(mol * nz * ny):
        m, t = divmod(device, nz * ny)
        z, y = divmod(t, ny)
        dz, dy = steps_first if m % 2 == 0 else steps_second
        to = ((z + dz) % nz) * ny + (y + dy) % ny
        pairs.append((device, m * nz * ny + to))
    return lax.ppermute(value, ("mol", "task"), pairs)


def body(
    node_embed,
    wigner,
    source,
    target,
    rotation,
    edge_filter,
    edge_count,
    w_zero,
    w_one_real,
    w_one_imag,
    w_two_real,
    w_two_imag,
    atom_struct,
    struct_task,
    task_head,
):
    sizes = (8, 8, 4)
    core = lax.axis_index("mol") % 2
    task = lax.axis_index("task")
    z, y = task // 4, task % 4
    first = core == 0

    core_vec = core.reshape(1).astype(jnp.int32)

    def pick(a, b):
        return jnp.where(first, a, b)

    b0 = pack(core_vec, w_zero, w_one_real, w_one_imag, w_two_real, w_two_imag)
    a1 = exchange(b0, sizes, (0, 1), (1, 0))
    a2 = exchange(b0, sizes, (0, -1), (-1, 0))
    a3 = exchange(b0, sizes, (0, 2), (4, 0))
    h0 = jnp.concatenate((b0, a1))
    h1 = jnp.concatenate((a2, a3))

    def forth(value, second=(0, 1)):
        return exchange(value, sizes, (1, 0), second)

    def aft(value, second=(0, -1)):
        return exchange(value, sizes, (-1, 0), second)

    p1p = forth(pick(h0, jnp.concatenate((a1, a3))), (1, 0))
    p1m = aft(h1, (-1, 0))
    s1p = forth(jnp.concatenate((pick(h1, h0), pick(p1p, h1))))
    s1m = aft(jnp.concatenate((h0, pick(p1m, h1))))
    p1 = jnp.concatenate((p1p, p1m))
    s2p, s2m = forth(pick(s1p, p1)), aft(pick(s1m, p1))
    live = (jnp.arange(EDGES, dtype=jnp.int32) < edge_count[0])[:, None]
    filters = jnp.where(live, edge_filter, jnp.zeros_like(edge_filter))
    own, send, entries = features(
        core_vec,
        node_embed,
        wigner.transpose(1, 2, 0),
        source.reshape(EDGES, 1),
        target.reshape(EDGES, 1),
        rotation.reshape(EDGES, 1),
        filters,
    )
    hot = ends_of(entries, rotation.reshape(1, EDGES), target.reshape(1, EDGES), s1m)
    s2p, s2m, hot = lax.optimization_barrier((s2p, s2m, hot))
    s3p, s3m = forth(pick(s2p, s1p)), aft(s2m)

    blocks = (b0, a1, a2, a3, p1p, p1m, s1p, s1m, s2p, s2m)
    offsets_first, offsets_second = block_offsets()
    table = jnp.asarray((offsets_first, offsets_second), jnp.int32)[core]
    shard = ((z + table[:, 0]) % 8) * 4 + (y + table[:, 1]) % 4

    swap = [(i, i ^ 1) for i in range(8)]
    got = lax.ppermute(send, "mol", swap)
    parts = mix_early(core_vec, shard, blocks, own, got)
    held = (4, TILES, 8, C)
    mine, other = mix_late(core_vec, s3p.reshape(held), s3m.reshape(held), *parts, own, got)
    back = lax.ppermute(other, "mol", swap)
    places = jnp.asarray(MADE, jnp.int32)
    update, energy = turn_back(
        places[core],
        places[1 - core],
        struct_task,
        mine,
        back,
        hot,
        node_embed,
        atom_struct.reshape(ATOMS, 1),
        task_head,
    )
    return update, energy


def solution(mesh):
    both = P(("mol", "task"))
    wide = P(("mol", "task"), None)
    rows = P("task", None)
    in_specs = (wide, P(), both, both, both, wide, both, rows, rows, rows, rows, rows, both, both, P())
    return jax.shard_map(
        body, mesh=mesh, in_specs=in_specs, out_specs=(wide, both), check_vma=False
    )
```

```python
import jax
import jax.numpy as jnp
from jax import lax
from jax.experimental import pallas as pl
from jax.experimental.pallas import tpu as pltpu
from jax.sharding import PartitionSpec as P

C = 128
COEF = 49
MROWS = 29
EDGES = 192
ATOMS = 48
NROT = 256
TILES = 86
LATE = 8
VMEM = pltpu.VMEM
SMEM = pltpu.SMEM
BF = jnp.bfloat16
F32 = jnp.float32

ROWS = [[degree] for degree in range(7)]
for degree in range(1, 7):
    ROWS[degree] += [6 + degree, 12 + degree]
for degree in range(2, 7):
    ROWS[degree] += [17 + degree, 22 + degree]

MADE = (
    tuple(range(7, 19)) + (0, 1),
    tuple(range(19, 29)) + (2, 3, 4, 5, 6),
)

H0 = ((0, 0), (0, -1))
H1 = ((0, 1), (0, 2))
U = (
    ((0, 0), (-1, 0)),
    ((1, 0), (4, 0)),
    ((-2, 0), (3, 0)),
    ((2, 0), (-3, 0)),
)


def moved(blocks, z, y):
    return [(a + z, b + y) for a, b in blocks]


def block_offsets():
    first = moved(H0, 0, 0) + moved(H1, 0, 0) + moved(H0, -1, 0) + moved(H1, 1, 0)
    for step in (1, 2, 3):
        first += moved(H1, -step, 0) + moved(H0, -step - 1, 0)
        first += moved(H0, step, 0) + moved(H1, step + 1, 0)
    second = [block for part in U for block in part]
    for part in (0, 2):
        for y in (-1, 1):
            second += moved(U[part], 0, y) + moved(U[part + 1], 0, y)
    for part in (0, 2):
        second += moved(U[part], 0, 2) + moved(U[part + 1], 0, 2)
    return first, second


def feature_kernel(
    core, node, wig, source, target, rotation, filt, own, send, wc_out, node_out, x, xs, xt, wc, fz, fa, sem
):
    wc[...] = jnp.zeros_like(wc)
    for degree in range(7):
        at = degree * degree
        for r in ROWS[degree]:
            wc[r * 16 : r * 16 + 2 * degree + 1, :] = wig[r, at : at + 2 * degree + 1, :].astype(F32)
    entries = wc[...].astype(BF)
    wc_out[...] = entries
    for j in range(COEF):
        x[j * ATOMS : (j + 1) * ATOMS, :] = node[:, j * C : (j + 1) * C]
    width = 13 * ATOMS
    lane = lax.broadcasted_iota(jnp.int32, (1, width), 1)
    atom = lane % ATOMS
    xs[...] = (source[...] == atom).astype(F32).astype(BF)
    xt[...] = (target[...] == atom).astype(F32).astype(BF)
    hot_r = (rotation[...] == lax.broadcasted_iota(jnp.int32, (1, NROT), 1)).astype(F32).astype(BF)
    d_all = lax.dot_general(
        hot_r, entries, (((1,), (1,)), ((), ())), preferred_element_type=F32
    ).astype(BF)
    node_out[...] = node[:, :C]
    slot_one = core[0]
    slot_two = 1 - core[0]
    for slot in range(2):
        fa[slot, :EDGES, 12 * C : 13 * C] = filt[...]
    for degree in range(7):
        wide = (2 * degree + 1) * ATOMS
        at = degree * degree
        which = lax.broadcasted_iota(jnp.int32, (C, wide), 0)
        which = which - lax.broadcasted_iota(jnp.int32, (C, wide), 1) // ATOMS
        coefs = x[at * ATOMS : at * ATOMS + wide, :]
        for r in ROWS[degree]:
            part, offset = divmod(r, 8)
            spread = (which == offset * 16).astype(F32).astype(BF)
            d = d_all[:, part * C : (part + 1) * C]
            d = jnp.dot(d, spread, preferred_element_type=F32).astype(BF)
            one = jnp.dot(d * xs[:, :wide], coefs, preferred_element_type=F32).astype(BF)
            two = jnp.dot(d * xt[:, :wide], coefs, preferred_element_type=F32).astype(BF)
            for at_lane, value in ((0, one), (C, two)):
                if r < 7:
                    fz[:, r * 2 * C + at_lane : r * 2 * C + at_lane + C] = value
                    continue
                slot = slot_one if r < 19 else slot_two
                sign, k = divmod(r - 7, 6) if r < 19 else divmod(r - 19, 5)
                lanes = slice(k * 2 * C + at_lane, k * 2 * C + at_lane + C)
                fa[slot, sign * EDGES : (sign + 1) * EDGES, lanes] = value
    copies = []
    for slot, out in enumerate((own, send)):
        copies += [
            pltpu.make_async_copy(fz, out.at[pl.ds(0, EDGES)], sem.at[2 * slot]),
            pltpu.make_async_copy(
                fa.at[slot], out.at[pl.ds(EDGES, 2 * EDGES)], sem.at[2 * slot + 1]
            ),
        ]
    for copy in copies:
        copy.start()
    for copy in copies:
        copy.wait()


def features(core, node, wig, source, target, rotation, filt):
    vm = pl.BlockSpec(memory_space=VMEM)
    anywhere = pl.BlockSpec(memory_space=pl.ANY)
    return pl.pallas_call(
        feature_kernel,
        out_shape=(
            jax.ShapeDtypeStruct((3 * EDGES, 14 * C), BF),
            jax.ShapeDtypeStruct((3 * EDGES, 14 * C), BF),
            jax.ShapeDtypeStruct((4 * C, NROT), BF),
            jax.ShapeDtypeStruct((ATOMS, C), BF),
        ),
        in_specs=[pl.BlockSpec(memory_space=SMEM)] + [vm] * 6,
        out_specs=(anywhere, anywhere, vm, vm),
        scratch_shapes=[
            VMEM((COEF * ATOMS, C), BF),
            VMEM((EDGES, 13 * ATOMS), BF),
            VMEM((EDGES, 13 * ATOMS), BF),
            VMEM((4 * C, NROT), F32),
            VMEM((EDGES, 14 * C), BF),
            VMEM((2, 2 * EDGES, 14 * C), BF),
            pltpu.SemaphoreType.DMA((4,)),
        ],
        compiler_params=pltpu.CompilerParams(vmem_limit_bytes=8 * 2**20),
        cost_estimate=pl.CostEstimate(flops=6 * 10**9, bytes_accessed=8 * 10**6, transcendentals=0),
        name="features",
    )(core, node, wig, source, target, rotation, filt)


def pack_kernel(core, *refs):
    given, out, held, sem = refs[:5], refs[5], refs[6:11], refs[11]
    zero, one_real, one_imag, two_real, two_imag = held

    def run(parts):
        copies = []
        for i in range(5):
            if any(held[i] is part[0] for part in parts):
                copies.append(pltpu.make_async_copy(given[i], held[i], sem.at[i]))
        for copy in copies:
            copy.start()
        for copy in copies:
            copy.wait()
        at = 0
        for ref, first, groups in parts:
            tiles = ref.shape[0] // 8
            for g in range(first, first + groups):
                out[at : at + tiles] = ref[:, g * C : (g + 1) * C].reshape(tiles, 8, C)
                at += tiles
        if at < TILES:
            out[at:] = jnp.zeros((TILES - at, 8, C), BF)

    @pl.when(core[0] == 0)
    def _():
        run(((one_real, 0, 6), (one_imag, 0, 6), (zero, 0, 2)))

    @pl.when(core[0] == 1)
    def _():
        run(((two_real, 0, 5), (two_imag, 0, 5), (zero, 2, 5)))


def pack(core, zero, one_real, one_imag, two_real, two_imag):
    vm = pl.BlockSpec(memory_space=VMEM)
    return pl.pallas_call(
        pack_kernel,
        out_shape=jax.ShapeDtypeStruct((TILES, 8, C), BF),
        in_specs=[pl.BlockSpec(memory_space=SMEM)] + [pl.BlockSpec(memory_space=pltpu.HBM)] * 5,
        out_specs=vm,
        scratch_shapes=[VMEM(w.shape, BF) for w in (zero, one_real, one_imag, two_real, two_imag)]
        + [pltpu.SemaphoreType.DMA((5,))],
        compiler_params=pltpu.CompilerParams(vmem_limit_bytes=60 * 2**20),
        name="pack",
    )(core, zero, one_real, one_imag, two_real, two_imag)


def by_core(core, run):
    @pl.when(core[0] == 0)
    def _():
        run(6, 6, 2)

    @pl.when(core[0] == 1)
    def _():
        run(5, 5, 5)


def group_rows(held, first, count, g):
    tiles = held[:, pl.ds(first + g * count, count)]
    return tiles.reshape(held.shape[0] * count * 8, C)


def zero_features(own, got):
    return jnp.concatenate((own[:EDGES, :], got[:EDGES, :]), axis=0)


def order_features(own, got, deep):
    return jnp.concatenate((own[EDGES:, :deep], got[EDGES:, :deep]), axis=0)


def early_kernel(core, shard, *refs):
    blocks = refs[:10]
    own, got, part, part_zero, late, late_zero, w_all = refs[10:]

    def chosen(rows, deep):
        lane = lax.broadcasted_iota(jnp.int32, (1, LATE * rows), 1)
        wanted = lane
        for i in range(LATE):
            here = jnp.logical_and(lane >= i * rows, lane < (i + 1) * rows)
            wanted = jnp.where(here, lane + (shard[32 - LATE + i] - i) * rows, wanted)
        return (lax.broadcasted_iota(jnp.int32, (deep, 1), 0) == wanted).astype(F32).astype(BF)

    def run(pieces, tiles, zero_groups):
        deep = pieces * 2 * C
        size = pieces * tiles

        def column(g, carry):
            w = jnp.concatenate(
                (group_rows(w_all, 0, tiles, g), group_rows(w_all, size, tiles, g)), axis=1
            )
            part[g] = jnp.dot(order_features(own, got, deep), w, preferred_element_type=F32)
            return carry

        lax.fori_loop(0, pieces, column, 0)
        for g in range(0, zero_groups, 2):
            count = min(2, zero_groups - g)
            w = jnp.concatenate(
                [group_rows(w_all, 2 * size, 7, g + i) for i in range(count)], axis=1
            )
            part_zero[g // 2, :, : count * C] = jnp.dot(
                zero_features(own, got), w, preferred_element_type=F32
            )
        rows = tiles * 8
        late[:, : LATE * rows] = jnp.dot(
            order_features(own, got, deep), chosen(rows, deep), preferred_element_type=F32
        ).astype(BF)
        late_zero[...] = jnp.dot(
            zero_features(own, got), chosen(56, 14 * C), preferred_element_type=F32
        ).astype(BF)

    def place(block, index):
        def one(i, carry):
            w_all[shard[index + i]] = block[pl.ds(i * TILES, TILES)]
            return carry

        lax.fori_loop(0, block.shape[0] // TILES, one, 0)

    index = 0
    for block in blocks:
        place(block, index)
        index += block.shape[0] // TILES

    def clear(i, carry):
        w_all[shard[32 - LATE + i]] = jnp.zeros((TILES, 8, C), BF)
        return carry

    lax.fori_loop(0, LATE, clear, 0)
    by_core(core, run)


def mix_early(core, shard, blocks, own, got):
    vm = pl.BlockSpec(memory_space=VMEM)
    smem = pl.BlockSpec(memory_space=SMEM)
    return pl.pallas_call(
        early_kernel,
        out_shape=(
            jax.ShapeDtypeStruct((6, 4 * EDGES, 2 * C), F32),
            jax.ShapeDtypeStruct((3, 2 * EDGES, 2 * C), F32),
            jax.ShapeDtypeStruct((4 * EDGES, LATE * 48), BF),
            jax.ShapeDtypeStruct((2 * EDGES, LATE * 56), BF),
        ),
        in_specs=[smem, smem] + [vm] * 12,
        out_specs=(vm,) * 4,
        scratch_shapes=[VMEM((32, TILES, 8, C), BF)],
        compiler_params=pltpu.CompilerParams(vmem_limit_bytes=20 * 2**20),
        cost_estimate=pl.CostEstimate(flops=4 * 10**9, bytes_accessed=12 * 10**6, transcendentals=0),
        name="mix_early",
    )(core, shard, *blocks, own, got)


def late_kernel(core, up, down, part, part_zero, late, late_zero, own, got, mine, other):
    def finish(plane, own_value, got_value, filters):
        mine[plane] = (own_value * filters[0]).astype(BF)
        other[plane] = (got_value * filters[1]).astype(BF)

    def run(pieces, tiles, zero_groups):
        filters = [ref[EDGES : 2 * EDGES, 12 * C : 13 * C].astype(F32) for ref in (own, got)]
        size = pieces * tiles

        def rows_of(first, count, g):
            return jnp.concatenate(
                (group_rows(up, first, count, g), group_rows(down, first, count, g)), axis=0
            )

        def column(g, carry):
            w = jnp.concatenate((rows_of(0, tiles, g), rows_of(size, tiles, g)), axis=1)
            both = part[g] + jnp.dot(
                late[:, : LATE * tiles * 8], w, preferred_element_type=F32
            )
            real = [both[i * EDGES : (i + 1) * EDGES, :C] for i in range(4)]
            imag = [both[i * EDGES : (i + 1) * EDGES, C:] for i in range(4)]
            finish(g, real[0] - imag[1], real[2] - imag[3], filters)
            finish(pieces + g, real[1] + imag[0], real[3] + imag[2], filters)
            return carry

        lax.fori_loop(0, pieces, column, 0)
        for g in range(0, zero_groups, 2):
            count = min(2, zero_groups - g)
            w = jnp.concatenate([rows_of(2 * size, 7, g + i) for i in range(count)], axis=1)
            total = part_zero[g // 2, :, : count * C] + jnp.dot(
                late_zero[...], w, preferred_element_type=F32
            )
            for i in range(count):
                value = total[:, i * C : (i + 1) * C]
                finish(2 * pieces + g + i, value[:EDGES], value[EDGES:], filters)

    by_core(core, run)


def mix_late(core, up, down, part, part_zero, late, late_zero, own, got):
    vm = pl.BlockSpec(memory_space=VMEM)
    out = jax.ShapeDtypeStruct((15, EDGES, C), BF)
    return pl.pallas_call(
        late_kernel,
        out_shape=(out, out),
        in_specs=[pl.BlockSpec(memory_space=SMEM)] + [vm] * 8,
        out_specs=(vm, vm),
        compiler_params=pltpu.CompilerParams(vmem_limit_bytes=8 * 2**20),
        cost_estimate=pl.CostEstimate(flops=10**9, bytes_accessed=8 * 10**6, transcendentals=0),
        name="mix_late",
    )(core, up, down, part, part_zero, late, late_zero, own, got)


def ends_kernel(wig, rotation, target, after, out):
    del after
    hot_r = lax.broadcasted_iota(jnp.int32, (NROT, EDGES), 0) == rotation[...]
    d = jnp.dot(wig[...], hot_r.astype(F32).astype(BF), preferred_element_type=F32)
    ends = lax.broadcasted_iota(jnp.int32, (ATOMS, EDGES), 0) == target[...]
    at = 0
    for degree in range(7):
        for r in ROWS[degree]:
            for j in range(2 * degree + 1):
                entry = d[r * 16 + j : r * 16 + j + 1, :]
                out[at : at + ATOMS, :] = jnp.where(ends, entry, 0.0).astype(BF)
                at += ATOMS


def ends_of(wig, rotation, target, after):
    vm = pl.BlockSpec(memory_space=VMEM)
    return pl.pallas_call(
        ends_kernel,
        out_shape=jax.ShapeDtypeStruct((235 * ATOMS, EDGES), BF),
        in_specs=[vm] * 3 + [pl.BlockSpec(memory_space=pl.ANY)],
        out_specs=vm,
        compiler_params=pltpu.CompilerParams(vmem_limit_bytes=4 * 2**20),
        cost_estimate=pl.CostEstimate(flops=10**8, bytes_accessed=6 * 10**6, transcendentals=0),
        name="ends_of",
    )(wig, rotation, target, after)


def back_kernel(core, task, mine, got, hot, node, struct, head, update, energy):
    is_first = core[0] == 0

    def message(r):
        if r in MADE[0]:
            i = MADE[0].index(r)
            return jnp.where(is_first, mine[i], got[i])
        i = MADE[1].index(r)
        return jnp.where(is_first, got[i], mine[i])

    at = 0
    for degree in range(7):
        span = 2 * degree + 1
        total = None
        for r in ROWS[degree]:
            term = jnp.dot(hot[at : at + span * ATOMS, :], message(r), preferred_element_type=F32)
            total = term if total is None else total + term
            at += span * ATOMS
        for place in range(span):
            value = total[place * ATOMS : (place + 1) * ATOMS]
            j = degree * degree + place
            update[:, j * C : (j + 1) * C] = value.astype(BF)
            if j == 0:
                scalar_part = node[...].astype(F32) + value
    for s in range(4):
        member = jnp.where(struct[...] == s, scalar_part, 0.0) * head[pl.ds(task[s], 1), :]
        energy[s] = jnp.sum(member)


def turn_back(core, task, mine, got, hot, node, struct, head):
    vm = pl.BlockSpec(memory_space=VMEM)
    smem = pl.BlockSpec(memory_space=SMEM)
    return pl.pallas_call(
        back_kernel,
        out_shape=(
            jax.ShapeDtypeStruct((ATOMS, COEF * C), BF),
            jax.ShapeDtypeStruct((4,), F32),
        ),
        in_specs=[smem] * 2 + [vm] * 6,
        out_specs=(vm, smem),
        compiler_params=pltpu.CompilerParams(vmem_limit_bytes=6 * 2**20),
        cost_estimate=pl.CostEstimate(flops=10**9, bytes_accessed=4 * 10**6, transcendentals=0),
        name="turn_back",
    )(core, task, mine, got, hot, node, struct, head)


def exchange(value, sizes, steps_first, steps_second):
    mol, nz, ny = sizes
    pairs = []
    for device in range(mol * nz * ny):
        m, t = divmod(device, nz * ny)
        z, y = divmod(t, ny)
        dz, dy = steps_first if m % 2 == 0 else steps_second
        to = ((z + dz) % nz) * ny + (y + dy) % ny
        pairs.append((device, m * nz * ny + to))
    return lax.ppermute(value, ("mol", "task"), pairs)


def body(
    node_embed,
    wigner,
    source,
    target,
    rotation,
    edge_filter,
    edge_count,
    w_zero,
    w_one_real,
    w_one_imag,
    w_two_real,
    w_two_imag,
    atom_struct,
    struct_task,
    task_head,
):
    sizes = (8, 8, 4)
    core = lax.axis_index("mol") % 2
    task = lax.axis_index("task")
    z, y = task // 4, task % 4
    first = core == 0

    core_vec = core.reshape(1).astype(jnp.int32)

    def pick(a, b):
        return jnp.where(first, a, b)

    b0 = pack(core_vec, w_zero, w_one_real, w_one_imag, w_two_real, w_two_imag)
    a1 = exchange(b0, sizes, (0, 1), (1, 0))
    a2 = exchange(b0, sizes, (0, -1), (-1, 0))
    a3 = exchange(b0, sizes, (0, 2), (4, 0))
    h0 = jnp.concatenate((b0, a1))
    h1 = jnp.concatenate((a2, a3))

    def forth(value, second=(0, 1)):
        return exchange(value, sizes, (1, 0), second)

    def aft(value, second=(0, -1)):
        return exchange(value, sizes, (-1, 0), second)

    p1p = forth(pick(h0, jnp.concatenate((a1, a3))), (1, 0))
    p1m = aft(h1, (-1, 0))
    s1p = forth(jnp.concatenate((pick(h1, h0), pick(p1p, h1))))
    s1m = aft(jnp.concatenate((h0, pick(p1m, h1))))
    p1 = jnp.concatenate((p1p, p1m))
    s2p, s2m = forth(pick(s1p, p1)), aft(pick(s1m, p1))
    live = (jnp.arange(EDGES, dtype=jnp.int32) < edge_count[0])[:, None]
    filters = jnp.where(live, edge_filter, jnp.zeros_like(edge_filter))
    own, send, entries, node_first = features(
        core_vec,
        node_embed,
        wigner.transpose(1, 2, 0),
        source.reshape(EDGES, 1),
        target.reshape(EDGES, 1),
        rotation.reshape(EDGES, 1),
        filters,
    )
    s3p, s3m = forth(pick(s2p, s1p)), aft(s2m)

    blocks = (b0, a1, a2, a3, p1p, p1m, s1p, s1m, s2p, s2m)
    offsets_first, offsets_second = block_offsets()
    table = jnp.asarray((offsets_first, offsets_second), jnp.int32)[core]
    shard = ((z + table[:, 0]) % 8) * 4 + (y + table[:, 1]) % 4

    swap = [(i, i ^ 1) for i in range(8)]
    got = lax.ppermute(send, "mol", swap)
    parts = mix_early(core_vec, shard, blocks, own, got)
    held = (4, TILES, 8, C)
    mine, other = mix_late(core_vec, s3p.reshape(held), s3m.reshape(held), *parts, own, got)
    back = lax.ppermute(other, "mol", swap)
    hot = ends_of(entries, rotation.reshape(1, EDGES), target.reshape(1, EDGES), mine)
    update, energy = turn_back(
        core_vec,
        struct_task,
        mine,
        back,
        hot,
        node_first,
        atom_struct.reshape(ATOMS, 1),
        task_head,
    )
    return update, energy


def solution(mesh):
    both = P(("mol", "task"))
    wide = P(("mol", "task"), None)
    rows = P("task", None)
    in_specs = (wide, P(), both, both, both, wide, both, rows, rows, rows, rows, rows, both, both, P())
    return jax.shard_map(
        body, mesh=mesh, in_specs=in_specs, out_specs=(wide, both), check_vma=False
    )
```

```python
import jax
import jax.numpy as jnp
from jax import lax
from jax.experimental import pallas as pl
from jax.experimental.pallas import tpu as pltpu
from jax.sharding import PartitionSpec as P

C = 128
COEF = 49
MROWS = 29
EDGES = 192
ATOMS = 48
NROT = 256
TILES = 86
LATE = 8
VMEM = pltpu.VMEM
SMEM = pltpu.SMEM
BF = jnp.bfloat16
F32 = jnp.float32

ROWS = [[degree] for degree in range(7)]
for degree in range(1, 7):
    ROWS[degree] += [6 + degree, 12 + degree]
for degree in range(2, 7):
    ROWS[degree] += [17 + degree, 22 + degree]

MADE = (
    tuple(range(7, 19)) + (0, 1),
    tuple(range(19, 29)) + (2, 3, 4, 5, 6),
)

H0 = ((0, 0), (0, -1))
H1 = ((0, 1), (0, 2))
U = (
    ((0, 0), (-1, 0)),
    ((1, 0), (4, 0)),
    ((-2, 0), (3, 0)),
    ((2, 0), (-3, 0)),
)


def moved(blocks, z, y):
    return [(a + z, b + y) for a, b in blocks]


def block_offsets():
    first = moved(H0, 0, 0) + moved(H1, 0, 0) + moved(H0, -1, 0) + moved(H1, 1, 0)
    for step in (1, 2, 3):
        first += moved(H1, -step, 0) + moved(H0, -step - 1, 0)
        first += moved(H0, step, 0) + moved(H1, step + 1, 0)
    second = [block for part in U for block in part]
    for step in (1, 2, 3):
        second += moved(U[0], 0, -step) + moved(U[1], 0, -step)
        second += moved(U[2], 0, step) + moved(U[3], 0, step)
    return first, second


def feature_kernel(
    core, node, wig, source, target, rotation, filt, own, send, wc_out, node_out, x, xs, xt, wc, fz, fa, sem
):
    wc[...] = jnp.zeros_like(wc)
    for degree in range(7):
        at = degree * degree
        for r in ROWS[degree]:
            wc[r * 16 : r * 16 + 2 * degree + 1, :] = wig[r, at : at + 2 * degree + 1, :].astype(F32)
    entries = wc[...].astype(BF)
    wc_out[...] = entries
    for j in range(COEF):
        x[j * ATOMS : (j + 1) * ATOMS, :] = node[:, j * C : (j + 1) * C]
    width = 13 * ATOMS
    lane = lax.broadcasted_iota(jnp.int32, (1, width), 1)
    atom = lane % ATOMS
    xs[...] = (source[...] == atom).astype(F32).astype(BF)
    xt[...] = (target[...] == atom).astype(F32).astype(BF)
    hot_r = (rotation[...] == lax.broadcasted_iota(jnp.int32, (1, NROT), 1)).astype(F32).astype(BF)
    d_all = lax.dot_general(
        hot_r, entries, (((1,), (1,)), ((), ())), preferred_element_type=F32
    ).astype(BF)
    node_out[...] = node[:, :C]
    slot_one = core[0]
    slot_two = 1 - core[0]
    for slot in range(2):
        fa[slot, :EDGES, 12 * C : 13 * C] = filt[...]
    for degree in range(7):
        wide = (2 * degree + 1) * ATOMS
        at = degree * degree
        which = lax.broadcasted_iota(jnp.int32, (C, wide), 0)
        which = which - lax.broadcasted_iota(jnp.int32, (C, wide), 1) // ATOMS
        coefs = x[at * ATOMS : at * ATOMS + wide, :]
        for r in ROWS[degree]:
            part, offset = divmod(r, 8)
            spread = (which == offset * 16).astype(F32).astype(BF)
            d = d_all[:, part * C : (part + 1) * C]
            d = jnp.dot(d, spread, preferred_element_type=F32).astype(BF)
            one = jnp.dot(d * xs[:, :wide], coefs, preferred_element_type=F32).astype(BF)
            two = jnp.dot(d * xt[:, :wide], coefs, preferred_element_type=F32).astype(BF)
            for at_lane, value in ((0, one), (C, two)):
                if r < 7:
                    fz[:, r * 2 * C + at_lane : r * 2 * C + at_lane + C] = value
                    continue
                slot = slot_one if r < 19 else slot_two
                sign, k = divmod(r - 7, 6) if r < 19 else divmod(r - 19, 5)
                lanes = slice(k * 2 * C + at_lane, k * 2 * C + at_lane + C)
                fa[slot, sign * EDGES : (sign + 1) * EDGES, lanes] = value
    copies = []
    for slot, out in enumerate((own, send)):
        copies += [
            pltpu.make_async_copy(fz, out.at[pl.ds(0, EDGES)], sem.at[2 * slot]),
            pltpu.make_async_copy(
                fa.at[slot], out.at[pl.ds(EDGES, 2 * EDGES)], sem.at[2 * slot + 1]
            ),
        ]
    for copy in copies:
        copy.start()
    for copy in copies:
        copy.wait()


def features(core, node, wig, source, target, rotation, filt):
    vm = pl.BlockSpec(memory_space=VMEM)
    anywhere = pl.BlockSpec(memory_space=pl.ANY)
    return pl.pallas_call(
        feature_kernel,
        out_shape=(
            jax.ShapeDtypeStruct((3 * EDGES, 14 * C), BF),
            jax.ShapeDtypeStruct((3 * EDGES, 14 * C), BF),
            jax.ShapeDtypeStruct((4 * C, NROT), BF),
            jax.ShapeDtypeStruct((ATOMS, C), BF),
        ),
        in_specs=[pl.BlockSpec(memory_space=SMEM)] + [vm] * 6,
        out_specs=(anywhere, anywhere, vm, vm),
        scratch_shapes=[
            VMEM((COEF * ATOMS, C), BF),
            VMEM((EDGES, 13 * ATOMS), BF),
            VMEM((EDGES, 13 * ATOMS), BF),
            VMEM((4 * C, NROT), F32),
            VMEM((EDGES, 14 * C), BF),
            VMEM((2, 2 * EDGES, 14 * C), BF),
            pltpu.SemaphoreType.DMA((4,)),
        ],
        compiler_params=pltpu.CompilerParams(vmem_limit_bytes=8 * 2**20),
        cost_estimate=pl.CostEstimate(flops=6 * 10**9, bytes_accessed=8 * 10**6, transcendentals=0),
        name="features",
    )(core, node, wig, source, target, rotation, filt)


def pack_kernel(core, *refs):
    given, out, held, sem = refs[:5], refs[5], refs[6:11], refs[11]
    zero, one_real, one_imag, two_real, two_imag = held

    def run(parts):
        copies = []
        for i in range(5):
            if any(held[i] is part[0] for part in parts):
                copies.append(pltpu.make_async_copy(given[i], held[i], sem.at[i]))
        for copy in copies:
            copy.start()
        for copy in copies:
            copy.wait()
        at = 0
        for ref, first, groups in parts:
            tiles = ref.shape[0] // 8
            for g in range(first, first + groups):
                out[at : at + tiles] = ref[:, g * C : (g + 1) * C].reshape(tiles, 8, C)
                at += tiles
        if at < TILES:
            out[at:] = jnp.zeros((TILES - at, 8, C), BF)

    @pl.when(core[0] == 0)
    def _():
        run(((one_real, 0, 6), (one_imag, 0, 6), (zero, 0, 2)))

    @pl.when(core[0] == 1)
    def _():
        run(((two_real, 0, 5), (two_imag, 0, 5), (zero, 2, 5)))


def pack(core, zero, one_real, one_imag, two_real, two_imag):
    vm = pl.BlockSpec(memory_space=VMEM)
    return pl.pallas_call(
        pack_kernel,
        out_shape=jax.ShapeDtypeStruct((TILES, 8, C), BF),
        in_specs=[pl.BlockSpec(memory_space=SMEM)] + [pl.BlockSpec(memory_space=pltpu.HBM)] * 5,
        out_specs=vm,
        scratch_shapes=[VMEM(w.shape, BF) for w in (zero, one_real, one_imag, two_real, two_imag)]
        + [pltpu.SemaphoreType.DMA((5,))],
        compiler_params=pltpu.CompilerParams(vmem_limit_bytes=60 * 2**20),
        name="pack",
    )(core, zero, one_real, one_imag, two_real, two_imag)


def by_core(core, run):
    @pl.when(core[0] == 0)
    def _():
        run(6, 6, 2)

    @pl.when(core[0] == 1)
    def _():
        run(5, 5, 5)


def group_rows(held, first, count, g):
    tiles = held[:, pl.ds(first + g * count, count)]
    return tiles.reshape(held.shape[0] * count * 8, C)


def zero_features(own, got):
    return jnp.concatenate((own[:EDGES, :], got[:EDGES, :]), axis=0)


def order_features(own, got, deep):
    return jnp.concatenate((own[EDGES:, :deep], got[EDGES:, :deep]), axis=0)


def early_kernel(core, shard, *refs):
    blocks = refs[:10]
    own, got, part, part_zero, late, late_zero, w_all = refs[10:]

    def chosen(rows, deep):
        lane = lax.broadcasted_iota(jnp.int32, (1, LATE * rows), 1)
        wanted = lane
        for i in range(LATE):
            here = jnp.logical_and(lane >= i * rows, lane < (i + 1) * rows)
            wanted = jnp.where(here, lane + (shard[32 - LATE + i] - i) * rows, wanted)
        return (lax.broadcasted_iota(jnp.int32, (deep, 1), 0) == wanted).astype(F32).astype(BF)

    def run(pieces, tiles, zero_groups):
        deep = pieces * 2 * C
        size = pieces * tiles

        def column(g, carry):
            w = jnp.concatenate(
                (group_rows(w_all, 0, tiles, g), group_rows(w_all, size, tiles, g)), axis=1
            )
            part[g] = jnp.dot(order_features(own, got, deep), w, preferred_element_type=F32)
            return carry

        lax.fori_loop(0, pieces, column, 0)
        for g in range(0, zero_groups, 2):
            count = min(2, zero_groups - g)
            w = jnp.concatenate(
                [group_rows(w_all, 2 * size, 7, g + i) for i in range(count)], axis=1
            )
            part_zero[g // 2, :, : count * C] = jnp.dot(
                zero_features(own, got), w, preferred_element_type=F32
            )
        rows = tiles * 8
        late[:, : LATE * rows] = jnp.dot(
            order_features(own, got, deep), chosen(rows, deep), preferred_element_type=F32
        ).astype(BF)
        late_zero[...] = jnp.dot(
            zero_features(own, got), chosen(56, 14 * C), preferred_element_type=F32
        ).astype(BF)

    def place(block, index):
        def one(i, carry):
            w_all[shard[index + i]] = block[pl.ds(i * TILES, TILES)]
            return carry

        lax.fori_loop(0, block.shape[0] // TILES, one, 0)

    index = 0
    for block in blocks:
        place(block, index)
        index += block.shape[0] // TILES

    def clear(i, carry):
        w_all[shard[32 - LATE + i]] = jnp.zeros((TILES, 8, C), BF)
        return carry

    lax.fori_loop(0, LATE, clear, 0)
    by_core(core, run)


def mix_early(core, shard, blocks, own, got):
    vm = pl.BlockSpec(memory_space=VMEM)
    smem = pl.BlockSpec(memory_space=SMEM)
    return pl.pallas_call(
        early_kernel,
        out_shape=(
            jax.ShapeDtypeStruct((6, 4 * EDGES, 2 * C), F32),
            jax.ShapeDtypeStruct((3, 2 * EDGES, 2 * C), F32),
            jax.ShapeDtypeStruct((4 * EDGES, LATE * 48), BF),
            jax.ShapeDtypeStruct((2 * EDGES, LATE * 56), BF),
        ),
        in_specs=[smem, smem] + [vm] * 12,
        out_specs=(vm,) * 4,
        scratch_shapes=[VMEM((32, TILES, 8, C), BF)],
        compiler_params=pltpu.CompilerParams(vmem_limit_bytes=20 * 2**20),
        cost_estimate=pl.CostEstimate(flops=4 * 10**9, bytes_accessed=12 * 10**6, transcendentals=0),
        name="mix_early",
    )(core, shard, *blocks, own, got)


def late_kernel(core, up, down, part, part_zero, late, late_zero, own, got, mine, other):
    def finish(plane, own_value, got_value, filters):
        mine[plane] = (own_value * filters[0]).astype(BF)
        other[plane] = (got_value * filters[1]).astype(BF)

    def run(pieces, tiles, zero_groups):
        filters = [ref[EDGES : 2 * EDGES, 12 * C : 13 * C].astype(F32) for ref in (own, got)]
        size = pieces * tiles

        def rows_of(first, count, g):
            return jnp.concatenate(
                (group_rows(up, first, count, g), group_rows(down, first, count, g)), axis=0
            )

        def column(g, carry):
            w = jnp.concatenate((rows_of(0, tiles, g), rows_of(size, tiles, g)), axis=1)
            both = part[g] + jnp.dot(
                late[:, : LATE * tiles * 8], w, preferred_element_type=F32
            )
            real = [both[i * EDGES : (i + 1) * EDGES, :C] for i in range(4)]
            imag = [both[i * EDGES : (i + 1) * EDGES, C:] for i in range(4)]
            finish(g, real[0] - imag[1], real[2] - imag[3], filters)
            finish(pieces + g, real[1] + imag[0], real[3] + imag[2], filters)
            return carry

        lax.fori_loop(0, pieces, column, 0, unroll=True)
        for g in range(0, zero_groups, 2):
            count = min(2, zero_groups - g)
            w = jnp.concatenate([rows_of(2 * size, 7, g + i) for i in range(count)], axis=1)
            total = part_zero[g // 2, :, : count * C] + jnp.dot(
                late_zero[...], w, preferred_element_type=F32
            )
            for i in range(count):
                value = total[:, i * C : (i + 1) * C]
                finish(2 * pieces + g + i, value[:EDGES], value[EDGES:], filters)

    by_core(core, run)


def mix_late(core, up, down, part, part_zero, late, late_zero, own, got):
    vm = pl.BlockSpec(memory_space=VMEM)
    out = jax.ShapeDtypeStruct((15, EDGES, C), BF)
    return pl.pallas_call(
        late_kernel,
        out_shape=(out, out),
        in_specs=[pl.BlockSpec(memory_space=SMEM)] + [vm] * 8,
        out_specs=(vm, vm),
        compiler_params=pltpu.CompilerParams(vmem_limit_bytes=8 * 2**20),
        cost_estimate=pl.CostEstimate(flops=10**9, bytes_accessed=8 * 10**6, transcendentals=0),
        name="mix_late",
    )(core, up, down, part, part_zero, late, late_zero, own, got)


def ends_kernel(wig, rotation, target, after, out):
    del after
    hot_r = lax.broadcasted_iota(jnp.int32, (NROT, EDGES), 0) == rotation[...]
    d = jnp.dot(wig[...], hot_r.astype(F32).astype(BF), preferred_element_type=F32)
    ends = lax.broadcasted_iota(jnp.int32, (ATOMS, EDGES), 0) == target[...]
    at = 0
    for degree in range(7):
        for r in ROWS[degree]:
            for j in range(2 * degree + 1):
                entry = d[r * 16 + j : r * 16 + j + 1, :]
                out[at : at + ATOMS, :] = jnp.where(ends, entry, 0.0).astype(BF)
                at += ATOMS


def ends_of(wig, rotation, target, after):
    vm = pl.BlockSpec(memory_space=VMEM)
    return pl.pallas_call(
        ends_kernel,
        out_shape=jax.ShapeDtypeStruct((235 * ATOMS, EDGES), BF),
        in_specs=[vm] * 3 + [pl.BlockSpec(memory_space=pl.ANY)],
        out_specs=vm,
        compiler_params=pltpu.CompilerParams(vmem_limit_bytes=4 * 2**20),
        cost_estimate=pl.CostEstimate(flops=10**8, bytes_accessed=6 * 10**6, transcendentals=0),
        name="ends_of",
    )(wig, rotation, target, after)


def back_kernel(core, task, mine, got, hot, node, struct, head, update, energy):
    is_first = core[0] == 0

    def message(r):
        if r in MADE[0]:
            i = MADE[0].index(r)
            return jnp.where(is_first, mine[i], got[i])
        i = MADE[1].index(r)
        return jnp.where(is_first, got[i], mine[i])

    at = 0
    for degree in range(7):
        span = 2 * degree + 1
        total = None
        for r in ROWS[degree]:
            term = jnp.dot(hot[at : at + span * ATOMS, :], message(r), preferred_element_type=F32)
            total = term if total is None else total + term
            at += span * ATOMS
        for place in range(span):
            value = total[place * ATOMS : (place + 1) * ATOMS]
            j = degree * degree + place
            update[:, j * C : (j + 1) * C] = value.astype(BF)
            if j == 0:
                scalar_part = node[...].astype(F32) + value
    for s in range(4):
        member = jnp.where(struct[...] == s, scalar_part, 0.0) * head[pl.ds(task[s], 1), :]
        energy[s] = jnp.sum(member)


def turn_back(core, task, mine, got, hot, node, struct, head):
    vm = pl.BlockSpec(memory_space=VMEM)
    smem = pl.BlockSpec(memory_space=SMEM)
    return pl.pallas_call(
        back_kernel,
        out_shape=(
            jax.ShapeDtypeStruct((ATOMS, COEF * C), BF),
            jax.ShapeDtypeStruct((4,), F32),
        ),
        in_specs=[smem] * 2 + [vm] * 6,
        out_specs=(vm, smem),
        compiler_params=pltpu.CompilerParams(vmem_limit_bytes=6 * 2**20),
        cost_estimate=pl.CostEstimate(flops=10**9, bytes_accessed=4 * 10**6, transcendentals=0),
        name="turn_back",
    )(core, task, mine, got, hot, node, struct, head)


def exchange(value, sizes, steps_first, steps_second):
    mol, nz, ny = sizes
    pairs = []
    for device in range(mol * nz * ny):
        m, t = divmod(device, nz * ny)
        z, y = divmod(t, ny)
        dz, dy = steps_first if m % 2 == 0 else steps_second
        to = ((z + dz) % nz) * ny + (y + dy) % ny
        pairs.append((device, m * nz * ny + to))
    return lax.ppermute(value, ("mol", "task"), pairs)


def body(
    node_embed,
    wigner,
    source,
    target,
    rotation,
    edge_filter,
    edge_count,
    w_zero,
    w_one_real,
    w_one_imag,
    w_two_real,
    w_two_imag,
    atom_struct,
    struct_task,
    task_head,
):
    sizes = (8, 8, 4)
    core = lax.axis_index("mol") % 2
    task = lax.axis_index("task")
    z, y = task // 4, task % 4
    first = core == 0

    core_vec = core.reshape(1).astype(jnp.int32)

    def pick(a, b):
        return jnp.where(first, a, b)

    b0 = pack(core_vec, w_zero, w_one_real, w_one_imag, w_two_real, w_two_imag)
    a1 = exchange(b0, sizes, (0, 1), (1, 0))
    a2 = exchange(b0, sizes, (0, -1), (-1, 0))
    a3 = exchange(b0, sizes, (0, 2), (4, 0))
    h0 = jnp.concatenate((b0, a1))
    h1 = jnp.concatenate((a2, a3))

    def forth(value, second=(0, 1)):
        return exchange(value, sizes, (1, 0), second)

    def aft(value, second=(0, -1)):
        return exchange(value, sizes, (-1, 0), second)

    p1p = forth(pick(h0, jnp.concatenate((a1, a3))), (1, 0))
    p1m = aft(h1, (-1, 0))
    def both(a, b):
        return jnp.concatenate((a, b))

    x1p = both(pick(h1, h0), pick(p1p, h1))
    x1m = both(pick(h0, p1p), p1m)
    s1p, s1m = forth(x1p), aft(x1m)

    live = (jnp.arange(EDGES, dtype=jnp.int32) < edge_count[0])[:, None]
    filters = jnp.where(live, edge_filter, jnp.zeros_like(edge_filter))
    own, send, entries, node_first = features(
        core_vec,
        node_embed,
        wigner.transpose(1, 2, 0),
        source.reshape(EDGES, 1),
        target.reshape(EDGES, 1),
        rotation.reshape(EDGES, 1),
        filters,
    )

    s1p, s1m, node_first = lax.optimization_barrier((s1p, s1m, node_first))
    s2p, s2m = lax.optimization_barrier((forth(s1p), aft(s1m)))
    s3p, s3m = forth(s2p), aft(s2m)

    blocks = (b0, a1, a2, a3, p1p, p1m, s1p, s1m, s2p, s2m)
    offsets_first, offsets_second = block_offsets()
    table = jnp.asarray((offsets_first, offsets_second), jnp.int32)[core]
    shard = ((z + table[:, 0]) % 8) * 4 + (y + table[:, 1]) % 4

    swap = [(i, i ^ 1) for i in range(8)]
    got = lax.ppermute(send, "mol", swap)
    parts = mix_early(core_vec, shard, blocks, own, got)
    held = (4, TILES, 8, C)
    mine, other = mix_late(core_vec, s3p.reshape(held), s3m.reshape(held), *parts, own, got)
    back = lax.ppermute(other, "mol", swap)
    hot = ends_of(entries, rotation.reshape(1, EDGES), target.reshape(1, EDGES), mine)
    update, energy = turn_back(
        core_vec,
        struct_task,
        mine,
        back,
        hot,
        node_first,
        atom_struct.reshape(ATOMS, 1),
        task_head,
    )
    return update, energy


def solution(mesh):
    both = P(("mol", "task"))
    wide = P(("mol", "task"), None)
    rows = P("task", None)
    in_specs = (wide, P(), both, both, both, wide, both, rows, rows, rows, rows, rows, both, both, P())
    return jax.shard_map(
        body, mesh=mesh, in_specs=in_specs, out_specs=(wide, both), check_vma=False
    )
```

```python
import jax
import jax.numpy as jnp
from jax import lax
from jax.experimental import pallas as pl
from jax.experimental.pallas import tpu as pltpu
from jax.sharding import PartitionSpec as P

C = 128
COEF = 49
MROWS = 29
EDGES = 192
ATOMS = 48
NROT = 256
TILES = 86
LATE = 8
VMEM = pltpu.VMEM
SMEM = pltpu.SMEM
BF = jnp.bfloat16
F32 = jnp.float32

ROWS = [[degree] for degree in range(7)]
for degree in range(1, 7):
    ROWS[degree] += [6 + degree, 12 + degree]
for degree in range(2, 7):
    ROWS[degree] += [17 + degree, 22 + degree]

MADE = (
    tuple(range(7, 19)) + (0, 1),
    tuple(range(19, 29)) + (2, 3, 4, 5, 6),
)

H0 = ((0, 0), (0, -1))
H1 = ((0, 1), (0, 2))
U = (
    ((0, 0), (-1, 0)),
    ((1, 0), (4, 0)),
    ((-2, 0), (3, 0)),
    ((2, 0), (-3, 0)),
)


def moved(blocks, z, y):
    return [(a + z, b + y) for a, b in blocks]


def block_offsets():
    first = moved(H0, 0, 0) + moved(H1, 0, 0) + moved(H0, -1, 0) + moved(H1, 1, 0)
    for step in (1, 2, 3):
        first += moved(H1, -step, 0) + moved(H0, -step - 1, 0)
        first += moved(H0, step, 0) + moved(H1, step + 1, 0)
    second = [block for part in U for block in part]
    for step in (1, 2, 3):
        second += moved(U[0], 0, -step) + moved(U[1], 0, -step)
        second += moved(U[2], 0, step) + moved(U[3], 0, step)
    return first, second


def feature_kernel(
    core, node, wig, source, target, rotation, filt, own, send, wc_out, node_out, x, xs, xt, wc, fz, fa, sem
):
    wc[...] = jnp.zeros_like(wc)
    for degree in range(7):
        at = degree * degree
        for r in ROWS[degree]:
            wc[r * 16 : r * 16 + 2 * degree + 1, :] = wig[r, at : at + 2 * degree + 1, :].astype(F32)
    entries = wc[...].astype(BF)
    wc_out[...] = entries
    for j in range(COEF):
        x[j * ATOMS : (j + 1) * ATOMS, :] = node[:, j * C : (j + 1) * C]
    width = 13 * ATOMS
    lane = lax.broadcasted_iota(jnp.int32, (1, width), 1)
    atom = lane % ATOMS
    xs[...] = (source[...] == atom).astype(F32).astype(BF)
    xt[...] = (target[...] == atom).astype(F32).astype(BF)
    hot_r = (rotation[...] == lax.broadcasted_iota(jnp.int32, (1, NROT), 1)).astype(F32).astype(BF)
    d_all = lax.dot_general(
        hot_r, entries, (((1,), (1,)), ((), ())), preferred_element_type=F32
    ).astype(BF)
    node_out[...] = node[:, :C]
    slot_one = core[0]
    slot_two = 1 - core[0]
    for slot in range(2):
        fa[slot, :EDGES, 12 * C : 13 * C] = filt[...]
    for degree in range(7):
        wide = (2 * degree + 1) * ATOMS
        at = degree * degree
        which = lax.broadcasted_iota(jnp.int32, (C, wide), 0)
        which = which - lax.broadcasted_iota(jnp.int32, (C, wide), 1) // ATOMS
        coefs = x[at * ATOMS : at * ATOMS + wide, :]
        for r in ROWS[degree]:
            part, offset = divmod(r, 8)
            spread = (which == offset * 16).astype(F32).astype(BF)
            d = d_all[:, part * C : (part + 1) * C]
            d = jnp.dot(d, spread, preferred_element_type=F32).astype(BF)
            one = jnp.dot(d * xs[:, :wide], coefs, preferred_element_type=F32).astype(BF)
            two = jnp.dot(d * xt[:, :wide], coefs, preferred_element_type=F32).astype(BF)
            for at_lane, value in ((0, one), (C, two)):
                if r < 7:
                    fz[:, r * 2 * C + at_lane : r * 2 * C + at_lane + C] = value
                    continue
                slot = slot_one if r < 19 else slot_two
                sign, k = divmod(r - 7, 6) if r < 19 else divmod(r - 19, 5)
                lanes = slice(k * 2 * C + at_lane, k * 2 * C + at_lane + C)
                fa[slot, sign * EDGES : (sign + 1) * EDGES, lanes] = value
    copies = []
    for slot, out in enumerate((own, send)):
        copies += [
            pltpu.make_async_copy(fz, out.at[pl.ds(0, EDGES)], sem.at[2 * slot]),
            pltpu.make_async_copy(
                fa.at[slot], out.at[pl.ds(EDGES, 2 * EDGES)], sem.at[2 * slot + 1]
            ),
        ]
    for copy in copies:
        copy.start()
    for copy in copies:
        copy.wait()


def features(core, node, wig, source, target, rotation, filt):
    vm = pl.BlockSpec(memory_space=VMEM)
    anywhere = pl.BlockSpec(memory_space=pl.ANY)
    return pl.pallas_call(
        feature_kernel,
        out_shape=(
            jax.ShapeDtypeStruct((3 * EDGES, 14 * C), BF),
            jax.ShapeDtypeStruct((3 * EDGES, 14 * C), BF),
            jax.ShapeDtypeStruct((4 * C, NROT), BF),
            jax.ShapeDtypeStruct((ATOMS, C), BF),
        ),
        in_specs=[pl.BlockSpec(memory_space=SMEM)] + [vm] * 6,
        out_specs=(anywhere, anywhere, vm, vm),
        scratch_shapes=[
            VMEM((COEF * ATOMS, C), BF),
            VMEM((EDGES, 13 * ATOMS), BF),
            VMEM((EDGES, 13 * ATOMS), BF),
            VMEM((4 * C, NROT), F32),
            VMEM((EDGES, 14 * C), BF),
            VMEM((2, 2 * EDGES, 14 * C), BF),
            pltpu.SemaphoreType.DMA((4,)),
        ],
        compiler_params=pltpu.CompilerParams(vmem_limit_bytes=8 * 2**20),
        cost_estimate=pl.CostEstimate(flops=6 * 10**9, bytes_accessed=8 * 10**6, transcendentals=0),
        name="features",
    )(core, node, wig, source, target, rotation, filt)


def pack_kernel(core, *refs):
    given, out, held, sem = refs[:5], refs[5], refs[6:11], refs[11]
    zero, one_real, one_imag, two_real, two_imag = held

    def run(parts):
        copies = []
        for i in range(5):
            if any(held[i] is part[0] for part in parts):
                copies.append(pltpu.make_async_copy(given[i], held[i], sem.at[i]))
        for copy in copies:
            copy.start()
        for copy in copies:
            copy.wait()
        at = 0
        for ref, first, groups in parts:
            tiles = ref.shape[0] // 8
            for g in range(first, first + groups):
                out[at : at + tiles] = ref[:, g * C : (g + 1) * C].reshape(tiles, 8, C)
                at += tiles
        if at < TILES:
            out[at:] = jnp.zeros((TILES - at, 8, C), BF)

    @pl.when(core[0] == 0)
    def _():
        run(((one_real, 0, 6), (one_imag, 0, 6), (zero, 0, 2)))

    @pl.when(core[0] == 1)
    def _():
        run(((two_real, 0, 5), (two_imag, 0, 5), (zero, 2, 5)))


def pack(core, zero, one_real, one_imag, two_real, two_imag):
    vm = pl.BlockSpec(memory_space=VMEM)
    return pl.pallas_call(
        pack_kernel,
        out_shape=jax.ShapeDtypeStruct((TILES, 8, C), BF),
        in_specs=[pl.BlockSpec(memory_space=SMEM)] + [pl.BlockSpec(memory_space=pltpu.HBM)] * 5,
        out_specs=vm,
        scratch_shapes=[VMEM(w.shape, BF) for w in (zero, one_real, one_imag, two_real, two_imag)]
        + [pltpu.SemaphoreType.DMA((5,))],
        compiler_params=pltpu.CompilerParams(vmem_limit_bytes=60 * 2**20),
        name="pack",
    )(core, zero, one_real, one_imag, two_real, two_imag)


def by_core(core, run):
    @pl.when(core[0] == 0)
    def _():
        run(6, 6, 2)

    @pl.when(core[0] == 1)
    def _():
        run(5, 5, 5)


def group_rows(held, first, count, g):
    tiles = held[:, pl.ds(first + g * count, count)]
    return tiles.reshape(held.shape[0] * count * 8, C)


def zero_features(own, got):
    return jnp.concatenate((own[:EDGES, :], got[:EDGES, :]), axis=0)


def order_features(own, got, deep):
    return jnp.concatenate((own[EDGES:, :deep], got[EDGES:, :deep]), axis=0)


def choose_kernel(core, shard, own, got, *refs):
    late, late_zero = refs[6:]

    def chosen(rows, deep):
        lane = lax.broadcasted_iota(jnp.int32, (1, LATE * rows), 1)
        wanted = lane
        for i in range(LATE):
            here = jnp.logical_and(lane >= i * rows, lane < (i + 1) * rows)
            wanted = jnp.where(here, lane + (shard[32 - LATE + i] - i) * rows, wanted)
        return (lax.broadcasted_iota(jnp.int32, (deep, 1), 0) == wanted).astype(F32).astype(BF)

    def run(pieces, tiles, zero_groups):
        del zero_groups
        deep = pieces * 2 * C
        rows = tiles * 8
        late[:, : LATE * rows] = jnp.dot(
            order_features(own, got, deep), chosen(rows, deep), preferred_element_type=F32
        ).astype(BF)
        late_zero[...] = jnp.dot(
            zero_features(own, got), chosen(56, 14 * C), preferred_element_type=F32
        ).astype(BF)

    by_core(core, run)


def choose(core, shard, own, got, blocks):
    vm = pl.BlockSpec(memory_space=VMEM)
    smem = pl.BlockSpec(memory_space=SMEM)
    return pl.pallas_call(
        choose_kernel,
        out_shape=(
            jax.ShapeDtypeStruct((4 * EDGES, LATE * 48), BF),
            jax.ShapeDtypeStruct((2 * EDGES, LATE * 56), BF),
        ),
        in_specs=[smem, smem] + [vm] * 8,
        out_specs=(vm, vm),
        compiler_params=pltpu.CompilerParams(vmem_limit_bytes=8 * 2**20),
        cost_estimate=pl.CostEstimate(flops=10**9, bytes_accessed=4 * 10**6, transcendentals=0),
        name="choose",
    )(core, shard, own, got, *blocks)


def early_kernel(core, shard, *refs):
    blocks = refs[:10]
    own, got, part, part_zero, w_all = refs[10:]

    def run(pieces, tiles, zero_groups):
        deep = pieces * 2 * C
        size = pieces * tiles

        def column(g, carry):
            w = jnp.concatenate(
                (group_rows(w_all, 0, tiles, g), group_rows(w_all, size, tiles, g)), axis=1
            )
            part[g] = jnp.dot(order_features(own, got, deep), w, preferred_element_type=F32)
            return carry

        lax.fori_loop(0, pieces, column, 0)
        for g in range(0, zero_groups, 2):
            count = min(2, zero_groups - g)
            w = jnp.concatenate(
                [group_rows(w_all, 2 * size, 7, g + i) for i in range(count)], axis=1
            )
            part_zero[g // 2, :, : count * C] = jnp.dot(
                zero_features(own, got), w, preferred_element_type=F32
            )

    def place(block, index):
        def one(i, carry):
            w_all[shard[index + i]] = block[pl.ds(i * TILES, TILES)]
            return carry

        lax.fori_loop(0, block.shape[0] // TILES, one, 0)

    index = 0
    for block in blocks:
        place(block, index)
        index += block.shape[0] // TILES

    def clear(i, carry):
        w_all[shard[32 - LATE + i]] = jnp.zeros((TILES, 8, C), BF)
        return carry

    lax.fori_loop(0, LATE, clear, 0)
    by_core(core, run)


def mix_early(core, shard, blocks, own, got):
    vm = pl.BlockSpec(memory_space=VMEM)
    smem = pl.BlockSpec(memory_space=SMEM)
    return pl.pallas_call(
        early_kernel,
        out_shape=(
            jax.ShapeDtypeStruct((6, 4 * EDGES, 2 * C), F32),
            jax.ShapeDtypeStruct((3, 2 * EDGES, 2 * C), F32),
        ),
        in_specs=[smem, smem] + [vm] * 12,
        out_specs=(vm, vm),
        scratch_shapes=[VMEM((32, TILES, 8, C), BF)],
        compiler_params=pltpu.CompilerParams(vmem_limit_bytes=16 * 2**20),
        cost_estimate=pl.CostEstimate(flops=4 * 10**9, bytes_accessed=12 * 10**6, transcendentals=0),
        name="mix_early",
    )(core, shard, *blocks, own, got)


def late_kernel(core, up, down, part, part_zero, late, late_zero, own, got, mine, other):
    def finish(plane, own_value, got_value, filters):
        mine[plane] = (own_value * filters[0]).astype(BF)
        other[plane] = (got_value * filters[1]).astype(BF)

    def run(pieces, tiles, zero_groups):
        filters = [ref[EDGES : 2 * EDGES, 12 * C : 13 * C].astype(F32) for ref in (own, got)]
        size = pieces * tiles

        def rows_of(first, count, g):
            return jnp.concatenate(
                (group_rows(up, first, count, g), group_rows(down, first, count, g)), axis=0
            )

        def column(g, carry):
            w = jnp.concatenate((rows_of(0, tiles, g), rows_of(size, tiles, g)), axis=1)
            both = part[g] + jnp.dot(
                late[:, : LATE * tiles * 8], w, preferred_element_type=F32
            )
            real = [both[i * EDGES : (i + 1) * EDGES, :C] for i in range(4)]
            imag = [both[i * EDGES : (i + 1) * EDGES, C:] for i in range(4)]
            finish(g, real[0] - imag[1], real[2] - imag[3], filters)
            finish(pieces + g, real[1] + imag[0], real[3] + imag[2], filters)
            return carry

        lax.fori_loop(0, pieces, column, 0, unroll=True)
        for g in range(0, zero_groups, 2):
            count = min(2, zero_groups - g)
            w = jnp.concatenate([rows_of(2 * size, 7, g + i) for i in range(count)], axis=1)
            total = part_zero[g // 2, :, : count * C] + jnp.dot(
                late_zero[...], w, preferred_element_type=F32
            )
            for i in range(count):
                value = total[:, i * C : (i + 1) * C]
                finish(2 * pieces + g + i, value[:EDGES], value[EDGES:], filters)

    by_core(core, run)


def mix_late(core, up, down, part, part_zero, late, late_zero, own, got):
    vm = pl.BlockSpec(memory_space=VMEM)
    out = jax.ShapeDtypeStruct((15, EDGES, C), BF)
    return pl.pallas_call(
        late_kernel,
        out_shape=(out, out),
        in_specs=[pl.BlockSpec(memory_space=SMEM)] + [vm] * 8,
        out_specs=(vm, vm),
        compiler_params=pltpu.CompilerParams(vmem_limit_bytes=8 * 2**20),
        cost_estimate=pl.CostEstimate(flops=10**9, bytes_accessed=8 * 10**6, transcendentals=0),
        name="mix_late",
    )(core, up, down, part, part_zero, late, late_zero, own, got)


def ends_kernel(wig, rotation, target, after, out):
    del after
    hot_r = lax.broadcasted_iota(jnp.int32, (NROT, EDGES), 0) == rotation[...]
    d = jnp.dot(wig[...], hot_r.astype(F32).astype(BF), preferred_element_type=F32)
    ends = lax.broadcasted_iota(jnp.int32, (ATOMS, EDGES), 0) == target[...]
    at = 0
    for degree in range(7):
        for r in ROWS[degree]:
            for j in range(2 * degree + 1):
                entry = d[r * 16 + j : r * 16 + j + 1, :]
                out[at : at + ATOMS, :] = jnp.where(ends, entry, 0.0).astype(BF)
                at += ATOMS


def ends_of(wig, rotation, target, after):
    vm = pl.BlockSpec(memory_space=VMEM)
    return pl.pallas_call(
        ends_kernel,
        out_shape=jax.ShapeDtypeStruct((235 * ATOMS, EDGES), BF),
        in_specs=[vm] * 3 + [pl.BlockSpec(memory_space=pl.ANY)],
        out_specs=vm,
        compiler_params=pltpu.CompilerParams(vmem_limit_bytes=4 * 2**20),
        cost_estimate=pl.CostEstimate(flops=10**8, bytes_accessed=6 * 10**6, transcendentals=0),
        name="ends_of",
    )(wig, rotation, target, after)


def back_kernel(core, task, mine, got, hot, node, struct, head, update, energy):
    is_first = core[0] == 0

    def message(r):
        if r in MADE[0]:
            i = MADE[0].index(r)
            return jnp.where(is_first, mine[i], got[i])
        i = MADE[1].index(r)
        return jnp.where(is_first, got[i], mine[i])

    at = 0
    for degree in range(7):
        span = 2 * degree + 1
        total = None
        for r in ROWS[degree]:
            term = jnp.dot(hot[at : at + span * ATOMS, :], message(r), preferred_element_type=F32)
            total = term if total is None else total + term
            at += span * ATOMS
        for place in range(span):
            value = total[place * ATOMS : (place + 1) * ATOMS]
            j = degree * degree + place
            update[:, j * C : (j + 1) * C] = value.astype(BF)
            if j == 0:
                scalar_part = node[...].astype(F32) + value
    for s in range(4):
        member = jnp.where(struct[...] == s, scalar_part, 0.0) * head[pl.ds(task[s], 1), :]
        energy[s] = jnp.sum(member)


def turn_back(core, task, mine, got, hot, node, struct, head):
    vm = pl.BlockSpec(memory_space=VMEM)
    smem = pl.BlockSpec(memory_space=SMEM)
    return pl.pallas_call(
        back_kernel,
        out_shape=(
            jax.ShapeDtypeStruct((ATOMS, COEF * C), BF),
            jax.ShapeDtypeStruct((4,), F32),
        ),
        in_specs=[smem] * 2 + [vm] * 6,
        out_specs=(vm, smem),
        compiler_params=pltpu.CompilerParams(vmem_limit_bytes=6 * 2**20),
        cost_estimate=pl.CostEstimate(flops=10**9, bytes_accessed=4 * 10**6, transcendentals=0),
        name="turn_back",
    )(core, task, mine, got, hot, node, struct, head)


def exchange(value, sizes, steps_first, steps_second):
    mol, nz, ny = sizes
    pairs = []
    for device in range(mol * nz * ny):
        m, t = divmod(device, nz * ny)
        z, y = divmod(t, ny)
        dz, dy = steps_first if m % 2 == 0 else steps_second
        to = ((z + dz) % nz) * ny + (y + dy) % ny
        pairs.append((device, m * nz * ny + to))
    return lax.ppermute(value, ("mol", "task"), pairs)


def body(
    node_embed,
    wigner,
    source,
    target,
    rotation,
    edge_filter,
    edge_count,
    w_zero,
    w_one_real,
    w_one_imag,
    w_two_real,
    w_two_imag,
    atom_struct,
    struct_task,
    task_head,
):
    sizes = (8, 8, 4)
    core = lax.axis_index("mol") % 2
    task = lax.axis_index("task")
    z, y = task // 4, task % 4
    first = core == 0

    core_vec = core.reshape(1).astype(jnp.int32)

    def pick(a, b):
        return jnp.where(first, a, b)

    b0 = pack(core_vec, w_zero, w_one_real, w_one_imag, w_two_real, w_two_imag)
    a1 = exchange(b0, sizes, (0, 1), (1, 0))
    a2 = exchange(b0, sizes, (0, -1), (-1, 0))
    a3 = exchange(b0, sizes, (0, 2), (4, 0))
    h0 = jnp.concatenate((b0, a1))
    h1 = jnp.concatenate((a2, a3))

    def forth(value, second=(0, 1)):
        return exchange(value, sizes, (1, 0), second)

    def aft(value, second=(0, -1)):
        return exchange(value, sizes, (-1, 0), second)

    p1p = forth(pick(h0, jnp.concatenate((a1, a3))), (1, 0))
    p1m = aft(h1, (-1, 0))
    def both(a, b):
        return jnp.concatenate((a, b))

    x1p = both(pick(h1, h0), pick(p1p, h1))
    x1m = both(pick(h0, p1p), p1m)
    s1p, s1m = forth(x1p), aft(x1m)

    live = (jnp.arange(EDGES, dtype=jnp.int32) < edge_count[0])[:, None]
    filters = jnp.where(live, edge_filter, jnp.zeros_like(edge_filter))
    own, send, entries, node_first = features(
        core_vec,
        node_embed,
        wigner.transpose(1, 2, 0),
        source.reshape(EDGES, 1),
        target.reshape(EDGES, 1),
        rotation.reshape(EDGES, 1),
        filters,
    )

    s1p, s1m, send = lax.optimization_barrier((s1p, s1m, send))
    offsets_first, offsets_second = block_offsets()
    table = jnp.asarray((offsets_first, offsets_second), jnp.int32)[core]
    shard = ((z + table[:, 0]) % 8) * 4 + (y + table[:, 1]) % 4

    swap = [(i, i ^ 1) for i in range(8)]
    got = lax.ppermute(send, "mol", swap)
    late, late_zero = choose(core_vec, shard, own, got, (b0, a1, a2, a3, p1p, p1m))
    s2p, s2m, late = lax.optimization_barrier((forth(s1p), aft(s1m), late))
    s3p, s3m = forth(s2p), aft(s2m)
    blocks = (b0, a1, a2, a3, p1p, p1m, s1p, s1m, s2p, s2m)
    parts = mix_early(core_vec, shard, blocks, own, got)
    held = (4, TILES, 8, C)
    mine, other = mix_late(core_vec, s3p.reshape(held), s3m.reshape(held), *parts, late, late_zero, own, got)
    back = lax.ppermute(other, "mol", swap)
    hot = ends_of(entries, rotation.reshape(1, EDGES), target.reshape(1, EDGES), mine)
    update, energy = turn_back(
        core_vec,
        struct_task,
        mine,
        back,
        hot,
        node_first,
        atom_struct.reshape(ATOMS, 1),
        task_head,
    )
    return update, energy


def solution(mesh):
    both = P(("mol", "task"))
    wide = P(("mol", "task"), None)
    rows = P("task", None)
    in_specs = (wide, P(), both, both, both, wide, both, rows, rows, rows, rows, rows, both, both, P())
    return jax.shard_map(
        body, mesh=mesh, in_specs=in_specs, out_specs=(wide, both), check_vma=False
    )
```

```python
import jax
import jax.numpy as jnp
from jax import lax
from jax.experimental import pallas as pl
from jax.experimental.pallas import tpu as pltpu
from jax.sharding import PartitionSpec as P

C = 128
COEF = 49
MROWS = 29
EDGES = 192
ATOMS = 48
NROT = 256
TILES = 86
LATE = 8
VMEM = pltpu.VMEM
SMEM = pltpu.SMEM
BF = jnp.bfloat16
F32 = jnp.float32

ROWS = [[degree] for degree in range(7)]
for degree in range(1, 7):
    ROWS[degree] += [6 + degree, 12 + degree]
for degree in range(2, 7):
    ROWS[degree] += [17 + degree, 22 + degree]

MADE = (
    tuple(range(7, 19)) + (0, 1),
    tuple(range(19, 29)) + (2, 3, 4, 5, 6),
)

H0 = ((0, 0), (0, -1))
H1 = ((0, 1), (0, 2))
U = (
    ((0, 0), (-1, 0)),
    ((1, 0), (4, 0)),
    ((-2, 0), (3, 0)),
    ((2, 0), (-3, 0)),
)


def moved(blocks, z, y):
    return [(a + z, b + y) for a, b in blocks]


def block_offsets():
    first = moved(H0, 0, 0) + moved(H1, 0, 0) + moved(H0, -1, 0) + moved(H1, 1, 0)
    for step in (1, 2, 3):
        first += moved(H1, -step, 0) + moved(H0, -step - 1, 0)
        first += moved(H0, step, 0) + moved(H1, step + 1, 0)
    second = [block for part in U for block in part]
    for step in (1, 2, 3):
        second += moved(U[0], 0, -step) + moved(U[1], 0, -step)
        second += moved(U[2], 0, step) + moved(U[3], 0, step)
    return first, second


def feature_kernel(
    core, node, wig, source, target, rotation, filt, own, send, wc_out, node_out, x, xs, xt, wc, fz, fa, sem
):
    wc[...] = jnp.zeros_like(wc)
    for degree in range(7):
        at = degree * degree
        for r in ROWS[degree]:
            wc[r * 16 : r * 16 + 2 * degree + 1, :] = wig[r, at : at + 2 * degree + 1, :].astype(F32)
    entries = wc[...].astype(BF)
    wc_out[...] = entries
    for j in range(COEF):
        x[j * ATOMS : (j + 1) * ATOMS, :] = node[:, j * C : (j + 1) * C]
    width = 13 * ATOMS
    lane = lax.broadcasted_iota(jnp.int32, (1, width), 1)
    atom = lane % ATOMS
    xs[...] = (source[...] == atom).astype(F32).astype(BF)
    xt[...] = (target[...] == atom).astype(F32).astype(BF)
    hot_r = (rotation[...] == lax.broadcasted_iota(jnp.int32, (1, NROT), 1)).astype(F32).astype(BF)
    d_all = lax.dot_general(
        hot_r, entries, (((1,), (1,)), ((), ())), preferred_element_type=F32
    ).astype(BF)
    node_out[...] = node[:, :C]
    slot_one = core[0]
    slot_two = 1 - core[0]
    for slot in range(2):
        fa[slot, :EDGES, 12 * C : 13 * C] = filt[...]
    for degree in range(7):
        wide = (2 * degree + 1) * ATOMS
        at = degree * degree
        which = lax.broadcasted_iota(jnp.int32, (C, wide), 0)
        which = which - lax.broadcasted_iota(jnp.int32, (C, wide), 1) // ATOMS
        coefs = x[at * ATOMS : at * ATOMS + wide, :]
        for r in ROWS[degree]:
            part, offset = divmod(r, 8)
            spread = (which == offset * 16).astype(F32).astype(BF)
            d = d_all[:, part * C : (part + 1) * C]
            d = jnp.dot(d, spread, preferred_element_type=F32).astype(BF)
            one = jnp.dot(d * xs[:, :wide], coefs, preferred_element_type=F32).astype(BF)
            two = jnp.dot(d * xt[:, :wide], coefs, preferred_element_type=F32).astype(BF)
            for at_lane, value in ((0, one), (C, two)):
                if r < 7:
                    fz[:, r * 2 * C + at_lane : r * 2 * C + at_lane + C] = value
                    continue
                slot = slot_one if r < 19 else slot_two
                sign, k = divmod(r - 7, 6) if r < 19 else divmod(r - 19, 5)
                lanes = slice(k * 2 * C + at_lane, k * 2 * C + at_lane + C)
                fa[slot, sign * EDGES : (sign + 1) * EDGES, lanes] = value
    copies = []
    for slot, out in enumerate((own, send)):
        copies += [
            pltpu.make_async_copy(fz, out.at[pl.ds(0, EDGES)], sem.at[2 * slot]),
            pltpu.make_async_copy(
                fa.at[slot], out.at[pl.ds(EDGES, 2 * EDGES)], sem.at[2 * slot + 1]
            ),
        ]
    for copy in copies:
        copy.start()
    for copy in copies:
        copy.wait()


def features(core, node, wig, source, target, rotation, filt):
    vm = pl.BlockSpec(memory_space=VMEM)
    anywhere = pl.BlockSpec(memory_space=pl.ANY)
    return pl.pallas_call(
        feature_kernel,
        out_shape=(
            jax.ShapeDtypeStruct((3 * EDGES, 14 * C), BF),
            jax.ShapeDtypeStruct((3 * EDGES, 14 * C), BF),
            jax.ShapeDtypeStruct((4 * C, NROT), BF),
            jax.ShapeDtypeStruct((ATOMS, C), BF),
        ),
        in_specs=[pl.BlockSpec(memory_space=SMEM)] + [vm] * 6,
        out_specs=(anywhere, anywhere, vm, vm),
        scratch_shapes=[
            VMEM((COEF * ATOMS, C), BF),
            VMEM((EDGES, 13 * ATOMS), BF),
            VMEM((EDGES, 13 * ATOMS), BF),
            VMEM((4 * C, NROT), F32),
            VMEM((EDGES, 14 * C), BF),
            VMEM((2, 2 * EDGES, 14 * C), BF),
            pltpu.SemaphoreType.DMA((4,)),
        ],
        compiler_params=pltpu.CompilerParams(vmem_limit_bytes=8 * 2**20),
        cost_estimate=pl.CostEstimate(flops=6 * 10**9, bytes_accessed=8 * 10**6, transcendentals=0),
        name="features",
    )(core, node, wig, source, target, rotation, filt)


def pack_kernel(core, *refs):
    given, out, held, sem = refs[:5], refs[5], refs[6:11], refs[11]
    zero, one_real, one_imag, two_real, two_imag = held

    def run(parts):
        copies = []
        for i in range(5):
            if any(held[i] is part[0] for part in parts):
                copies.append(pltpu.make_async_copy(given[i], held[i], sem.at[i]))
        for copy in copies:
            copy.start()
        for copy in copies:
            copy.wait()
        at = 0
        for ref, first, groups in parts:
            tiles = ref.shape[0] // 8
            for g in range(first, first + groups):
                out[at : at + tiles] = ref[:, g * C : (g + 1) * C].reshape(tiles, 8, C)
                at += tiles
        if at < TILES:
            out[at:] = jnp.zeros((TILES - at, 8, C), BF)

    @pl.when(core[0] == 0)
    def _():
        run(((one_real, 0, 6), (one_imag, 0, 6), (zero, 0, 2)))

    @pl.when(core[0] == 1)
    def _():
        run(((two_real, 0, 5), (two_imag, 0, 5), (zero, 2, 5)))


def pack(core, zero, one_real, one_imag, two_real, two_imag):
    vm = pl.BlockSpec(memory_space=VMEM)
    return pl.pallas_call(
        pack_kernel,
        out_shape=jax.ShapeDtypeStruct((TILES, 8, C), BF),
        in_specs=[pl.BlockSpec(memory_space=SMEM)] + [pl.BlockSpec(memory_space=pltpu.HBM)] * 5,
        out_specs=vm,
        scratch_shapes=[VMEM(w.shape, BF) for w in (zero, one_real, one_imag, two_real, two_imag)]
        + [pltpu.SemaphoreType.DMA((5,))],
        compiler_params=pltpu.CompilerParams(vmem_limit_bytes=60 * 2**20),
        name="pack",
    )(core, zero, one_real, one_imag, two_real, two_imag)


def by_core(core, run):
    @pl.when(core[0] == 0)
    def _():
        run(6, 6, 2)

    @pl.when(core[0] == 1)
    def _():
        run(5, 5, 5)


def group_rows(held, first, count, g):
    tiles = held[:, pl.ds(first + g * count, count)]
    return tiles.reshape(held.shape[0] * count * 8, C)


def zero_features(own, got):
    return jnp.concatenate((own[:EDGES, :], got[:EDGES, :]), axis=0)


def order_features(own, got, deep):
    return jnp.concatenate((own[EDGES:, :deep], got[EDGES:, :deep]), axis=0)


def choose_kernel(core, shard, own, got, *refs):
    late, late_zero = refs[6:]

    def chosen(rows, deep):
        lane = lax.broadcasted_iota(jnp.int32, (1, LATE * rows), 1)
        wanted = lane
        for i in range(LATE):
            here = jnp.logical_and(lane >= i * rows, lane < (i + 1) * rows)
            wanted = jnp.where(here, lane + (shard[32 - LATE + i] - i) * rows, wanted)
        return (lax.broadcasted_iota(jnp.int32, (deep, 1), 0) == wanted).astype(F32).astype(BF)

    def run(pieces, tiles, zero_groups):
        del zero_groups
        deep = pieces * 2 * C
        rows = tiles * 8
        late[:, : LATE * rows] = jnp.dot(
            order_features(own, got, deep), chosen(rows, deep), preferred_element_type=F32
        ).astype(BF)
        late_zero[...] = jnp.dot(
            zero_features(own, got), chosen(56, 14 * C), preferred_element_type=F32
        ).astype(BF)

    by_core(core, run)


def choose(core, shard, own, got, blocks):
    vm = pl.BlockSpec(memory_space=VMEM)
    smem = pl.BlockSpec(memory_space=SMEM)
    return pl.pallas_call(
        choose_kernel,
        out_shape=(
            jax.ShapeDtypeStruct((4 * EDGES, LATE * 48), BF),
            jax.ShapeDtypeStruct((2 * EDGES, LATE * 56), BF),
        ),
        in_specs=[smem, smem] + [vm] * 8,
        out_specs=(vm, vm),
        compiler_params=pltpu.CompilerParams(vmem_limit_bytes=8 * 2**20),
        cost_estimate=pl.CostEstimate(flops=10**9, bytes_accessed=4 * 10**6, transcendentals=0),
        name="choose",
    )(core, shard, own, got, *blocks)


def early_kernel(core, shard, *refs):
    blocks = refs[:10]
    own, got, part, part_zero, w_all = refs[10:]

    def run(pieces, tiles, zero_groups):
        deep = pieces * 2 * C
        size = pieces * tiles

        def column(g, carry):
            w = jnp.concatenate(
                (group_rows(w_all, 0, tiles, g), group_rows(w_all, size, tiles, g)), axis=1
            )
            part[g] = jnp.dot(order_features(own, got, deep), w, preferred_element_type=F32)
            return carry

        lax.fori_loop(0, pieces, column, 0)
        for g in range(0, zero_groups, 2):
            count = min(2, zero_groups - g)
            w = jnp.concatenate(
                [group_rows(w_all, 2 * size, 7, g + i) for i in range(count)], axis=1
            )
            part_zero[g // 2, :, : count * C] = jnp.dot(
                zero_features(own, got), w, preferred_element_type=F32
            )

    def place(block, index):
        def one(i, carry):
            w_all[shard[index + i]] = block[pl.ds(i * TILES, TILES)]
            return carry

        lax.fori_loop(0, block.shape[0] // TILES, one, 0)

    index = 0
    for block in blocks:
        place(block, index)
        index += block.shape[0] // TILES

    def clear(i, carry):
        w_all[shard[32 - LATE + i]] = jnp.zeros((TILES, 8, C), BF)
        return carry

    lax.fori_loop(0, LATE, clear, 0)
    by_core(core, run)


def mix_early(core, shard, blocks, own, got):
    vm = pl.BlockSpec(memory_space=VMEM)
    smem = pl.BlockSpec(memory_space=SMEM)
    return pl.pallas_call(
        early_kernel,
        out_shape=(
            jax.ShapeDtypeStruct((6, 4 * EDGES, 2 * C), F32),
            jax.ShapeDtypeStruct((3, 2 * EDGES, 2 * C), F32),
        ),
        in_specs=[smem, smem] + [vm] * 12,
        out_specs=(vm, vm),
        scratch_shapes=[VMEM((32, TILES, 8, C), BF)],
        compiler_params=pltpu.CompilerParams(vmem_limit_bytes=16 * 2**20),
        cost_estimate=pl.CostEstimate(flops=4 * 10**9, bytes_accessed=12 * 10**6, transcendentals=0),
        name="mix_early",
    )(core, shard, *blocks, own, got)


def late_kernel(core, up, down, part, part_zero, late, late_zero, own, got, mine, other):
    def finish(plane, own_value, got_value, filters):
        mine[plane] = (own_value * filters[0]).astype(BF)
        other[plane] = (got_value * filters[1]).astype(BF)

    def run(pieces, tiles, zero_groups):
        filters = [ref[EDGES : 2 * EDGES, 12 * C : 13 * C].astype(F32) for ref in (own, got)]
        size = pieces * tiles

        def rows_of(first, count, g):
            return jnp.concatenate(
                (group_rows(up, first, count, g), group_rows(down, first, count, g)), axis=0
            )

        def column(g, carry):
            w = jnp.concatenate((rows_of(0, tiles, g), rows_of(size, tiles, g)), axis=1)
            both = part[g] + jnp.dot(
                late[:, : LATE * tiles * 8], w, preferred_element_type=F32
            )
            real = [both[i * EDGES : (i + 1) * EDGES, :C] for i in range(4)]
            imag = [both[i * EDGES : (i + 1) * EDGES, C:] for i in range(4)]
            finish(g, real[0] - imag[1], real[2] - imag[3], filters)
            finish(pieces + g, real[1] + imag[0], real[3] + imag[2], filters)
            return carry

        lax.fori_loop(0, pieces, column, 0, unroll=True)
        for g in range(0, zero_groups, 2):
            count = min(2, zero_groups - g)
            w = jnp.concatenate([rows_of(2 * size, 7, g + i) for i in range(count)], axis=1)
            total = part_zero[g // 2, :, : count * C] + jnp.dot(
                late_zero[...], w, preferred_element_type=F32
            )
            for i in range(count):
                value = total[:, i * C : (i + 1) * C]
                finish(2 * pieces + g + i, value[:EDGES], value[EDGES:], filters)

    by_core(core, run)


def mix_late(core, up, down, part, part_zero, late, late_zero, own, got):
    vm = pl.BlockSpec(memory_space=VMEM)
    out = jax.ShapeDtypeStruct((15, EDGES, C), BF)
    return pl.pallas_call(
        late_kernel,
        out_shape=(out, out),
        in_specs=[pl.BlockSpec(memory_space=SMEM)] + [vm] * 8,
        out_specs=(vm, vm),
        compiler_params=pltpu.CompilerParams(vmem_limit_bytes=8 * 2**20),
        cost_estimate=pl.CostEstimate(flops=10**9, bytes_accessed=8 * 10**6, transcendentals=0),
        name="mix_late",
    )(core, up, down, part, part_zero, late, late_zero, own, got)


def ends_kernel(wig, rotation, target, after, out):
    del after
    hot_r = lax.broadcasted_iota(jnp.int32, (NROT, EDGES), 0) == rotation[...]
    d = jnp.dot(wig[...], hot_r.astype(F32).astype(BF), preferred_element_type=F32)
    ends = lax.broadcasted_iota(jnp.int32, (ATOMS, EDGES), 0) == target[...]
    at = 0
    for degree in range(7):
        for r in ROWS[degree]:
            for j in range(2 * degree + 1):
                entry = d[r * 16 + j : r * 16 + j + 1, :]
                out[at : at + ATOMS, :] = jnp.where(ends, entry, 0.0).astype(BF)
                at += ATOMS


def ends_of(wig, rotation, target, after):
    vm = pl.BlockSpec(memory_space=VMEM)
    return pl.pallas_call(
        ends_kernel,
        out_shape=jax.ShapeDtypeStruct((235 * ATOMS, EDGES), BF),
        in_specs=[vm] * 3 + [pl.BlockSpec(memory_space=pl.ANY)],
        out_specs=vm,
        compiler_params=pltpu.CompilerParams(vmem_limit_bytes=4 * 2**20),
        cost_estimate=pl.CostEstimate(flops=10**8, bytes_accessed=6 * 10**6, transcendentals=0),
        name="ends_of",
    )(wig, rotation, target, after)


def back_kernel(core, task, mine, got, hot, node, struct, head, update, energy):
    is_first = core[0] == 0

    def message(r):
        if r in MADE[0]:
            i = MADE[0].index(r)
            return jnp.where(is_first, mine[i], got[i])
        i = MADE[1].index(r)
        return jnp.where(is_first, got[i], mine[i])

    at = 0
    for degree in range(7):
        span = 2 * degree + 1
        total = None
        for r in ROWS[degree]:
            term = jnp.dot(hot[at : at + span * ATOMS, :], message(r), preferred_element_type=F32)
            total = term if total is None else total + term
            at += span * ATOMS
        for place in range(span):
            value = total[place * ATOMS : (place + 1) * ATOMS]
            j = degree * degree + place
            update[:, j * C : (j + 1) * C] = value.astype(BF)
            if j == 0:
                scalar_part = node[...].astype(F32) + value
    for s in range(4):
        member = jnp.where(struct[...] == s, scalar_part, 0.0) * head[pl.ds(task[s], 1), :]
        energy[s] = jnp.sum(member)


def turn_back(core, task, mine, got, hot, node, struct, head):
    vm = pl.BlockSpec(memory_space=VMEM)
    smem = pl.BlockSpec(memory_space=SMEM)
    return pl.pallas_call(
        back_kernel,
        out_shape=(
            jax.ShapeDtypeStruct((ATOMS, COEF * C), BF),
            jax.ShapeDtypeStruct((4,), F32),
        ),
        in_specs=[smem] * 2 + [vm] * 6,
        out_specs=(vm, smem),
        compiler_params=pltpu.CompilerParams(vmem_limit_bytes=6 * 2**20),
        cost_estimate=pl.CostEstimate(flops=10**9, bytes_accessed=4 * 10**6, transcendentals=0),
        name="turn_back",
    )(core, task, mine, got, hot, node, struct, head)


def exchange(value, sizes, steps_first, steps_second):
    mol, nz, ny = sizes
    pairs = []
    for device in range(mol * nz * ny):
        m, t = divmod(device, nz * ny)
        z, y = divmod(t, ny)
        dz, dy = steps_first if m % 2 == 0 else steps_second
        to = ((z + dz) % nz) * ny + (y + dy) % ny
        pairs.append((device, m * nz * ny + to))
    return lax.ppermute(value, ("mol", "task"), pairs)


def body(
    node_embed,
    wigner,
    source,
    target,
    rotation,
    edge_filter,
    edge_count,
    w_zero,
    w_one_real,
    w_one_imag,
    w_two_real,
    w_two_imag,
    atom_struct,
    struct_task,
    task_head,
):
    sizes = (8, 8, 4)
    core = lax.axis_index("mol") % 2
    task = lax.axis_index("task")
    z, y = task // 4, task % 4
    first = core == 0

    core_vec = core.reshape(1).astype(jnp.int32)

    def pick(a, b):
        return jnp.where(first, a, b)

    b0 = pack(core_vec, w_zero, w_one_real, w_one_imag, w_two_real, w_two_imag)
    a1 = exchange(b0, sizes, (0, 1), (1, 0))
    a2 = exchange(b0, sizes, (0, -1), (-1, 0))
    a3 = exchange(b0, sizes, (0, 2), (4, 0))
    h0 = jnp.concatenate((b0, a1))
    h1 = jnp.concatenate((a2, a3))

    def forth(value, second=(0, 1)):
        return exchange(value, sizes, (1, 0), second)

    def aft(value, second=(0, -1)):
        return exchange(value, sizes, (-1, 0), second)

    q, h1 = lax.optimization_barrier((pick(h0, jnp.concatenate((a1, a3))), h1))
    p1p, p1m = lax.optimization_barrier((forth(q, (1, 0)), aft(h1, (-1, 0))))
    def both(a, b):
        return jnp.concatenate((a, b))

    x1p = both(pick(h1, h0), pick(p1p, h1))
    x1m = both(pick(h0, p1p), p1m)
    s1p, s1m = forth(x1p), aft(x1m)

    live = (jnp.arange(EDGES, dtype=jnp.int32) < edge_count[0])[:, None]
    filters = jnp.where(live, edge_filter, jnp.zeros_like(edge_filter))
    own, send, entries, node_first = features(
        core_vec,
        node_embed,
        wigner.transpose(1, 2, 0),
        source.reshape(EDGES, 1),
        target.reshape(EDGES, 1),
        rotation.reshape(EDGES, 1),
        filters,
    )

    s1p, s1m, send = lax.optimization_barrier((s1p, s1m, send))
    offsets_first, offsets_second = block_offsets()
    table = jnp.asarray((offsets_first, offsets_second), jnp.int32)[core]
    shard = ((z + table[:, 0]) % 8) * 4 + (y + table[:, 1]) % 4

    swap = [(i, i ^ 1) for i in range(8)]
    got = lax.ppermute(send, "mol", swap)
    late, late_zero = choose(core_vec, shard, own, got, (b0, a1, a2, a3, p1p, p1m))
    s2p, s2m, late = lax.optimization_barrier((forth(s1p), aft(s1m), late))
    s3p, s3m = forth(s2p), aft(s2m)
    blocks = (b0, a1, a2, a3, p1p, p1m, s1p, s1m, s2p, s2m)
    parts = mix_early(core_vec, shard, blocks, own, got)
    held = (4, TILES, 8, C)
    mine, other = mix_late(core_vec, s3p.reshape(held), s3m.reshape(held), *parts, late, late_zero, own, got)
    back = lax.ppermute(other, "mol", swap)
    hot = ends_of(entries, rotation.reshape(1, EDGES), target.reshape(1, EDGES), mine)
    update, energy = turn_back(
        core_vec,
        struct_task,
        mine,
        back,
        hot,
        node_first,
        atom_struct.reshape(ATOMS, 1),
        task_head,
    )
    return update, energy


def solution(mesh):
    both = P(("mol", "task"))
    wide = P(("mol", "task"), None)
    rows = P("task", None)
    in_specs = (wide, P(), both, both, both, wide, both, rows, rows, rows, rows, rows, both, both, P())
    return jax.shard_map(
        body, mesh=mesh, in_specs=in_specs, out_specs=(wide, both), check_vma=False
    )
```

```python
import jax
import jax.numpy as jnp
from jax import lax
from jax.experimental import pallas as pl
from jax.experimental.pallas import tpu as pltpu
from jax.sharding import PartitionSpec as P

C = 128
COEF = 49
MROWS = 29
EDGES = 192
ATOMS = 48
NROT = 256
TILES = 86
LATE = 8
VMEM = pltpu.VMEM
SMEM = pltpu.SMEM
BF = jnp.bfloat16
F32 = jnp.float32

ROWS = [[degree] for degree in range(7)]
for degree in range(1, 7):
    ROWS[degree] += [6 + degree, 12 + degree]
for degree in range(2, 7):
    ROWS[degree] += [17 + degree, 22 + degree]

MADE = (
    tuple(range(7, 19)) + (0, 1),
    tuple(range(19, 29)) + (2, 3, 4, 5, 6),
)

H0 = ((0, 0), (0, -1))
H1 = ((0, 1), (0, 2))
U = (
    ((0, 0), (-1, 0)),
    ((1, 0), (4, 0)),
    ((-2, 0), (3, 0)),
    ((2, 0), (-3, 0)),
)


def moved(blocks, z, y):
    return [(a + z, b + y) for a, b in blocks]


def block_offsets():
    first = moved(H0, 0, 0) + moved(H1, 0, 0) + moved(H0, -1, 0) + moved(H1, 1, 0)
    for step in (1, 2, 3):
        first += moved(H1, -step, 0) + moved(H0, -step - 1, 0)
        first += moved(H0, step, 0) + moved(H1, step + 1, 0)
    second = [block for part in U for block in part]
    for step in (1, 2, 3):
        second += moved(U[0], 0, -step) + moved(U[1], 0, -step)
        second += moved(U[2], 0, step) + moved(U[3], 0, step)
    return first, second


def feature_kernel(
    core, node, wig, source, target, rotation, filt, own, send, wc_out, node_out, x, xs, xt, wc, fz, fa, sem
):
    wc[...] = jnp.zeros_like(wc)
    for degree in range(7):
        at = degree * degree
        for r in ROWS[degree]:
            wc[r * 16 : r * 16 + 2 * degree + 1, :] = wig[r, at : at + 2 * degree + 1, :].astype(F32)
    entries = wc[...].astype(BF)
    wc_out[...] = entries
    for j in range(COEF):
        x[j * ATOMS : (j + 1) * ATOMS, :] = node[:, j * C : (j + 1) * C]
    width = 13 * ATOMS
    lane = lax.broadcasted_iota(jnp.int32, (1, width), 1)
    atom = lane % ATOMS
    xs[...] = (source[...] == atom).astype(F32).astype(BF)
    xt[...] = (target[...] == atom).astype(F32).astype(BF)
    hot_r = (rotation[...] == lax.broadcasted_iota(jnp.int32, (1, NROT), 1)).astype(F32).astype(BF)
    d_all = lax.dot_general(
        hot_r, entries, (((1,), (1,)), ((), ())), preferred_element_type=F32
    ).astype(BF)
    node_out[...] = node[:, :C]
    slot_one = core[0]
    slot_two = 1 - core[0]
    for slot in range(2):
        fa[slot, :EDGES, 12 * C : 13 * C] = filt[...]
    for degree in range(7):
        wide = (2 * degree + 1) * ATOMS
        at = degree * degree
        which = lax.broadcasted_iota(jnp.int32, (C, wide), 0)
        which = which - lax.broadcasted_iota(jnp.int32, (C, wide), 1) // ATOMS
        coefs = x[at * ATOMS : at * ATOMS + wide, :]
        for r in ROWS[degree]:
            part, offset = divmod(r, 8)
            spread = (which == offset * 16).astype(F32).astype(BF)
            d = d_all[:, part * C : (part + 1) * C]
            d = jnp.dot(d, spread, preferred_element_type=F32).astype(BF)
            one = jnp.dot(d * xs[:, :wide], coefs, preferred_element_type=F32).astype(BF)
            two = jnp.dot(d * xt[:, :wide], coefs, preferred_element_type=F32).astype(BF)
            for at_lane, value in ((0, one), (C, two)):
                if r < 7:
                    fz[:, r * 2 * C + at_lane : r * 2 * C + at_lane + C] = value
                    continue
                slot = slot_one if r < 19 else slot_two
                sign, k = divmod(r - 7, 6) if r < 19 else divmod(r - 19, 5)
                lanes = slice(k * 2 * C + at_lane, k * 2 * C + at_lane + C)
                fa[slot, sign * EDGES : (sign + 1) * EDGES, lanes] = value
    copies = []
    for slot, out in enumerate((own, send)):
        copies += [
            pltpu.make_async_copy(fz, out.at[pl.ds(0, EDGES)], sem.at[2 * slot]),
            pltpu.make_async_copy(
                fa.at[slot], out.at[pl.ds(EDGES, 2 * EDGES)], sem.at[2 * slot + 1]
            ),
        ]
    for copy in copies:
        copy.start()
    for copy in copies:
        copy.wait()


def features(core, node, wig, source, target, rotation, filt):
    vm = pl.BlockSpec(memory_space=VMEM)
    anywhere = pl.BlockSpec(memory_space=pl.ANY)
    return pl.pallas_call(
        feature_kernel,
        out_shape=(
            jax.ShapeDtypeStruct((3 * EDGES, 14 * C), BF),
            jax.ShapeDtypeStruct((3 * EDGES, 14 * C), BF),
            jax.ShapeDtypeStruct((4 * C, NROT), BF),
            jax.ShapeDtypeStruct((ATOMS, C), BF),
        ),
        in_specs=[pl.BlockSpec(memory_space=SMEM)] + [vm] * 6,
        out_specs=(anywhere, anywhere, vm, vm),
        scratch_shapes=[
            VMEM((COEF * ATOMS, C), BF),
            VMEM((EDGES, 13 * ATOMS), BF),
            VMEM((EDGES, 13 * ATOMS), BF),
            VMEM((4 * C, NROT), F32),
            VMEM((EDGES, 14 * C), BF),
            VMEM((2, 2 * EDGES, 14 * C), BF),
            pltpu.SemaphoreType.DMA((4,)),
        ],
        compiler_params=pltpu.CompilerParams(vmem_limit_bytes=8 * 2**20),
        cost_estimate=pl.CostEstimate(flops=6 * 10**9, bytes_accessed=8 * 10**6, transcendentals=0),
        name="features",
    )(core, node, wig, source, target, rotation, filt)


def pack_kernel(core, *refs):
    given, out, held, sem = refs[:5], refs[5], refs[6:11], refs[11]
    zero, one_real, one_imag, two_real, two_imag = held

    def run(parts):
        copies = []
        for i in range(5):
            if any(held[i] is part[0] for part in parts):
                copies.append(pltpu.make_async_copy(given[i], held[i], sem.at[i]))
        for copy in copies:
            copy.start()
        for copy in copies:
            copy.wait()
        at = 0
        for ref, first, groups in parts:
            tiles = ref.shape[0] // 8
            for g in range(first, first + groups):
                out[at : at + tiles] = ref[:, g * C : (g + 1) * C].reshape(tiles, 8, C)
                at += tiles
        if at < TILES:
            out[at:] = jnp.zeros((TILES - at, 8, C), BF)

    @pl.when(core[0] == 0)
    def _():
        run(((one_real, 0, 6), (one_imag, 0, 6), (zero, 0, 2)))

    @pl.when(core[0] == 1)
    def _():
        run(((two_real, 0, 5), (two_imag, 0, 5), (zero, 2, 5)))


def pack(core, zero, one_real, one_imag, two_real, two_imag):
    vm = pl.BlockSpec(memory_space=VMEM)
    return pl.pallas_call(
        pack_kernel,
        out_shape=jax.ShapeDtypeStruct((TILES, 8, C), BF),
        in_specs=[pl.BlockSpec(memory_space=SMEM)] + [pl.BlockSpec(memory_space=pltpu.HBM)] * 5,
        out_specs=vm,
        scratch_shapes=[VMEM(w.shape, BF) for w in (zero, one_real, one_imag, two_real, two_imag)]
        + [pltpu.SemaphoreType.DMA((5,))],
        compiler_params=pltpu.CompilerParams(vmem_limit_bytes=60 * 2**20),
        name="pack",
    )(core, zero, one_real, one_imag, two_real, two_imag)


def by_core(core, run):
    @pl.when(core[0] == 0)
    def _():
        run(6, 6, 2)

    @pl.when(core[0] == 1)
    def _():
        run(5, 5, 5)


def group_rows(held, first, count, g):
    tiles = held[:, pl.ds(first + g * count, count)]
    return tiles.reshape(held.shape[0] * count * 8, C)


def zero_features(own, got):
    return jnp.concatenate((own[:EDGES, :], got[:EDGES, :]), axis=0)


def order_features(own, got, deep):
    return jnp.concatenate((own[EDGES:, :deep], got[EDGES:, :deep]), axis=0)


def choose_kernel(core, shard, own, got, *refs):
    late, late_zero = refs[6:]

    def chosen(rows, deep):
        lane = lax.broadcasted_iota(jnp.int32, (1, LATE * rows), 1)
        wanted = lane
        for i in range(LATE):
            here = jnp.logical_and(lane >= i * rows, lane < (i + 1) * rows)
            wanted = jnp.where(here, lane + (shard[32 - LATE + i] - i) * rows, wanted)
        return (lax.broadcasted_iota(jnp.int32, (deep, 1), 0) == wanted).astype(F32).astype(BF)

    def run(pieces, tiles, zero_groups):
        del zero_groups
        deep = pieces * 2 * C
        rows = tiles * 8
        late[:, : LATE * rows] = jnp.dot(
            order_features(own, got, deep), chosen(rows, deep), preferred_element_type=F32
        ).astype(BF)
        late_zero[...] = jnp.dot(
            zero_features(own, got), chosen(56, 14 * C), preferred_element_type=F32
        ).astype(BF)

    by_core(core, run)


def choose(core, shard, own, got, blocks):
    vm = pl.BlockSpec(memory_space=VMEM)
    smem = pl.BlockSpec(memory_space=SMEM)
    return pl.pallas_call(
        choose_kernel,
        out_shape=(
            jax.ShapeDtypeStruct((4 * EDGES, LATE * 48), BF),
            jax.ShapeDtypeStruct((2 * EDGES, LATE * 56), BF),
        ),
        in_specs=[smem, smem] + [vm] * 8,
        out_specs=(vm, vm),
        compiler_params=pltpu.CompilerParams(vmem_limit_bytes=8 * 2**20),
        cost_estimate=pl.CostEstimate(flops=10**9, bytes_accessed=4 * 10**6, transcendentals=0),
        name="choose",
    )(core, shard, own, got, *blocks)


def early_kernel(core, shard, *refs):
    blocks = refs[:10]
    own, got, part, part_zero, w_all = refs[10:]

    def run(pieces, tiles, zero_groups):
        deep = pieces * 2 * C
        size = pieces * tiles

        def column(g, carry):
            w = jnp.concatenate(
                (group_rows(w_all, 0, tiles, g), group_rows(w_all, size, tiles, g)), axis=1
            )
            part[g] = jnp.dot(order_features(own, got, deep), w, preferred_element_type=F32)
            return carry

        lax.fori_loop(0, pieces, column, 0)
        for g in range(0, zero_groups, 2):
            count = min(2, zero_groups - g)
            w = jnp.concatenate(
                [group_rows(w_all, 2 * size, 7, g + i) for i in range(count)], axis=1
            )
            part_zero[g // 2, :, : count * C] = jnp.dot(
                zero_features(own, got), w, preferred_element_type=F32
            )

    def place(block, index):
        def one(i, carry):
            w_all[shard[index + i]] = block[pl.ds(i * TILES, TILES)]
            return carry

        lax.fori_loop(0, block.shape[0] // TILES, one, 0)

    index = 0
    for block in blocks:
        place(block, index)
        index += block.shape[0] // TILES

    def clear(i, carry):
        w_all[shard[32 - LATE + i]] = jnp.zeros((TILES, 8, C), BF)
        return carry

    lax.fori_loop(0, LATE, clear, 0)
    by_core(core, run)


def mix_early(core, shard, blocks, own, got):
    vm = pl.BlockSpec(memory_space=VMEM)
    smem = pl.BlockSpec(memory_space=SMEM)
    return pl.pallas_call(
        early_kernel,
        out_shape=(
            jax.ShapeDtypeStruct((6, 4 * EDGES, 2 * C), F32),
            jax.ShapeDtypeStruct((3, 2 * EDGES, 2 * C), F32),
        ),
        in_specs=[smem, smem] + [vm] * 12,
        out_specs=(vm, vm),
        scratch_shapes=[VMEM((32, TILES, 8, C), BF)],
        compiler_params=pltpu.CompilerParams(vmem_limit_bytes=16 * 2**20),
        cost_estimate=pl.CostEstimate(flops=4 * 10**9, bytes_accessed=12 * 10**6, transcendentals=0),
        name="mix_early",
    )(core, shard, *blocks, own, got)


def late_kernel(core, up, down, part, part_zero, late, late_zero, own, got, mine, other):
    def finish(plane, own_value, got_value, filters):
        mine[plane] = (own_value * filters[0]).astype(BF)
        other[plane] = (got_value * filters[1]).astype(BF)

    def run(pieces, tiles, zero_groups):
        filters = [ref[EDGES : 2 * EDGES, 12 * C : 13 * C].astype(F32) for ref in (own, got)]
        size = pieces * tiles

        def rows_of(first, count, g):
            return jnp.concatenate(
                (group_rows(up, first, count, g), group_rows(down, first, count, g)), axis=0
            )

        def column(g, carry):
            w = jnp.concatenate((rows_of(0, tiles, g), rows_of(size, tiles, g)), axis=1)
            both = part[g] + jnp.dot(
                late[:, : LATE * tiles * 8], w, preferred_element_type=F32
            )
            real = [both[i * EDGES : (i + 1) * EDGES, :C] for i in range(4)]
            imag = [both[i * EDGES : (i + 1) * EDGES, C:] for i in range(4)]
            finish(g, real[0] - imag[1], real[2] - imag[3], filters)
            finish(pieces + g, real[1] + imag[0], real[3] + imag[2], filters)
            return carry

        lax.fori_loop(0, pieces, column, 0, unroll=True)
        for g in range(0, zero_groups, 2):
            count = min(2, zero_groups - g)
            w = jnp.concatenate([rows_of(2 * size, 7, g + i) for i in range(count)], axis=1)
            total = part_zero[g // 2, :, : count * C] + jnp.dot(
                late_zero[...], w, preferred_element_type=F32
            )
            for i in range(count):
                value = total[:, i * C : (i + 1) * C]
                finish(2 * pieces + g + i, value[:EDGES], value[EDGES:], filters)

    by_core(core, run)


def mix_late(core, up, down, part, part_zero, late, late_zero, own, got):
    vm = pl.BlockSpec(memory_space=VMEM)
    out = jax.ShapeDtypeStruct((15, EDGES, C), BF)
    return pl.pallas_call(
        late_kernel,
        out_shape=(out, out),
        in_specs=[pl.BlockSpec(memory_space=SMEM)] + [vm] * 8,
        out_specs=(vm, vm),
        compiler_params=pltpu.CompilerParams(vmem_limit_bytes=8 * 2**20),
        cost_estimate=pl.CostEstimate(flops=10**9, bytes_accessed=8 * 10**6, transcendentals=0),
        name="mix_late",
    )(core, up, down, part, part_zero, late, late_zero, own, got)


def ends_kernel(wig, rotation, target, after, out):
    del after
    hot_r = lax.broadcasted_iota(jnp.int32, (NROT, EDGES), 0) == rotation[...]
    d = jnp.dot(wig[...], hot_r.astype(F32).astype(BF), preferred_element_type=F32)
    ends = lax.broadcasted_iota(jnp.int32, (ATOMS, EDGES), 0) == target[...]
    at = 0
    for degree in range(7):
        for r in ROWS[degree]:
            for j in range(2 * degree + 1):
                entry = d[r * 16 + j : r * 16 + j + 1, :]
                out[at : at + ATOMS, :] = jnp.where(ends, entry, 0.0).astype(BF)
                at += ATOMS


def ends_of(wig, rotation, target, after):
    vm = pl.BlockSpec(memory_space=VMEM)
    return pl.pallas_call(
        ends_kernel,
        out_shape=jax.ShapeDtypeStruct((235 * ATOMS, EDGES), BF),
        in_specs=[vm] * 3 + [pl.BlockSpec(memory_space=pl.ANY)],
        out_specs=vm,
        compiler_params=pltpu.CompilerParams(vmem_limit_bytes=4 * 2**20),
        cost_estimate=pl.CostEstimate(flops=10**8, bytes_accessed=6 * 10**6, transcendentals=0),
        name="ends_of",
    )(wig, rotation, target, after)


def back_kernel(core, task, mine, got, hot, node, struct, head, update, energy):
    is_first = core[0] == 0

    def message(r):
        if r in MADE[0]:
            i = MADE[0].index(r)
            return jnp.where(is_first, mine[i], got[i])
        i = MADE[1].index(r)
        return jnp.where(is_first, got[i], mine[i])

    at = 0
    for degree in range(7):
        span = 2 * degree + 1
        total = None
        for r in ROWS[degree]:
            term = jnp.dot(hot[at : at + span * ATOMS, :], message(r), preferred_element_type=F32)
            total = term if total is None else total + term
            at += span * ATOMS
        for place in range(span):
            value = total[place * ATOMS : (place + 1) * ATOMS]
            j = degree * degree + place
            update[:, j * C : (j + 1) * C] = value.astype(BF)
            if j == 0:
                scalar_part = node[...].astype(F32) + value
    for s in range(4):
        member = jnp.where(struct[...] == s, scalar_part, 0.0) * head[pl.ds(task[s], 1), :]
        energy[s] = jnp.sum(member)


def turn_back(core, task, mine, got, hot, node, struct, head):
    vm = pl.BlockSpec(memory_space=VMEM)
    smem = pl.BlockSpec(memory_space=SMEM)
    return pl.pallas_call(
        back_kernel,
        out_shape=(
            jax.ShapeDtypeStruct((ATOMS, COEF * C), BF),
            jax.ShapeDtypeStruct((4,), F32),
        ),
        in_specs=[smem] * 2 + [vm] * 6,
        out_specs=(vm, smem),
        compiler_params=pltpu.CompilerParams(vmem_limit_bytes=6 * 2**20),
        cost_estimate=pl.CostEstimate(flops=10**9, bytes_accessed=4 * 10**6, transcendentals=0),
        name="turn_back",
    )(core, task, mine, got, hot, node, struct, head)


def exchange(value, sizes, steps_first, steps_second):
    mol, nz, ny = sizes
    pairs = []
    for device in range(mol * nz * ny):
        m, t = divmod(device, nz * ny)
        z, y = divmod(t, ny)
        dz, dy = steps_first if m % 2 == 0 else steps_second
        to = ((z + dz) % nz) * ny + (y + dy) % ny
        pairs.append((device, m * nz * ny + to))
    return lax.ppermute(value, ("mol", "task"), pairs)


def body(
    node_embed,
    wigner,
    source,
    target,
    rotation,
    edge_filter,
    edge_count,
    w_zero,
    w_one_real,
    w_one_imag,
    w_two_real,
    w_two_imag,
    atom_struct,
    struct_task,
    task_head,
):
    sizes = (8, 8, 4)
    core = lax.axis_index("mol") % 2
    task = lax.axis_index("task")
    z, y = task // 4, task % 4
    first = core == 0

    core_vec = core.reshape(1).astype(jnp.int32)

    def pick(a, b):
        return jnp.where(first, a, b)

    b0 = pack(core_vec, w_zero, w_one_real, w_one_imag, w_two_real, w_two_imag)
    a1 = exchange(b0, sizes, (0, 1), (1, 0))
    a2 = exchange(b0, sizes, (0, -1), (-1, 0))
    a3 = exchange(b0, sizes, (0, 2), (4, 0))
    h0 = jnp.concatenate((b0, a1))
    h1 = jnp.concatenate((a2, a3))

    def forth(value, second=(0, 1)):
        return exchange(value, sizes, (1, 0), second)

    def aft(value, second=(0, -1)):
        return exchange(value, sizes, (-1, 0), second)

    q, h1 = lax.optimization_barrier((pick(h0, jnp.concatenate((a1, a3))), h1))
    p1p, p1m = lax.optimization_barrier((forth(q, (1, 0)), aft(h1, (-1, 0))))
    def both(a, b):
        return jnp.concatenate((a, b))

    x1p = both(pick(h1, h0), pick(p1p, h1))
    x1m = both(pick(h0, p1p), p1m)
    x1p, x1m = lax.optimization_barrier((x1p, x1m))
    s1p, s1m = forth(x1p), aft(x1m)

    live = (jnp.arange(EDGES, dtype=jnp.int32) < edge_count[0])[:, None]
    filters = jnp.where(live, edge_filter, jnp.zeros_like(edge_filter))
    own, send, entries, node_first = features(
        core_vec,
        node_embed,
        wigner.transpose(1, 2, 0),
        source.reshape(EDGES, 1),
        target.reshape(EDGES, 1),
        rotation.reshape(EDGES, 1),
        filters,
    )

    s1p, s1m, send = lax.optimization_barrier((s1p, s1m, send))
    offsets_first, offsets_second = block_offsets()
    table = jnp.asarray((offsets_first, offsets_second), jnp.int32)[core]
    shard = ((z + table[:, 0]) % 8) * 4 + (y + table[:, 1]) % 4

    swap = [(i, i ^ 1) for i in range(8)]
    got = lax.ppermute(send, "mol", swap)
    late, late_zero = choose(core_vec, shard, own, got, (b0, a1, a2, a3, p1p, p1m))
    s2p, s2m, late = lax.optimization_barrier((forth(s1p), aft(s1m), late))
    s3p, s3m = lax.optimization_barrier((forth(s2p), aft(s2m)))
    blocks = (b0, a1, a2, a3, p1p, p1m, s1p, s1m, s2p, s2m)
    parts = mix_early(core_vec, shard, blocks, own, got)
    held = (4, TILES, 8, C)
    mine, other = mix_late(core_vec, s3p.reshape(held), s3m.reshape(held), *parts, late, late_zero, own, got)
    back = lax.ppermute(other, "mol", swap)
    hot = ends_of(entries, rotation.reshape(1, EDGES), target.reshape(1, EDGES), mine)
    update, energy = turn_back(
        core_vec,
        struct_task,
        mine,
        back,
        hot,
        node_first,
        atom_struct.reshape(ATOMS, 1),
        task_head,
    )
    return update, energy


def solution(mesh):
    both = P(("mol", "task"))
    wide = P(("mol", "task"), None)
    rows = P("task", None)
    in_specs = (wide, P(), both, both, both, wide, both, rows, rows, rows, rows, rows, both, both, P())
    return jax.shard_map(
        body, mesh=mesh, in_specs=in_specs, out_specs=(wide, both), check_vma=False
    )
```

```python
import jax
import jax.numpy as jnp
from jax import lax
from jax.experimental import pallas as pl
from jax.experimental.pallas import tpu as pltpu
from jax.sharding import PartitionSpec as P

C = 128
COEF = 49
MROWS = 29
EDGES = 192
ATOMS = 48
NROT = 256
TILES = 86
LATE = 8
VMEM = pltpu.VMEM
SMEM = pltpu.SMEM
BF = jnp.bfloat16
F32 = jnp.float32

ROWS = [[degree] for degree in range(7)]
for degree in range(1, 7):
    ROWS[degree] += [6 + degree, 12 + degree]
for degree in range(2, 7):
    ROWS[degree] += [17 + degree, 22 + degree]

MADE = (
    tuple(range(7, 19)) + (0, 1),
    tuple(range(19, 29)) + (2, 3, 4, 5, 6),
)

H0 = ((0, 0), (0, -1))
H1 = ((0, 1), (0, 2))
U = (
    ((0, 0), (-1, 0)),
    ((1, 0), (4, 0)),
    ((-2, 0), (3, 0)),
    ((2, 0), (-3, 0)),
)


def moved(blocks, z, y):
    return [(a + z, b + y) for a, b in blocks]


def block_offsets():
    first = moved(H0, 0, 0) + moved(H1, 0, 0) + moved(H0, -1, 0) + moved(H1, 1, 0)
    for step in (1, 2, 3):
        first += moved(H1, -step, 0) + moved(H0, -step - 1, 0)
        first += moved(H0, step, 0) + moved(H1, step + 1, 0)
    second = [block for part in U for block in part]
    for step in (1, 2, 3):
        second += moved(U[0], 0, -step) + moved(U[1], 0, -step)
        second += moved(U[2], 0, step) + moved(U[3], 0, step)
    return first, second


def feature_kernel(
    core, node, wig, source, target, rotation, filt, own, send, wc_out, node_out, x, xs, xt, wc, fz, fa, sem
):
    wc[...] = jnp.zeros_like(wc)
    for degree in range(7):
        at = degree * degree
        for r in ROWS[degree]:
            wc[r * 16 : r * 16 + 2 * degree + 1, :] = wig[r, at : at + 2 * degree + 1, :].astype(F32)
    entries = wc[...].astype(BF)
    wc_out[...] = entries
    for j in range(COEF):
        x[j * ATOMS : (j + 1) * ATOMS, :] = node[:, j * C : (j + 1) * C]
    width = 13 * ATOMS
    lane = lax.broadcasted_iota(jnp.int32, (1, width), 1)
    atom = lane % ATOMS
    xs[...] = (source[...] == atom).astype(F32).astype(BF)
    xt[...] = (target[...] == atom).astype(F32).astype(BF)
    hot_r = (rotation[...] == lax.broadcasted_iota(jnp.int32, (1, NROT), 1)).astype(F32).astype(BF)
    d_all = lax.dot_general(
        hot_r, entries, (((1,), (1,)), ((), ())), preferred_element_type=F32
    ).astype(BF)
    node_out[...] = node[:, :C]
    slot_one = core[0]
    slot_two = 1 - core[0]
    for slot in range(2):
        fa[slot, :EDGES, 12 * C : 13 * C] = filt[...]
    for degree in range(7):
        wide = (2 * degree + 1) * ATOMS
        at = degree * degree
        which = lax.broadcasted_iota(jnp.int32, (C, wide), 0)
        which = which - lax.broadcasted_iota(jnp.int32, (C, wide), 1) // ATOMS
        coefs = x[at * ATOMS : at * ATOMS + wide, :]
        for r in ROWS[degree]:
            part, offset = divmod(r, 8)
            spread = (which == offset * 16).astype(F32).astype(BF)
            d = d_all[:, part * C : (part + 1) * C]
            d = jnp.dot(d, spread, preferred_element_type=F32).astype(BF)
            one = jnp.dot(d * xs[:, :wide], coefs, preferred_element_type=F32).astype(BF)
            two = jnp.dot(d * xt[:, :wide], coefs, preferred_element_type=F32).astype(BF)
            for at_lane, value in ((0, one), (C, two)):
                if r < 7:
                    fz[:, r * 2 * C + at_lane : r * 2 * C + at_lane + C] = value
                    continue
                slot = slot_one if r < 19 else slot_two
                sign, k = divmod(r - 7, 6) if r < 19 else divmod(r - 19, 5)
                lanes = slice(k * 2 * C + at_lane, k * 2 * C + at_lane + C)
                fa[slot, sign * EDGES : (sign + 1) * EDGES, lanes] = value
    copies = []
    for slot, out in enumerate((own, send)):
        copies += [
            pltpu.make_async_copy(fz, out.at[pl.ds(0, EDGES)], sem.at[2 * slot]),
            pltpu.make_async_copy(
                fa.at[slot], out.at[pl.ds(EDGES, 2 * EDGES)], sem.at[2 * slot + 1]
            ),
        ]
    for copy in copies:
        copy.start()
    for copy in copies:
        copy.wait()


def features(core, node, wig, source, target, rotation, filt):
    vm = pl.BlockSpec(memory_space=VMEM)
    anywhere = pl.BlockSpec(memory_space=pl.ANY)
    return pl.pallas_call(
        feature_kernel,
        out_shape=(
            jax.ShapeDtypeStruct((3 * EDGES, 14 * C), BF),
            jax.ShapeDtypeStruct((3 * EDGES, 14 * C), BF),
            jax.ShapeDtypeStruct((4 * C, NROT), BF),
            jax.ShapeDtypeStruct((ATOMS, C), BF),
        ),
        in_specs=[pl.BlockSpec(memory_space=SMEM)] + [vm] * 6,
        out_specs=(anywhere, anywhere, vm, vm),
        scratch_shapes=[
            VMEM((COEF * ATOMS, C), BF),
            VMEM((EDGES, 13 * ATOMS), BF),
            VMEM((EDGES, 13 * ATOMS), BF),
            VMEM((4 * C, NROT), F32),
            VMEM((EDGES, 14 * C), BF),
            VMEM((2, 2 * EDGES, 14 * C), BF),
            pltpu.SemaphoreType.DMA((4,)),
        ],
        compiler_params=pltpu.CompilerParams(vmem_limit_bytes=8 * 2**20),
        cost_estimate=pl.CostEstimate(flops=6 * 10**9, bytes_accessed=8 * 10**6, transcendentals=0),
        name="features",
    )(core, node, wig, source, target, rotation, filt)


def pack_kernel(core, *refs):
    given, out, held, sem = refs[:5], refs[5], refs[6:11], refs[11]
    zero, one_real, one_imag, two_real, two_imag = held

    def run(parts):
        copies = []
        for i in range(5):
            if any(held[i] is part[0] for part in parts):
                copies.append(pltpu.make_async_copy(given[i], held[i], sem.at[i]))
        for copy in copies:
            copy.start()
        for copy in copies:
            copy.wait()
        at = 0
        for ref, first, groups in parts:
            tiles = ref.shape[0] // 8
            for g in range(first, first + groups):
                out[at : at + tiles] = ref[:, g * C : (g + 1) * C].reshape(tiles, 8, C)
                at += tiles
        if at < TILES:
            out[at:] = jnp.zeros((TILES - at, 8, C), BF)

    @pl.when(core[0] == 0)
    def _():
        run(((one_real, 0, 6), (one_imag, 0, 6), (zero, 0, 2)))

    @pl.when(core[0] == 1)
    def _():
        run(((two_real, 0, 5), (two_imag, 0, 5), (zero, 2, 5)))


def pack(core, zero, one_real, one_imag, two_real, two_imag):
    vm = pl.BlockSpec(memory_space=VMEM)
    return pl.pallas_call(
        pack_kernel,
        out_shape=jax.ShapeDtypeStruct((TILES, 8, C), BF),
        in_specs=[pl.BlockSpec(memory_space=SMEM)] + [pl.BlockSpec(memory_space=pltpu.HBM)] * 5,
        out_specs=vm,
        scratch_shapes=[VMEM(w.shape, BF) for w in (zero, one_real, one_imag, two_real, two_imag)]
        + [pltpu.SemaphoreType.DMA((5,))],
        compiler_params=pltpu.CompilerParams(vmem_limit_bytes=60 * 2**20),
        name="pack",
    )(core, zero, one_real, one_imag, two_real, two_imag)


def by_core(core, run):
    @pl.when(core[0] == 0)
    def _():
        run(6, 6, 2)

    @pl.when(core[0] == 1)
    def _():
        run(5, 5, 5)


def group_rows(held, first, count, g):
    tiles = held[:, pl.ds(first + g * count, count)]
    return tiles.reshape(held.shape[0] * count * 8, C)


def zero_features(own, got):
    return jnp.concatenate((own[:EDGES, :], got[:EDGES, :]), axis=0)


def order_features(own, got, deep):
    return jnp.concatenate((own[EDGES:, :deep], got[EDGES:, :deep]), axis=0)


def choose_kernel(core, shard, own, got, *refs):
    late, late_zero = refs[6:]

    def chosen(rows, deep):
        lane = lax.broadcasted_iota(jnp.int32, (1, LATE * rows), 1)
        wanted = lane
        for i in range(LATE):
            here = jnp.logical_and(lane >= i * rows, lane < (i + 1) * rows)
            wanted = jnp.where(here, lane + (shard[32 - LATE + i] - i) * rows, wanted)
        return (lax.broadcasted_iota(jnp.int32, (deep, 1), 0) == wanted).astype(F32).astype(BF)

    def run(pieces, tiles, zero_groups):
        del zero_groups
        deep = pieces * 2 * C
        rows = tiles * 8
        late[:, : LATE * rows] = jnp.dot(
            order_features(own, got, deep), chosen(rows, deep), preferred_element_type=F32
        ).astype(BF)
        late_zero[...] = jnp.dot(
            zero_features(own, got), chosen(56, 14 * C), preferred_element_type=F32
        ).astype(BF)

    by_core(core, run)


def choose(core, shard, own, got, blocks):
    vm = pl.BlockSpec(memory_space=VMEM)
    smem = pl.BlockSpec(memory_space=SMEM)
    return pl.pallas_call(
        choose_kernel,
        out_shape=(
            jax.ShapeDtypeStruct((4 * EDGES, LATE * 48), BF),
            jax.ShapeDtypeStruct((2 * EDGES, LATE * 56), BF),
        ),
        in_specs=[smem, smem] + [vm] * 8,
        out_specs=(vm, vm),
        compiler_params=pltpu.CompilerParams(vmem_limit_bytes=8 * 2**20),
        cost_estimate=pl.CostEstimate(flops=10**9, bytes_accessed=4 * 10**6, transcendentals=0),
        name="choose",
    )(core, shard, own, got, *blocks)


def early_kernel(core, shard, *refs):
    blocks = refs[:10]
    own, got, part, part_zero, w_all = refs[10:]

    def run(pieces, tiles, zero_groups):
        deep = pieces * 2 * C
        size = pieces * tiles

        def column(g, carry):
            w = jnp.concatenate(
                (group_rows(w_all, 0, tiles, g), group_rows(w_all, size, tiles, g)), axis=1
            )
            part[g] = jnp.dot(order_features(own, got, deep), w, preferred_element_type=F32)
            return carry

        lax.fori_loop(0, pieces, column, 0)
        for g in range(0, zero_groups, 2):
            count = min(2, zero_groups - g)
            w = jnp.concatenate(
                [group_rows(w_all, 2 * size, 7, g + i) for i in range(count)], axis=1
            )
            part_zero[g // 2, :, : count * C] = jnp.dot(
                zero_features(own, got), w, preferred_element_type=F32
            )

    def place(block, index):
        def one(i, carry):
            w_all[shard[index + i]] = block[pl.ds(i * TILES, TILES)]
            return carry

        lax.fori_loop(0, block.shape[0] // TILES, one, 0)

    index = 0
    for block in blocks:
        place(block, index)
        index += block.shape[0] // TILES

    def clear(i, carry):
        w_all[shard[32 - LATE + i]] = jnp.zeros((TILES, 8, C), BF)
        return carry

    lax.fori_loop(0, LATE, clear, 0)
    by_core(core, run)


def mix_early(core, shard, blocks, own, got):
    vm = pl.BlockSpec(memory_space=VMEM)
    smem = pl.BlockSpec(memory_space=SMEM)
    return pl.pallas_call(
        early_kernel,
        out_shape=(
            jax.ShapeDtypeStruct((6, 4 * EDGES, 2 * C), F32),
            jax.ShapeDtypeStruct((3, 2 * EDGES, 2 * C), F32),
        ),
        in_specs=[smem, smem] + [vm] * 12,
        out_specs=(vm, vm),
        scratch_shapes=[VMEM((32, TILES, 8, C), BF)],
        compiler_params=pltpu.CompilerParams(vmem_limit_bytes=16 * 2**20),
        cost_estimate=pl.CostEstimate(flops=4 * 10**9, bytes_accessed=12 * 10**6, transcendentals=0),
        name="mix_early",
    )(core, shard, *blocks, own, got)


def late_kernel(core, up, down, part, part_zero, late, late_zero, own, got, mine, other):
    def finish(plane, own_value, got_value, filters):
        mine[plane] = (own_value * filters[0]).astype(BF)
        other[plane] = (got_value * filters[1]).astype(BF)

    def run(pieces, tiles, zero_groups):
        filters = [ref[EDGES : 2 * EDGES, 12 * C : 13 * C].astype(F32) for ref in (own, got)]
        size = pieces * tiles

        def rows_of(first, count, g):
            return jnp.concatenate(
                (group_rows(up, first, count, g), group_rows(down, first, count, g)), axis=0
            )

        def column(g, carry):
            w = jnp.concatenate((rows_of(0, tiles, g), rows_of(size, tiles, g)), axis=1)
            both = part[g] + jnp.dot(
                late[:, : LATE * tiles * 8], w, preferred_element_type=F32
            )
            real = [both[i * EDGES : (i + 1) * EDGES, :C] for i in range(4)]
            imag = [both[i * EDGES : (i + 1) * EDGES, C:] for i in range(4)]
            finish(g, real[0] - imag[1], real[2] - imag[3], filters)
            finish(pieces + g, real[1] + imag[0], real[3] + imag[2], filters)
            return carry

        lax.fori_loop(0, pieces, column, 0, unroll=True)
        for g in range(0, zero_groups, 2):
            count = min(2, zero_groups - g)
            w = jnp.concatenate([rows_of(2 * size, 7, g + i) for i in range(count)], axis=1)
            total = part_zero[g // 2, :, : count * C] + jnp.dot(
                late_zero[...], w, preferred_element_type=F32
            )
            for i in range(count):
                value = total[:, i * C : (i + 1) * C]
                finish(2 * pieces + g + i, value[:EDGES], value[EDGES:], filters)

    by_core(core, run)


def mix_late(core, up, down, part, part_zero, late, late_zero, own, got):
    vm = pl.BlockSpec(memory_space=VMEM)
    out = jax.ShapeDtypeStruct((15, EDGES, C), BF)
    return pl.pallas_call(
        late_kernel,
        out_shape=(out, out),
        in_specs=[pl.BlockSpec(memory_space=SMEM)] + [vm] * 8,
        out_specs=(vm, vm),
        compiler_params=pltpu.CompilerParams(vmem_limit_bytes=8 * 2**20),
        cost_estimate=pl.CostEstimate(flops=10**9, bytes_accessed=8 * 10**6, transcendentals=0),
        name="mix_late",
    )(core, up, down, part, part_zero, late, late_zero, own, got)


def ends_kernel(wig, rotation, target, after, out):
    del after
    hot_r = lax.broadcasted_iota(jnp.int32, (NROT, EDGES), 0) == rotation[...]
    d = jnp.dot(wig[...], hot_r.astype(F32).astype(BF), preferred_element_type=F32)
    ends = lax.broadcasted_iota(jnp.int32, (ATOMS, EDGES), 0) == target[...]
    at = 0
    for degree in range(7):
        for r in ROWS[degree]:
            for j in range(2 * degree + 1):
                entry = d[r * 16 + j : r * 16 + j + 1, :]
                out[at : at + ATOMS, :] = jnp.where(ends, entry, 0.0).astype(BF)
                at += ATOMS


def ends_of(wig, rotation, target, after):
    vm = pl.BlockSpec(memory_space=VMEM)
    return pl.pallas_call(
        ends_kernel,
        out_shape=jax.ShapeDtypeStruct((235 * ATOMS, EDGES), BF),
        in_specs=[vm] * 3 + [pl.BlockSpec(memory_space=pl.ANY)],
        out_specs=vm,
        compiler_params=pltpu.CompilerParams(vmem_limit_bytes=4 * 2**20),
        cost_estimate=pl.CostEstimate(flops=10**8, bytes_accessed=6 * 10**6, transcendentals=0),
        name="ends_of",
    )(wig, rotation, target, after)


def back_kernel(core, task, mine, got, hot, node, struct, head, update, energy):
    is_first = core[0] == 0

    def message(r):
        if r in MADE[0]:
            i = MADE[0].index(r)
            return jnp.where(is_first, mine[i], got[i])
        i = MADE[1].index(r)
        return jnp.where(is_first, got[i], mine[i])

    at = 0
    for degree in range(7):
        span = 2 * degree + 1
        total = None
        for r in ROWS[degree]:
            term = jnp.dot(hot[at : at + span * ATOMS, :], message(r), preferred_element_type=F32)
            total = term if total is None else total + term
            at += span * ATOMS
        for place in range(span):
            value = total[place * ATOMS : (place + 1) * ATOMS]
            j = degree * degree + place
            update[:, j * C : (j + 1) * C] = value.astype(BF)
            if j == 0:
                scalar_part = node[...].astype(F32) + value
    for s in range(4):
        member = jnp.where(struct[...] == s, scalar_part, 0.0) * head[pl.ds(task[s], 1), :]
        energy[s] = jnp.sum(member)


def turn_back(core, task, mine, got, hot, node, struct, head):
    vm = pl.BlockSpec(memory_space=VMEM)
    smem = pl.BlockSpec(memory_space=SMEM)
    return pl.pallas_call(
        back_kernel,
        out_shape=(
            jax.ShapeDtypeStruct((ATOMS, COEF * C), BF),
            jax.ShapeDtypeStruct((4,), F32),
        ),
        in_specs=[smem] * 2 + [vm] * 6,
        out_specs=(vm, smem),
        compiler_params=pltpu.CompilerParams(vmem_limit_bytes=6 * 2**20),
        cost_estimate=pl.CostEstimate(flops=10**9, bytes_accessed=4 * 10**6, transcendentals=0),
        name="turn_back",
    )(core, task, mine, got, hot, node, struct, head)


def exchange(value, sizes, steps_first, steps_second):
    mol, nz, ny = sizes
    pairs = []
    for device in range(mol * nz * ny):
        m, t = divmod(device, nz * ny)
        z, y = divmod(t, ny)
        dz, dy = steps_first if m % 2 == 0 else steps_second
        to = ((z + dz) % nz) * ny + (y + dy) % ny
        pairs.append((device, m * nz * ny + to))
    return lax.ppermute(value, ("mol", "task"), pairs)


def body(
    node_embed,
    wigner,
    source,
    target,
    rotation,
    edge_filter,
    edge_count,
    w_zero,
    w_one_real,
    w_one_imag,
    w_two_real,
    w_two_imag,
    atom_struct,
    struct_task,
    task_head,
):
    sizes = (8, 8, 4)
    core = lax.axis_index("mol") % 2
    task = lax.axis_index("task")
    z, y = task // 4, task % 4
    first = core == 0

    core_vec = core.reshape(1).astype(jnp.int32)

    def pick(a, b):
        return jnp.where(first, a, b)

    b0 = pack(core_vec, w_zero, w_one_real, w_one_imag, w_two_real, w_two_imag)
    a3 = exchange(b0, sizes, (0, 2), (4, 0))
    a1 = exchange(b0, sizes, (0, 1), (1, 0))
    a2 = exchange(b0, sizes, (0, -1), (-1, 0))
    a3, a1, a2 = lax.optimization_barrier((a3, a1, a2))
    h0 = jnp.concatenate((b0, a1))
    h1 = jnp.concatenate((a2, a3))

    def forth(value, second=(0, 1)):
        return exchange(value, sizes, (1, 0), second)

    def aft(value, second=(0, -1)):
        return exchange(value, sizes, (-1, 0), second)

    q, h1 = lax.optimization_barrier((pick(h0, jnp.concatenate((a1, a3))), h1))
    p1p, p1m = lax.optimization_barrier((forth(q, (1, 0)), aft(h1, (-1, 0))))
    def both(a, b):
        return jnp.concatenate((a, b))

    x1p = both(pick(h1, h0), pick(p1p, h1))
    x1m = both(pick(h0, p1p), p1m)
    x1p, x1m = lax.optimization_barrier((x1p, x1m))
    s1p, s1m = forth(x1p), aft(x1m)

    live = (jnp.arange(EDGES, dtype=jnp.int32) < edge_count[0])[:, None]
    filters = jnp.where(live, edge_filter, jnp.zeros_like(edge_filter))
    own, send, entries, node_first = features(
        core_vec,
        node_embed,
        wigner.transpose(1, 2, 0),
        source.reshape(EDGES, 1),
        target.reshape(EDGES, 1),
        rotation.reshape(EDGES, 1),
        filters,
    )

    s1p, s1m, send = lax.optimization_barrier((s1p, s1m, send))
    offsets_first, offsets_second = block_offsets()
    table = jnp.asarray((offsets_first, offsets_second), jnp.int32)[core]
    shard = ((z + table[:, 0]) % 8) * 4 + (y + table[:, 1]) % 4

    swap = [(i, i ^ 1) for i in range(8)]
    got = lax.ppermute(send, "mol", swap)
    late, late_zero = choose(core_vec, shard, own, got, (b0, a1, a2, a3, p1p, p1m))
    s2p, s2m, late = lax.optimization_barrier((forth(s1p), aft(s1m), late))
    s3p, s3m = lax.optimization_barrier((forth(s2p), aft(s2m)))
    blocks = (b0, a1, a2, a3, p1p, p1m, s1p, s1m, s2p, s2m)
    parts = mix_early(core_vec, shard, blocks, own, got)
    held = (4, TILES, 8, C)
    mine, other = mix_late(core_vec, s3p.reshape(held), s3m.reshape(held), *parts, late, late_zero, own, got)
    back = lax.ppermute(other, "mol", swap)
    hot = ends_of(entries, rotation.reshape(1, EDGES), target.reshape(1, EDGES), mine)
    update, energy = turn_back(
        core_vec,
        struct_task,
        mine,
        back,
        hot,
        node_first,
        atom_struct.reshape(ATOMS, 1),
        task_head,
    )
    return update, energy


def solution(mesh):
    both = P(("mol", "task"))
    wide = P(("mol", "task"), None)
    rows = P("task", None)
    in_specs = (wide, P(), both, both, both, wide, both, rows, rows, rows, rows, rows, both, both, P())
    return jax.shard_map(
        body, mesh=mesh, in_specs=in_specs, out_specs=(wide, both), check_vma=False
    )
```
